128 devices in a mesh: grp: 4 (over z), head: 32 (over y, x, core).
Axes of the slice: x: 4, y: 4, z: 4, core: 2. Of those that a mesh axis runs over, the one named last changes fastest.
Arguments:
- prompt: bfloat16 [49152, 7168], P(('grp', 'head')), may hold values from -6 to 6
- w_dkv: bfloat16 [7168, 576], replicated, may hold values from -0.0625 to 0.0625
- kv_gain: float32 [512], replicated, may hold values from 0.1 to 1.9
- block_table: int32 [128, 16], replicated, may hold values from 0 to 767, as said below
- ctx_pages: int32 [128], replicated, may hold values from 1 to 16, as said below
- dec_hidden: bfloat16 [128, 2, 7168], P('grp'), may hold values from -6 to 6
- w_dq: bfloat16 [7168, 1536], P('head'), may hold values from -0.0625 to 0.0625
- q_gain: float32 [1536], replicated, may hold values from 0.1 to 1.9
- w_uq: bfloat16 [1536, 24576], P(None, 'head'), may hold values from -0.15625 to 0.15625
- w_uk: bfloat16 [128, 128, 512], P('head')
- w_uv: bfloat16 [128, 512, 128], P('head'), may hold values from -0.25 to 0.25
- w_o: bfloat16 [16384, 7168], P('head'), may hold values from -0.09375 to 0.09375
Outputs:
- attn_out: bfloat16 [128, 2, 7168], P('grp', None, 'head')
The draws below stay inside these ranges and needn't reach their ends.
Inputs may be any that keep to these rules, and one draw needn't show every extreme that they name: `block_table`: request r * 32 + q belongs to decode rank r. The first ctx_pages[q] entries of row q are that request's pages in order; over all requests they name every page id exactly once. Entries past ctx_pages[q] are arbitrary page ids. Page n was prefilled by device n // 6 (grp index times 32 plus head index); at most 3 pages of one prefill device belong to one decode rank, and every prefill device has 3 pages for some rank. `ctx_pages`: the lengths of one rank's requests sum to the number of pages that rank receives; some request has 16 pages in every draw.
All inputs are finite; a program needn't handle non-finite values.
Results may differ from the reference program's by a relative error of at most 0.039.
Values may be sent and summed in bfloat16 or wider, within the bound.
A program may use at most 192 MiB of HBM per device.

```python
import math
import jax
import jax.numpy as jnp
from jax import lax

D = 7168
HEADS = 128
NOPE = 128
ROPE = 64
VD = 128
LAT = 512
QL = 1536
PAGE = 64
PAGES_DEV = 6
MAXP = 16
REQ = 32
REQUESTS = 128
TOKENS = 49152
N_GRP = 4
N_HEAD = 32


def request_plan(key):
    rank_count = N_GRP
    device_count = N_GRP * N_HEAD
    page_total = device_count * PAGES_DEV
    k_rot, k_perm, k_order, k_pair, k_req, k_pad = jax.random.split(key, 6)
    devices_at = jnp.arange(device_count, dtype=jnp.int32)
    rot_table = jnp.array([0, 0, 0, 0, 1, 1, 2, 3], jnp.int32)
    picked = jax.random.randint(k_rot, (device_count,), 0, 8)
    shifts = jnp.where(devices_at < device_count // 2, devices_at % rank_count, rot_table[picked]).astype(jnp.int32)
    pattern_row = jnp.array([0, 0, 0, 1, 1, 2], jnp.int32)
    perm_keys = jax.random.split(k_perm, device_count)
    perms = jax.vmap(lambda one_key: jax.random.permutation(one_key, PAGES_DEV))(perm_keys)
    targets = ((shifts[:, None] + pattern_row[perms]) % rank_count).reshape(-1).astype(jnp.int32)
    order_keys = jax.random.permutation(k_order, page_total).astype(jnp.int32)
    ordered = jnp.argsort(targets * page_total + order_keys, stable=True).astype(jnp.int32)
    counts = jnp.sum((targets[None, :] == jnp.arange(rank_count, dtype=jnp.int32)[:, None]).astype(jnp.int32), axis=1)
    offsets = jnp.cumsum(counts) - counts
    remain = counts - MAXP
    index_at = jnp.arange(REQ - 1, dtype=jnp.int32)
    base_len = remain[:, None] * (index_at + 1) // (REQ - 1) - remain[:, None] * index_at // (REQ - 1)
    pair_count = (REQ - 1) // 2
    first_len = base_len[:, 0:2 * pair_count:2]
    second_len = base_len[:, 1:2 * pair_count:2]
    pair_sum = first_len + second_len
    lower = jnp.maximum(1, pair_sum - MAXP)
    upper = jnp.minimum(MAXP, pair_sum - 1) + 1
    new_first = jax.random.randint(k_pair, pair_sum.shape, lower, upper)
    paired = jnp.stack([new_first, pair_sum - new_first], axis=-1).reshape(rank_count, 2 * pair_count)
    lengths = jnp.concatenate([jnp.full((rank_count, 1), MAXP, jnp.int32), paired.astype(jnp.int32), base_len[:, 2 * pair_count:].astype(jnp.int32)], axis=1)
    req_keys = jax.random.split(k_req, rank_count)
    req_perm = jax.vmap(lambda one_key: jax.random.permutation(one_key, REQ))(req_keys)
    lengths = jnp.take_along_axis(lengths, req_perm, axis=1)
    starts = jnp.cumsum(lengths, axis=1) - lengths
    depth_at = jnp.arange(MAXP, dtype=jnp.int32)
    where_at = offsets[:, None, None] + starts[:, :, None] + depth_at[None, None, :]
    is_live = depth_at[None, None, :] < lengths[:, :, None]
    padding = jax.random.randint(k_pad, (rank_count, REQ, MAXP), 0, page_total)
    table = jnp.where(is_live, ordered[jnp.clip(where_at, 0, page_total - 1)], padding)
    return (table.reshape(rank_count * REQ, MAXP).astype(jnp.int32), lengths.reshape(-1).astype(jnp.int32))


def draw_block_table(key, part):
    table, lengths = request_plan(key)
    return table


def draw_ctx_pages(key, part):
    table, lengths = request_plan(key)
    return lengths


def draw_w_uk(key, part):
    key = jax.random.fold_in(key, 11)
    values = jax.random.normal(key, (HEADS, NOPE, LAT), jnp.float32) / math.sqrt(NOPE)
    return values.astype(jnp.bfloat16)


def strengthened(values, stream_key, source, target, parts, factor):
    owner, partner = [(jnp.arange(values.shape[dim]) // (values.shape[dim] // parts)).reshape([-1 if axis == dim else 1 for axis in range(values.ndim)]) for dim in (source, target)]
    chosen = jax.random.permutation(stream_key, parts)[partner]
    strong = (owner == chosen) | (owner == (partner + parts // 2) % parts)
    return jnp.where(strong, factor * values, values)


def block_scale(stream_key, dims, cuts, least, largest):
    loudness = 1.0
    for dim, parts in cuts:
        draws = jax.random.uniform(jax.random.fold_in(jax.random.fold_in(stream_key, 6), dim), (parts,), jnp.float32, least / len(cuts), largest / len(cuts))
        loudness = loudness * jnp.repeat(jnp.exp(draws), dims[dim] // parts).reshape((-1,) + (1,) * (len(dims) - 1 - dim))
    return loudness


def noise(rng, dims, deviation, limit, cuts=(), held_as=jnp.bfloat16):
    drawn = deviation * jax.random.normal(rng, dims, jnp.float32)
    if cuts:
        drawn = drawn * block_scale(rng, dims, cuts, -0.22, 0.18)
    return jnp.clip(drawn, -limit, limit).astype(held_as)


def heavy_noise(own_key, dims, scale, bound, pieces, heavy, kind=jnp.bfloat16):
    result = scale * jax.random.normal(own_key, dims, jnp.float32)
    if pieces:
        result = result * block_scale(own_key, dims, pieces, -0.22, 0.18)
    return jnp.clip(strengthened(result, jax.random.fold_in(own_key, 3), *heavy), -bound, bound).astype(kind)


def setup_inputs(seed: int = 0) -> dict:
    splits = jax.random.split(jax.random.key(seed), 13)
    prompt = noise(splits[0], (TOKENS, D), 1.0, 6.0, ((0, 128),))
    w_dkv = noise(splits[1], (D, LAT + ROPE), D ** -0.5, 0.0625)
    kv_gain = jnp.clip(1.0 + 0.18 * jax.random.normal(splits[2], (LAT,), jnp.float32), 0.1, 1.9)
    block_table = draw_block_table(jax.random.fold_in(splits[12], 71), 0)
    ctx_pages = draw_ctx_pages(jax.random.fold_in(splits[12], 71), 0)
    dec_hidden = noise(splits[5], (REQUESTS, 2, D), 1.0, 6.0, ((0, 4),))
    w_dq = noise(splits[6], (D, QL), D ** -0.5, 0.0625, ((0, 32),))
    q_gain = jnp.clip(1.0 + 0.18 * jax.random.normal(splits[7], (QL,), jnp.float32), 0.1, 1.9)
    w_uq = noise(splits[8], (QL, HEADS * (NOPE + ROPE)), QL ** -0.5, 0.15625, ((1, 32),))
    w_uk = draw_w_uk(jax.random.fold_in(splits[12], 71), 0)
    w_uv = noise(splits[10], (HEADS, LAT, VD), LAT ** -0.5, 0.25, ((0, 32),))
    w_o = heavy_noise(splits[11], (HEADS * VD, D), (HEADS * VD) ** -0.5, 0.09375, ((0, 32),), (0, 1, 32, 2.75))
    return {"prompt": prompt, "w_dkv": w_dkv, "kv_gain": kv_gain, "block_table": block_table, "ctx_pages": ctx_pages, "dec_hidden": dec_hidden, "w_dq": w_dq, "q_gain": q_gain, "w_uq": w_uq, "w_uk": w_uk, "w_uv": w_uv, "w_o": w_o}


def norm_rows(values, gain_row):
    return values * lax.rsqrt(lax.optimization_barrier(jnp.mean(values * values, axis=-1, keepdims=True)) + 1e-06) * gain_row

def rotate(values, positions):
    half_width = values.shape[-1] // 2
    inverse_freq = 10000.0 ** (-2.0 * jnp.arange(half_width, dtype=jnp.float32) / values.shape[-1])
    angles = positions.astype(jnp.float32)[..., None] * inverse_freq
    cosine = jnp.cos(angles)
    sine_part = jnp.sin(angles)
    first_half = values[..., :half_width]
    second_half = values[..., half_width:]
    return jnp.concatenate([first_half * cosine - second_half * sine_part, second_half * cosine + first_half * sine_part], axis=-1)

def product(pattern, factor, second):
    return jnp.einsum(pattern, factor.astype(jnp.float32), second.astype(jnp.float32))

def page_depths(block_table, ctx_pages, page_total):
    page_ids = jnp.arange(page_total, dtype=jnp.int32)
    columns = jnp.arange(block_table.shape[1], dtype=jnp.int32)
    is_live = columns[None, :] < ctx_pages[:, None]
    matched = (block_table[None, :, :] == page_ids[:, None, None]) & is_live[None]
    return lax.optimization_barrier(jnp.sum(jnp.where(matched, columns[None, None, :], 0), axis=(1, 2))).astype(jnp.int32)

def attend(query_latent, new_rows, ctx_latent, ctx_rope, lengths, kv_gain, q_gain, w_uq, w_uk, w_uv):
    request_count = lengths.shape[0]
    head_count, nope_width, latent_width = w_uk.shape
    rope_width = new_rows.shape[1] - latent_width
    positions = (lengths[:, None] * PAGE + jnp.arange(2, dtype=jnp.int32)[None, :]).reshape(-1)
    new_latent = norm_rows(new_rows[:, :latent_width], kv_gain).astype(jnp.bfloat16).reshape(request_count, 2, latent_width)
    new_rope = rotate(new_rows[:, latent_width:], positions).astype(jnp.bfloat16).reshape(request_count, 2, rope_width)
    query_norm = norm_rows(query_latent, q_gain).astype(jnp.bfloat16)
    queries = jnp.dot(query_norm, w_uq, preferred_element_type=jnp.float32).reshape(request_count * 2, head_count, nope_width + rope_width)
    query_nope = queries[..., :nope_width].astype(jnp.bfloat16)
    query_rope = rotate(queries[..., nope_width:], positions[:, None]).astype(jnp.bfloat16).reshape(request_count, 2, head_count, rope_width)
    absorbed = product('bhn,hnl->bhl', query_nope, w_uk).astype(jnp.bfloat16).reshape(request_count, 2, head_count, latent_width)
    keys_latent = jnp.concatenate([ctx_latent, new_latent], axis=1)
    keys_rope = jnp.concatenate([ctx_rope, new_rope], axis=1)
    scores = (product('rshl,rtl->rsht', absorbed, keys_latent) + product('rshe,rte->rsht', query_rope, keys_rope)) * (nope_width + rope_width) ** (-0.5)
    span = ctx_latent.shape[1]
    tokens_at = jnp.arange(span + 2, dtype=jnp.int32)
    steps_at = jnp.arange(2, dtype=jnp.int32)
    ctx_live = tokens_at[None, :] < (lengths * PAGE)[:, None]
    new_live = (tokens_at[None, :] >= span) & (tokens_at[None, :] - span <= steps_at[:, None])
    is_live = (ctx_live[:, None, :] | new_live[None, :, :])[:, :, None, :]
    scores = jnp.where(is_live, scores, -1e+30)
    highest = lax.optimization_barrier(jnp.max(scores, axis=-1, keepdims=True))
    weights = jnp.where(is_live, jnp.exp(scores - highest), 0.0)
    weights = (weights / lax.optimization_barrier(jnp.sum(weights, axis=-1, keepdims=True))).astype(jnp.bfloat16)
    mixed = product('rsht,rtl->rshl', weights, keys_latent).astype(jnp.bfloat16)
    values = product('rshl,hlv->rshv', mixed, w_uv).astype(jnp.bfloat16)
    return values.reshape(request_count, 2, head_count * w_uv.shape[2])

def reference(prompt, w_dkv, kv_gain, block_table, ctx_pages, dec_hidden, w_dq, q_gain, w_uq, w_uk, w_uv, w_o):
    page_total = prompt.shape[0] // PAGE
    latent_width = kv_gain.shape[0]
    page_rows = jnp.dot(prompt, w_dkv, preferred_element_type=jnp.float32)
    page_depth = page_depths(block_table, ctx_pages, page_total)
    positions = (page_depth[:, None] * PAGE + jnp.arange(PAGE, dtype=jnp.int32)[None, :]).reshape(-1)
    latent = norm_rows(page_rows[:, :latent_width], kv_gain).astype(jnp.bfloat16).reshape(page_total, PAGE, latent_width)
    rope_keys = rotate(page_rows[:, latent_width:], positions).astype(jnp.bfloat16).reshape(page_total, PAGE, -1)
    request_count = block_table.shape[0]
    ctx_latent = latent[block_table].reshape(request_count, MAXP * PAGE, latent_width)
    ctx_rope = rope_keys[block_table].reshape(request_count, MAXP * PAGE, -1)
    flat_hidden = dec_hidden.reshape(request_count * 2, -1)
    query_latent = jnp.dot(flat_hidden, w_dq, preferred_element_type=jnp.float32)
    new_rows = jnp.dot(flat_hidden, w_dkv, preferred_element_type=jnp.float32)
    values = attend(query_latent, new_rows, ctx_latent, ctx_rope, ctx_pages, kv_gain, q_gain, w_uq, w_uk, w_uv)
    mixed_out = jnp.dot(values.reshape(request_count * 2, -1), w_o, preferred_element_type=jnp.float32)
    return mixed_out.astype(jnp.bfloat16).reshape(dec_hidden.shape)
```

```python
import jax
import jax.numpy as jnp
from jax import lax
from jax.experimental import pallas as pl
from jax.experimental.pallas import tpu as pltpu
from jax.sharding import PartitionSpec as P

PAGE = 64
SLOT = 3
MAXP = 16
LAT = 512
ROPE = 64
NOPE = 128
QL = 1536
NH = 4
NG = 4
NY = 4
NB = 8
N_HEAD = 32
ROWS = SLOT * PAGE
RROWS = SLOT * PAGE // 2
KCHUNK = 1024
OFFS = (0, 1, 3, 2)
MESH = pl.DeviceIdType.MESH
F32 = jnp.float32
BF16 = jnp.bfloat16
LOW = -1e30


def dot(a, b):
    return jnp.dot(a, b, preferred_element_type=F32)


def dot_t(a, b):
    return lax.dot_general(a, b, (((1,), (1,)), ((), ())), preferred_element_type=F32)


def norm_rows(values, gain_row, width):
    mean = jnp.sum(values * values, axis=-1, keepdims=True) * (1.0 / width)
    return values * lax.rsqrt(mean + 1e-06) * gain_row


def rotate_pairs(x, cosine, signed_sine):
    lane = lax.broadcasted_iota(jnp.int32, x.shape, 1)
    swapped = jnp.where((lane & 63) < 32, pltpu.roll(x, 96, 1), pltpu.roll(x, 32, 1))
    return x * cosine + swapped * signed_sine


def rows_by_request(transposed):
    i = lax.broadcasted_iota(jnp.int32, (256, 256), 1 if transposed else 0)
    j = lax.broadcasted_iota(jnp.int32, (256, 256), 0 if transposed else 1)
    place = ((i >> 1) & 3) * 64 + (i >> 3) * 2 + (i & 1)
    return jnp.where(j == place, 1.0, 0.0).astype(BF16)


def gather_kernel(
    send_idx,
    hpart,
    w_dq,
    kv_gain,
    q_gain,
    page_cos,
    page_sin,
    new_cos,
    new_sin,
    prompt,
    hidden,
    w_dkv,
    w_uq,
    w_uk,
    lat_all,
    rope_all,
    q_lat,
    q_rope,
    new_lat,
    new_rope,
    pbuf,
    wbuf,
    acc,
    uq_buf,
    uk_buf,
    lat_own,
    rope_own,
    zlat,
    zrope,
    qpart,
    rq_land,
    red,
    qlat,
    qmine,
    qrmine,
    load_sem,
    w_sem,
    own_sem,
    z_send,
    z_recv,
    x_send,
    x_recv,
    f_send,
    f_recv,
    c_send,
    c_recv,
    r_send,
    r_recv,
    g_send,
    g_recv,
    y_send,
    y_recv,
):
    g = lax.axis_index("grp")
    h = lax.axis_index("head")
    y = h // NB
    b = h % NB
    x = b // 2
    c = b % 2
    sibling = h + 1 - 2 * c
    right = y * NB + ((x + 1) % 4) * 2 + c
    left = y * NB + ((x + 3) % 4) * 2 + c
    b_left = ((x + 3) % 4) * 2 + c
    b_right = ((x + 1) % 4) * 2 + c
    b_far = ((x + 2) % 4) * 2 + c

    barrier = pltpu.get_barrier_semaphore()

    @pl.loop(1, N_HEAD)
    def _(o):
        pl.semaphore_signal(
            barrier, inc=1, device_id={"head": (h + o) % N_HEAD}, device_id_type=MESH
        )

    for o in (1, 2, 3):
        pl.semaphore_signal(barrier, inc=1, device_id={"grp": (g + o) % NG}, device_id_type=MESH)

    depth = prompt.shape[1]
    tokens = prompt.shape[0]
    chunks = depth // KCHUNK
    loads = []
    for k in range(chunks):
        cols = pl.ds(k * KCHUNK, KCHUNK)
        loads.append(
            [
                pltpu.make_async_copy(
                    prompt.at[:, cols], pbuf.at[pl.ds(0, tokens), cols], load_sem.at[k, 0]
                ),
                pltpu.make_async_copy(
                    hidden.at[:, cols], pbuf.at[pl.ds(tokens, 64), cols], load_sem.at[k, 1]
                ),
                pltpu.make_async_copy(w_dkv.at[cols, :], wbuf.at[cols, :], load_sem.at[k, 2]),
            ]
        )
    for group in loads:
        for one in group:
            one.start()
    uq_copy = pltpu.make_async_copy(w_uq, uq_buf, w_sem.at[0])
    uk_copy = pltpu.make_async_copy(w_uk, uk_buf, w_sem.at[1])
    uq_copy.start()
    uk_copy.start()

    qpart[...] = dot(hpart[...], w_dq[...])
    pl.semaphore_wait(barrier, N_HEAD - 1 + 3)

    def q_block(i):
        return (
            pl.ds(pl.multiple_of((i // 4) * 8, 8), 8),
            pl.ds(pl.multiple_of((i % 4) * 384, 128), 384),
        )

    def share_copy(to):
        return pltpu.make_async_remote_copy(
            src_ref=qpart.at[q_block(to)],
            dst_ref=rq_land.at[h],
            send_sem=r_send.at[to],
            recv_sem=r_recv.at[h],
            device_id={"head": to},
            device_id_type=MESH,
        )

    @pl.loop(1, N_HEAD)
    def _(o):
        share_copy((h + o) % N_HEAD).start()

    for k in range(chunks):
        for one in loads[k]:
            one.wait()
        part = dot(pbuf[:, k * KCHUNK : (k + 1) * KCHUNK], wbuf[k * KCHUNK : (k + 1) * KCHUNK, :])
        if k == 0:
            acc[...] = part
        else:
            acc[...] += part

    pages = tokens // PAGE
    lat_own[...] = (
        norm_rows(acc[0:tokens, 0:LAT], kv_gain[...], LAT).astype(BF16).reshape(pages, PAGE, LAT)
    )
    halves = []
    for p in range(pages):
        first = acc[p * PAGE : p * PAGE + 32, LAT : LAT + ROPE]
        second = acc[p * PAGE + 32 : p * PAGE + 64, LAT : LAT + ROPE]
        halves.append(jnp.concatenate([first, second], axis=1))
    packed = jnp.concatenate(halves, axis=0)
    rope_own[...] = (
        rotate_pairs(packed, page_cos[...], page_sin[...]).astype(BF16).reshape(pages, 32, 128)
    )

    for j in range(4):
        rank = (g + OFFS[j]) % NG
        for k in range(SLOT):
            page = send_idx[rank * SLOT + k]
            zlat[j, k * PAGE : (k + 1) * PAGE, :] = lat_own[page]
            zrope[j, k * 32 : (k + 1) * 32, :] = rope_own[page]

    def z_copies(j):
        rank = (g + OFFS[j]) % NG
        return [
            pltpu.make_async_remote_copy(
                src_ref=src.at[j],
                dst_ref=dst.at[b, g],
                send_sem=z_send.at[j - 1, i],
                recv_sem=z_recv.at[j - 1, i],
                device_id={"grp": rank},
                device_id_type=MESH,
            )
            for i, (src, dst) in enumerate(((zlat, lat_all), (zrope, rope_all)))
        ]

    def plane(j):
        return (g + NG - OFFS[j]) % NG

    def ring_copies(j, block, to, send_sem, recv_sem):
        gs = plane(j)
        out = []
        for i, (mine, ref) in enumerate(((zlat, lat_all), (zrope, rope_all))):
            src = mine.at[0] if (j == 0 and block is b) else ref.at[block, gs]
            out.append(
                pltpu.make_async_remote_copy(
                    src_ref=src,
                    dst_ref=ref.at[block, gs],
                    send_sem=send_sem.at[i],
                    recv_sem=recv_sem.at[i],
                    device_id={"head": to},
                    device_id_type=MESH,
                )
            )
        return out

    def to_right(j):
        return ring_copies(j, b, right, x_send.at[j, 0], x_recv.at[j, 0])

    def to_left(j):
        return ring_copies(j, b, left, x_send.at[j, 1], x_recv.at[j, 1])

    def onward(j):
        if j in (0, 3):
            return ring_copies(j, b_left, right, f_send.at[j], f_recv.at[j])
        return ring_copies(j, b_right, left, f_send.at[j], f_recv.at[j])

    blocks = (b, b_left, b_right, b_far)

    def across(j, which):
        return ring_copies(j, blocks[which], sibling, c_send.at[j, which], c_recv.at[j, which])

    def start(copies):
        for one in copies:
            one.start()

    def wait_recv(copies):
        for one in copies:
            one.wait_recv()

    def wait_send(copies):
        for one in copies:
            one.wait_send()

    def arrived(ref_block, j, sem):
        gs = plane(j)
        for i, ref in enumerate((lat_all, rope_all)):
            pltpu.make_async_remote_copy(
                src_ref=ref.at[ref_block, gs],
                dst_ref=ref.at[ref_block, gs],
                send_sem=sem.at[i],
                recv_sem=sem.at[i],
                device_id={"head": sibling},
                device_id_type=MESH,
            ).wait_recv()

    def serve_own(j):
        start(to_right(j))
        start(to_left(j))
        start(across(j, 0))

    def serve_near(j):
        arrived(b_left, j, x_recv.at[j, 0])
        if j in (0, 3):
            start(onward(j))
        start(across(j, 1))
        arrived(b_right, j, x_recv.at[j, 1])
        if j in (1, 2):
            start(onward(j))
        start(across(j, 2))

    def serve_far(j):
        arrived(b_far, j, f_recv.at[j])
        start(across(j, 3))

    for j in (1, 2, 3):
        start(z_copies(j))
    own = [
        pltpu.make_async_copy(zlat.at[0], lat_all.at[b, g], own_sem.at[0]),
        pltpu.make_async_copy(zrope.at[0], rope_all.at[b, g], own_sem.at[1]),
    ]
    start(own)
    serve_own(0)

    new_lat[...] = norm_rows(acc[tokens : tokens + 64, 0:LAT], kv_gain[...], LAT).astype(BF16)
    new_r = acc[tokens : tokens + 64, LAT : LAT + ROPE]
    new_r = rotate_pairs(jnp.concatenate([new_r, new_r], axis=1), new_cos[...], new_sin[...])
    lane = lax.broadcasted_iota(jnp.int32, new_r.shape, 1)
    new_rope[...] = jnp.where(lane < ROPE, new_r, 0.0).astype(BF16)

    rq_land[h] = qpart[q_block(h)]

    @pl.loop(1, N_HEAD)
    def _(o):
        src = (h + o) % N_HEAD
        pltpu.make_async_remote_copy(
            src_ref=rq_land.at[src],
            dst_ref=rq_land.at[src],
            send_sem=r_send.at[src],
            recv_sem=r_recv.at[src],
            device_id={"head": src},
            device_id_type=MESH,
        ).wait_recv()

    red[...] = jnp.sum(rq_land[...], axis=0)
    qlat[q_block(h)] = red[...]

    def sum_copy(to):
        return pltpu.make_async_remote_copy(
            src_ref=red,
            dst_ref=qlat.at[q_block(h)],
            send_sem=g_send.at[to],
            recv_sem=g_recv.at[h],
            device_id={"head": to},
            device_id_type=MESH,
        )

    @pl.loop(1, N_HEAD)
    def _(o):
        sum_copy((h + o) % N_HEAD).start()

    def z_arrived(j):
        gs = plane(j)
        for i, ref in enumerate((lat_all, rope_all)):
            pltpu.make_async_remote_copy(
                src_ref=ref.at[b, gs],
                dst_ref=ref.at[b, gs],
                send_sem=z_send.at[j - 1, i],
                recv_sem=z_recv.at[j - 1, i],
                device_id={"grp": gs},
                device_id_type=MESH,
            ).wait_recv()

    for j in (1, 2):
        z_arrived(j)
        serve_own(j)
    serve_near(0)

    @pl.loop(1, N_HEAD)
    def _(o):
        src = (h + o) % N_HEAD
        pltpu.make_async_remote_copy(
            src_ref=red,
            dst_ref=qlat.at[q_block(src)],
            send_sem=g_send.at[src],
            recv_sem=g_recv.at[src],
            device_id={"head": src},
            device_id_type=MESH,
        ).wait_recv()

    uq_copy.wait()
    uk_copy.wait()
    query_norm = norm_rows(qlat[...], q_gain[...], QL).astype(BF16)
    queries = dot(query_norm, uq_buf[...])
    parts = []
    ropes = []
    for n in range(NH):
        at = n * (NOPE + ROPE)
        parts.append(dot(queries[:, at : at + NOPE].astype(BF16), uk_buf[n]).astype(BF16))
        one = queries[:, at + NOPE : at + NOPE + ROPE]
        one = jnp.concatenate([one, one], axis=1)
        ropes.append(rotate_pairs(one, new_cos[...], new_sin[...]).astype(BF16))
    order = rows_by_request(False)
    qmine[...] = dot(order, jnp.concatenate(parts, axis=0)).astype(BF16)
    qrmine[...] = dot(order, jnp.concatenate(ropes, axis=0)).astype(BF16)

    def y_copies(o):
        to = ((y + o) % NY) * NB + b
        return [
            pltpu.make_async_remote_copy(
                src_ref=src,
                dst_ref=dst.at[y],
                send_sem=y_send.at[o - 1, i],
                recv_sem=y_recv.at[o - 1, i],
                device_id={"head": to},
                device_id_type=MESH,
            )
            for i, (src, dst) in enumerate(((qmine, q_lat), (qrmine, q_rope)))
        ]

    for o in (1, 2, 3):
        start(y_copies(o))
    own_q = [
        pltpu.make_async_copy(qmine, q_lat.at[y], own_sem.at[2]),
        pltpu.make_async_copy(qrmine, q_rope.at[y], own_sem.at[3]),
    ]
    start(own_q)

    z_arrived(3)
    serve_own(3)
    serve_near(1)
    serve_near(2)
    serve_far(0)
    serve_near(3)
    serve_far(1)
    serve_far(2)
    serve_far(3)

    sib_blocks = tuple(blk + 1 - 2 * c for blk in blocks)
    for j in range(4):
        for which in range(4):
            arrived(sib_blocks[which], j, c_recv.at[j, which])
    for o in (1, 2, 3):
        src = (y + NY - o) % NY
        for i, ref in enumerate((q_lat, q_rope)):
            pltpu.make_async_remote_copy(
                src_ref=ref.at[src],
                dst_ref=ref.at[src],
                send_sem=y_send.at[o - 1, i],
                recv_sem=y_recv.at[o - 1, i],
                device_id={"head": src * NB + b},
                device_id_type=MESH,
            ).wait_recv()

    for one in own + own_q:
        one.wait()
    for j in (1, 2, 3):
        wait_send(z_copies(j))
    for j in range(4):
        wait_send(to_right(j))
        wait_send(to_left(j))
        wait_send(onward(j))
        for which in range(4):
            wait_send(across(j, which))
    for o in (1, 2, 3):
        wait_send(y_copies(o))

    @pl.loop(1, N_HEAD)
    def _(o):
        to = (h + o) % N_HEAD
        share_copy(to).wait_send()
        sum_copy(to).wait_send()


def attend_kernel(
    order,
    owner,
    count,
    lat,
    rope,
    q_lat,
    q_rope,
    new_lat,
    new_rope,
    out,
    stats,
    qf,
    qb,
    acc,
    m_ref,
    l_ref,
):
    my_y = count[1]
    requests = 32
    scale = (NOPE + ROPE) ** (-0.5)
    for yb in range(NY):
        qf[:, yb * 8 : (yb + 1) * 8, 0:LAT] = q_lat[yb].astype(F32).reshape(requests, 8, LAT)
        qf[:, yb * 8 : (yb + 1) * 8, LAT:] = q_rope[yb].astype(F32).reshape(requests, 8, 128)
    qb[0:requests] = qf[...].astype(BF16)
    qb[requests] = jnp.zeros((32, LAT + 128), BF16)

    group = 8
    for r0 in range(0, requests, group):
        rows = group * 32
        q_rows = qb[r0 : r0 + group].reshape(rows, LAT + 128)
        s = (dot_t(q_rows[:, 0:LAT], new_lat[...]) + dot_t(q_rows[:, LAT:], new_rope[...])) * scale
        i = lax.broadcasted_iota(jnp.int32, s.shape, 0) + r0 * 32
        j = lax.broadcasted_iota(jnp.int32, s.shape, 1)
        live = ((i >> 5) == (j >> 1)) & ((j & 1) <= (i & 1)) & (((i >> 3) & 3) == my_y)
        s = jnp.where(live, s, LOW)
        top = jnp.max(s, axis=1, keepdims=True)
        p = jnp.where(live, jnp.exp(s - top), 0.0)
        total = jnp.sum(p, axis=1, keepdims=True)
        acc[r0 : r0 + group] = dot(p.astype(BF16), new_lat[...]).reshape(group, 32, LAT)
        m_ref[r0 : r0 + group] = jnp.broadcast_to(top, (rows, 128)).reshape(group, 32, 128)
        l_ref[r0 : r0 + group] = jnp.broadcast_to(total, (rows, 128)).reshape(group, 32, 128)
    acc[requests] = jnp.zeros((32, LAT), F32)
    m_ref[requests] = jnp.full((32, 128), LOW, F32)
    l_ref[requests] = jnp.zeros((32, 128), F32)

    UNROLL = 4
    lane = lax.broadcasted_iota(jnp.int32, (32, 128), 1)

    @pl.loop(0, (count[0] + UNROLL - 1) // UNROLL)
    def _(it):
        done = []
        for u in range(UNROLL):
            slot = order[it * UNROLL + u]
            r = owner[it * UNROLL + u]
            keys = lat[pl.ds(pl.multiple_of(slot * PAGE, PAGE), PAGE), :]
            pair = rope[pl.ds(pl.multiple_of(slot * 32, 32), 32), :]
            zero = jnp.zeros_like(pair)
            both = jnp.concatenate(
                [jnp.where(lane < ROPE, pair, zero), jnp.where(lane >= ROPE, pair, zero)], axis=0
            )
            q = qb[r]
            s = (dot_t(q[:, 0:LAT], keys) + dot_t(q[:, LAT:], both)) * scale
            top = jnp.max(s, axis=1, keepdims=True)
            p = jnp.exp(s - top)
            total = jnp.sum(p, axis=1, keepdims=True)
            done.append((r, top, total, dot(p.astype(BF16), keys)))
        for r, top, total, o in done:
            m_old = m_ref[r]
            m_new = jnp.maximum(m_old, top)
            a = jnp.exp(m_old - m_new)
            e = jnp.exp(top - m_new)
            m_ref[r] = m_new
            l_ref[r] = l_ref[r] * a + total * e
            acc[r] = acc[r] * a[:, 0:1] + o * e[:, 0:1]

    for yb in range(NY):
        rows = slice(yb * 8, (yb + 1) * 8)
        total = l_ref[0:requests, rows, :]
        some = total > 0.0
        safe = jnp.where(some, total, 1.0)
        inverse = 1.0 / safe
        mixed = acc[0:requests, rows, :] * inverse[:, :, 0:1]
        out[yb] = mixed.reshape(256, LAT).astype(BF16)
        lse = jnp.where(some, m_ref[0:requests, rows, :] + jnp.log(safe), LOW)
        stats[yb] = jnp.transpose(lse.reshape(256, 128))[0:8, :]


def project_kernel(
    part,
    stats,
    w_uv,
    w_o,
    out,
    o_land,
    s_land,
    t_buf,
    wo_buf,
    vals,
    sbuf,
    rbuf,
    w_sem,
    y_send,
    y_recv,
    o_send,
    o_recv,
):
    h = lax.axis_index("head")
    y = h // NB
    b = h % NB
    barrier = pltpu.get_barrier_semaphore()

    @pl.loop(1, N_HEAD)
    def _(o):
        pl.semaphore_signal(
            barrier, inc=1, device_id={"head": (h + o) % N_HEAD}, device_id_type=MESH
        )

    wo_copy = pltpu.make_async_copy(w_o, wo_buf, w_sem)
    wo_copy.start()
    pl.semaphore_wait(barrier, N_HEAD - 1)

    def y_copies(o):
        ty = (y + o) % NY
        return [
            pltpu.make_async_remote_copy(
                src_ref=src.at[ty],
                dst_ref=dst.at[o - 1],
                send_sem=y_send.at[o - 1, i],
                recv_sem=y_recv.at[o - 1, i],
                device_id={"head": ty * NB + b},
                device_id_type=MESH,
            )
            for i, (src, dst) in enumerate(((part, o_land), (stats, s_land)))
        ]

    for o in (2, 1, 3):
        for one in y_copies(o):
            one.start()

    def column(block):
        t_buf[0:8, :] = block
        return jnp.transpose(t_buf[...])[:, 0:1]

    t_buf[...] = jnp.zeros_like(t_buf)
    lses = [column(stats[y])]
    mixes = [part[y].astype(F32)]
    for o in (1, 3, 2):
        for one in y_copies(o):
            one.wait_recv()
        lses.append(column(s_land[o - 1]))
        mixes.append(o_land[o - 1].astype(F32))
    top = jnp.maximum(jnp.maximum(lses[0], lses[1]), jnp.maximum(lses[2], lses[3]))
    weights = [jnp.exp(one - top) for one in lses]
    total = weights[0] + weights[1] + weights[2] + weights[3]
    mixed = mixes[0] * (weights[0] / total)
    for one, weight in zip(mixes[1:], weights[1:]):
        mixed += one * (weight / total)
    by_head = dot(rows_by_request(True), mixed.astype(BF16)).astype(BF16)
    for n in range(NH):
        vals[:, n * 128 : (n + 1) * 128] = dot(
            by_head[n * 64 : (n + 1) * 64, :], w_uv[n]
        ).astype(BF16)

    def out_copy(to):
        return pltpu.make_async_remote_copy(
            src_ref=sbuf.at[to],
            dst_ref=rbuf.at[h],
            send_sem=o_send.at[to],
            recv_sem=o_recv.at[h],
            device_id={"head": to},
            device_id_type=MESH,
        )

    wo_copy.wait()
    width = out.shape[1]
    span = width * NB
    for i in range(NY):
        ty = (y + i) % NY
        cols = pl.ds(pl.multiple_of(ty * span, 128), span)
        piece = dot(vals[...], wo_buf[:, cols])
        for k in range(NB):
            to = ty * NB + k
            sbuf[to] = piece[:, k * width : (k + 1) * width].astype(BF16)

            @pl.when(to != h)
            def _():
                out_copy(to).start()

    def body(o, total):
        src = (h + o) % N_HEAD
        pltpu.make_async_remote_copy(
            src_ref=rbuf.at[src],
            dst_ref=rbuf.at[src],
            send_sem=o_send.at[src],
            recv_sem=o_recv.at[src],
            device_id={"head": src},
            device_id_type=MESH,
        ).wait_recv()
        return total + rbuf[src].astype(F32)

    result = lax.fori_loop(1, N_HEAD, body, sbuf[h].astype(F32))
    out[...] = result.astype(BF16)

    for o in (1, 2, 3):
        for one in y_copies(o):
            one.wait_send()

    @pl.loop(1, N_HEAD)
    def _(o):
        out_copy((h + o) % N_HEAD).wait_send()


def spec(space):
    return pl.BlockSpec(memory_space=space)


VM, SM, ANY = pltpu.VMEM, pltpu.SMEM, pl.ANY


def page_plan(block_table, ctx_pages, g, y, b, per_rank, pages_dev):
    flat = jnp.where(
        jnp.arange(MAXP, dtype=jnp.int32)[None, :] < ctx_pages[:, None], block_table, -1
    ).reshape(1, -1)
    at = jnp.arange(NG * NB * pages_dev, dtype=jnp.int32)
    per_plane = NB * pages_dev
    ids = (at // per_plane) * (N_HEAD * pages_dev) + y * per_plane + at % per_plane
    codes = jnp.arange(flat.shape[1], dtype=jnp.int32)[None, :]
    code = jnp.sum(jnp.where(flat == ids[:, None], codes, 0), axis=1)
    code = code.reshape(NG, NB, pages_dev)
    target = code // (per_rank * MAXP)
    within = jnp.arange(pages_dev, dtype=jnp.int32)
    alike = (target[..., :, None] == target[..., None, :]) & (within[None, :] < within[:, None])
    slot = jnp.sum(alike.astype(jnp.int32), axis=-1)
    places = jnp.arange(SLOT, dtype=jnp.int32)
    request = (code // MAXP) % per_rank
    here = (target == g)[..., None, :] & (slot[..., None, :] == places[:, None])
    owner = jnp.sum(jnp.where(here, request[..., None, :] + 1, 0), axis=-1) - 1
    owner = owner.transpose(1, 0, 2).reshape(-1)
    mine = lax.dynamic_slice(code, (g, b, 0), (1, 1, pages_dev)).reshape(-1)
    my_target = lax.dynamic_slice(target, (g, b, 0), (1, 1, pages_dev)).reshape(-1)
    my_slot = lax.dynamic_slice(slot, (g, b, 0), (1, 1, pages_dev)).reshape(-1)
    sends = (my_target[None, :] * SLOT + my_slot[None, :]) == jnp.arange(
        NG * SLOT, dtype=jnp.int32
    )[:, None]
    send_idx = jnp.sum(jnp.where(sends, within[None, :], 0), axis=1)
    return owner, send_idx, mine % MAXP


def live_first(owner, spare):
    n = owner.shape[0]
    live = owner >= 0
    before = jnp.arange(n, dtype=jnp.int32)
    rank_live = jnp.sum((live[None, :] & (before[None, :] < before[:, None])).astype(jnp.int32), 1)
    count = jnp.sum(live.astype(jnp.int32))
    place = jnp.where(live, rank_live, count + before - rank_live)
    hit = place[None, :] == before[:, None]
    order = jnp.sum(jnp.where(hit, before[None, :], 0), axis=1)
    owners = jnp.sum(jnp.where(hit, jnp.where(live, owner, spare)[None, :], 0), axis=1)
    return order, owners, count


def angle_tables(positions):
    lane = jnp.arange(2 * ROPE, dtype=jnp.int32)
    inverse_freq = 10000.0 ** (-2.0 * (lane % 32).astype(F32) / ROPE)
    angles = jnp.repeat(positions.astype(F32), ROPE, axis=1) * inverse_freq[None, :]
    sign = jnp.where((lane % ROPE) < 32, -1.0, 1.0).astype(F32)
    return jnp.cos(angles), jnp.sin(angles) * sign[None, :]


def on_device(
    prompt, w_dkv, kv_gain, block_table, ctx_pages, dec_hidden, w_dq, q_gain, w_uq, w_uk, w_uv, w_o
):
    g = lax.axis_index("grp")
    h = lax.axis_index("head")
    y, b = h // NB, h % NB
    tokens, depth = prompt.shape
    pages_dev = tokens // PAGE
    per_rank = dec_hidden.shape[0]
    owner, send_idx, my_depth = page_plan(
        block_table, ctx_pages, g, y, b, per_rank, pages_dev
    )
    order, owners, count = live_first(owner, per_rank)
    lengths = lax.dynamic_slice_in_dim(ctx_pages, g * per_rank, per_rank, 0)
    t = jnp.arange(32, dtype=jnp.int32)
    page_pos = my_depth[:, None, None] * PAGE + t[None, :, None] + jnp.array([0, 32], jnp.int32)
    page_cos, page_sin = angle_tables(page_pos.reshape(-1, 2))
    new_pos = (lengths[:, None] * PAGE + jnp.arange(2, dtype=jnp.int32)[None, :]).reshape(-1, 1)
    new_cos, new_sin = angle_tables(jnp.concatenate([new_pos, new_pos], axis=1))
    hidden = dec_hidden.reshape(per_rank * 2, depth)
    share = w_dq.shape[0]
    hpart = lax.dynamic_slice_in_dim(hidden, h * share, share, 1)

    dma = pltpu.SemaphoreType.DMA
    lat_all, rope_all, q_lat, q_rope, new_lat, new_rope = pl.pallas_call(
        gather_kernel,
        out_shape=[
            jax.ShapeDtypeStruct((NB, NG, ROWS, LAT), BF16),
            jax.ShapeDtypeStruct((NB, NG, RROWS, 128), BF16),
            jax.ShapeDtypeStruct((NY, 256, LAT), BF16),
            jax.ShapeDtypeStruct((NY, 256, 128), BF16),
            jax.ShapeDtypeStruct((64, LAT), BF16),
            jax.ShapeDtypeStruct((64, 128), BF16),
        ],
        in_specs=[spec(SM)] + [spec(VM)] * 8 + [spec(ANY)] * 5,
        out_specs=[spec(ANY)] * 4 + [spec(VM)] * 2,
        scratch_shapes=[
            pltpu.VMEM((tokens + 64, depth), BF16),
            pltpu.VMEM((depth, LAT + ROPE), BF16),
            pltpu.VMEM((tokens + 64, LAT + ROPE), F32),
            pltpu.VMEM(w_uq.shape, BF16),
            pltpu.VMEM(w_uk.shape, BF16),
            pltpu.VMEM((pages_dev, PAGE, LAT), BF16),
            pltpu.VMEM((pages_dev, 32, 128), BF16),
            pltpu.VMEM((NG, ROWS, LAT), BF16),
            pltpu.VMEM((NG, RROWS, 128), BF16),
            pltpu.VMEM((64, QL), F32),
            pltpu.VMEM((N_HEAD, 8, 384), F32),
            pltpu.VMEM((8, 384), F32),
            pltpu.VMEM((64, QL), F32),
            pltpu.VMEM((256, LAT), BF16),
            pltpu.VMEM((256, 128), BF16),
            dma((depth // KCHUNK, 3)),
            dma((2,)),
            dma((4,)),
            dma((3, 2)),
            dma((3, 2)),
            dma((4, 2, 2)),
            dma((4, 2, 2)),
            dma((4, 2)),
            dma((4, 2)),
            dma((4, 4, 2)),
            dma((4, 4, 2)),
            dma((N_HEAD,)),
            dma((N_HEAD,)),
            dma((N_HEAD,)),
            dma((N_HEAD,)),
            dma((3, 2)),
            dma((3, 2)),
        ],
        compiler_params=pltpu.CompilerParams(
            collective_id=0, has_side_effects=True, vmem_limit_bytes=50 * 1024 * 1024
        ),
    )(
        send_idx,
        hpart,
        w_dq,
        kv_gain.reshape(1, -1),
        q_gain.reshape(1, -1),
        page_cos,
        page_sin,
        new_cos,
        new_sin,
        prompt,
        hidden,
        w_dkv,
        w_uq,
        w_uk,
    )

    part, stats = pl.pallas_call(
        attend_kernel,
        out_shape=[
            jax.ShapeDtypeStruct((NY, 256, LAT), BF16),
            jax.ShapeDtypeStruct((NY, 8, 256), F32),
        ],
        in_specs=[spec(SM)] * 3 + [spec(VM)] * 6,
        out_specs=[spec(VM)] * 2,
        scratch_shapes=[
            pltpu.VMEM((32, 32, LAT + 128), F32),
            pltpu.VMEM((33, 32, LAT + 128), BF16),
            pltpu.VMEM((33, 32, LAT), F32),
            pltpu.VMEM((33, 32, 128), F32),
            pltpu.VMEM((33, 32, 128), F32),
        ],
        compiler_params=pltpu.CompilerParams(vmem_limit_bytes=50 * 1024 * 1024),
    )(
        order,
        owners,
        jnp.stack([count, y]),
        lat_all.reshape(-1, LAT),
        rope_all.reshape(-1, 128),
        q_lat,
        q_rope,
        new_lat,
        new_rope,
    )

    width = depth // N_HEAD
    out = pl.pallas_call(
        project_kernel,
        out_shape=jax.ShapeDtypeStruct((64, width), BF16),
        in_specs=[spec(VM)] * 3 + [spec(ANY)],
        out_specs=spec(VM),
        scratch_shapes=[
            pltpu.VMEM((3, 256, LAT), BF16),
            pltpu.VMEM((3, 8, 256), F32),
            pltpu.VMEM((128, 256), F32),
            pltpu.VMEM(w_o.shape, BF16),
            pltpu.VMEM((64, LAT), BF16),
            pltpu.VMEM((N_HEAD, 64, width), BF16),
            pltpu.VMEM((N_HEAD, 64, width), BF16),
            dma(()),
            dma((3, 2)),
            dma((3, 2)),
            dma((N_HEAD,)),
            dma((N_HEAD,)),
        ],
        compiler_params=pltpu.CompilerParams(
            collective_id=1, has_side_effects=True, vmem_limit_bytes=50 * 1024 * 1024
        ),
    )(part, stats, w_uv, w_o)
    return out.reshape(per_rank, 2, width)


def solution(mesh):
    return jax.shard_map(
        on_device,
        mesh=mesh,
        in_specs=(
            P(("grp", "head"), None),
            P(),
            P(),
            P(),
            P(),
            P("grp", None, None),
            P("head", None),
            P(),
            P(None, "head"),
            P("head", None, None),
            P("head", None, None),
            P("head", None),
        ),
        out_specs=P("grp", None, "head"),
        check_vma=False,
    )
```

```python
import jax
import jax.numpy as jnp
from jax import lax
from jax.experimental import pallas as pl
from jax.experimental.pallas import tpu as pltpu
from jax.sharding import PartitionSpec as P

PAGE = 64
SLOT = 3
MAXP = 16
LAT = 512
ROPE = 64
NOPE = 128
QL = 1536
NH = 4
NG = 4
NY = 4
NB = 8
N_HEAD = 32
ROWS = SLOT * PAGE
RROWS = SLOT * PAGE // 2
KCHUNK = 1024
OFFS = (0, 1, 3, 2)
MESH = pl.DeviceIdType.MESH
F32 = jnp.float32
BF16 = jnp.bfloat16
LOW = -1e30


def dot(a, b):
    return jnp.dot(a, b, preferred_element_type=F32)


def dot_t(a, b):
    return lax.dot_general(a, b, (((1,), (1,)), ((), ())), preferred_element_type=F32)


def norm_rows(values, gain_row, width):
    mean = jnp.sum(values * values, axis=-1, keepdims=True) * (1.0 / width)
    return values * lax.rsqrt(mean + 1e-06) * gain_row


def rotate_pairs(x, cosine, signed_sine):
    lane = lax.broadcasted_iota(jnp.int32, x.shape, 1)
    swapped = jnp.where((lane & 63) < 32, pltpu.roll(x, 96, 1), pltpu.roll(x, 32, 1))
    return x * cosine + swapped * signed_sine


def rows_by_request(transposed):
    i = lax.broadcasted_iota(jnp.int32, (256, 256), 1 if transposed else 0)
    j = lax.broadcasted_iota(jnp.int32, (256, 256), 0 if transposed else 1)
    place = ((i >> 1) & 3) * 64 + (i >> 3) * 2 + (i & 1)
    return jnp.where(j == place, 1.0, 0.0).astype(BF16)


def fused_kernel(
    send_idx,
    owner,
    listed,
    hpart,
    w_dq,
    kv_gain,
    q_gain,
    page_cos,
    page_sin,
    new_cos,
    new_sin,
    prompt,
    hidden,
    w_dkv,
    w_uq,
    w_uk,
    w_uv,
    w_o,
    out,
    pbuf,
    hbuf,
    wbuf,
    acc,
    uq_buf,
    uk_buf,
    uv_buf,
    lat_own,
    rope_own,
    zlat,
    zrope,
    qpart,
    rq_land,
    red,
    qlat,
    qmine,
    qrmine,
    new_lat,
    new_rope,
    new_o,
    new_lse,
    lat_all,
    rope_all,
    q_lat,
    q_rope,
    qf,
    qb,
    o_slot,
    m_slot,
    l_slot,
    part,
    lse_rows,
    stats,
    o_land,
    s_land,
    t_buf,
    vals,
    sbuf,
    sib_land,
    tbuf,
    rbuf,
    load_sem,
    w_sem,
    own_sem,
    z_send,
    z_recv,
    x_send,
    x_recv,
    f_send,
    f_recv,
    c_send,
    c_recv,
    r_send,
    r_recv,
    g_send,
    g_recv,
    y_send,
    y_recv,
    o_send,
    o_recv,
    p_send,
    p_recv,
    d_send,
    d_recv,
):
    g = lax.axis_index("grp")
    h = lax.axis_index("head")
    y = h // NB
    b = h % NB
    x = b // 2
    c = b % 2
    other = 1 - c
    sibling = y * NB + x * 2 + other
    right = y * NB + ((x + 1) % 4) * 2 + c
    left = y * NB + ((x + 3) % 4) * 2 + c
    scale = (NOPE + ROPE) ** (-0.5)

    def start(copies):
        for one in copies:
            one.start()

    def wait_recv(copies):
        for one in copies:
            one.wait_recv()

    def wait_send(copies):
        for one in copies:
            one.wait_send()

    def remote(src, dst, send, recv, to):
        return pltpu.make_async_remote_copy(
            src_ref=src,
            dst_ref=dst,
            send_sem=send,
            recv_sem=recv,
            device_id=to,
            device_id_type=MESH,
        )

    barrier = pltpu.get_barrier_semaphore()

    @pl.loop(1, N_HEAD)
    def _(o):
        pl.semaphore_signal(
            barrier, inc=1, device_id={"head": (h + o) % N_HEAD}, device_id_type=MESH
        )

    for o in (1, 2, 3):
        pl.semaphore_signal(barrier, inc=1, device_id={"grp": (g + o) % NG}, device_id_type=MESH)

    depth = prompt.shape[1]
    tokens = prompt.shape[0]
    chunks = depth // KCHUNK
    loads = []
    for k in range(chunks):
        cols = pl.ds(k * KCHUNK, KCHUNK)
        loads.append(
            [
                pltpu.make_async_copy(
                    prompt.at[:, cols], pbuf.at[pl.ds(0, tokens), cols], load_sem.at[k, 0]
                ),
                pltpu.make_async_copy(
                    hidden.at[:, :, cols], hbuf.at[:, :, cols], load_sem.at[k, 1]
                ),
                pltpu.make_async_copy(w_dkv.at[:, cols], wbuf.at[:, cols], load_sem.at[k, 2]),
            ]
        )
    for group in loads:
        start(group)
    uq_copy = pltpu.make_async_copy(w_uq, uq_buf, w_sem.at[0])
    uk_copy = pltpu.make_async_copy(w_uk, uk_buf, w_sem.at[1])
    uv_copy = pltpu.make_async_copy(w_uv, uv_buf, w_sem.at[2])
    wo_copy = pltpu.make_async_copy(w_o, wbuf.at[pl.ds(0, w_o.shape[0])], w_sem.at[3])
    start([uq_copy, uk_copy, uv_copy])

    qpart[...] = dot(hpart[...], w_dq[...])
    pl.semaphore_wait(barrier, N_HEAD - 1 + 3)

    def q_block(i):
        return (
            pl.ds(pl.multiple_of((i // 4) * 8, 8), 8),
            pl.ds(pl.multiple_of((i % 4) * 384, 128), 384),
        )

    def share_copy(to):
        return remote(qpart.at[q_block(to)], rq_land.at[h], r_send.at[to], r_recv.at[h], {"head": to})

    def sum_copy(to):
        return remote(red, qlat.at[q_block(h)], g_send.at[to], g_recv.at[h], {"head": to})

    @pl.loop(1, N_HEAD)
    def _(o):
        share_copy((h + o) % N_HEAD).start()

    for k in range(chunks):
        if k == 4:
            rq_land[h] = qpart[q_block(h)]

            @pl.loop(1, N_HEAD)
            def _(o):
                src = (h + o) % N_HEAD
                remote(
                    rq_land.at[src], rq_land.at[src], r_send.at[src], r_recv.at[src], {"head": src}
                ).wait_recv()

            red[...] = jnp.sum(rq_land[...], axis=0)
            qlat[q_block(h)] = red[...]

            @pl.loop(1, N_HEAD)
            def _(o):
                sum_copy((h + o) % N_HEAD).start()

        for one in loads[k]:
            one.wait()
        cols = slice(k * KCHUNK, (k + 1) * KCHUNK)
        pbuf[tokens:, cols] = hbuf[:, :, cols].reshape(64, KCHUNK)
        piece = dot_t(pbuf[:, cols], wbuf[:, cols])
        if k == 0:
            acc[...] = piece
        else:
            acc[...] += piece
    wo_copy.start()

    pages = tokens // PAGE
    lat_own[...] = (
        norm_rows(acc[0:tokens, 0:LAT], kv_gain[...], LAT).astype(BF16).reshape(pages, PAGE, LAT)
    )
    halves = []
    for p in range(pages):
        first = acc[p * PAGE : p * PAGE + 32, LAT : LAT + ROPE]
        second = acc[p * PAGE + 32 : p * PAGE + 64, LAT : LAT + ROPE]
        halves.append(jnp.concatenate([first, second], axis=1))
    packed = jnp.concatenate(halves, axis=0)
    rope_own[...] = (
        rotate_pairs(packed, page_cos[...], page_sin[...]).astype(BF16).reshape(pages, 32, 128)
    )

    for j in range(4):
        rank = (g + OFFS[j]) % NG
        for k in range(SLOT):
            page = send_idx[rank * SLOT + k]
            zlat[j, k * PAGE : (k + 1) * PAGE, :] = lat_own[page]
            zrope[j, k * 32 : (k + 1) * 32, :] = rope_own[page]

    def z_copies(j):
        rank = (g + OFFS[j]) % NG
        return [
            remote(
                src.at[j], dst.at[b, g], z_send.at[j - 1, i], z_recv.at[j - 1, i], {"grp": rank}
            )
            for i, (src, dst) in enumerate(((zlat, lat_all), (zrope, rope_all)))
        ]

    def plane(j):
        return (g + NG - OFFS[j]) % NG

    def block_at(dx, core):
        return ((x + dx) % 4) * 2 + core

    def ring_copies(j, dx, to, send, recv):
        gs = plane(j)
        at = block_at(dx, c)
        res = []
        for i, (mine, ref) in enumerate(((zlat, lat_all), (zrope, rope_all))):
            src = mine.at[0] if (j == 0 and dx == 0) else ref.at[at, gs]
            res.append(remote(src, ref.at[at, gs], send.at[i], recv.at[i], {"head": to}))
        return res

    def to_right(j):
        return ring_copies(j, 0, right, x_send.at[j, 0], x_recv.at[j, 0])

    def to_left(j):
        return ring_copies(j, 0, left, x_send.at[j, 1], x_recv.at[j, 1])

    def onward(j):
        if j in (0, 3):
            return ring_copies(j, 3, right, f_send.at[j], f_recv.at[j])
        return ring_copies(j, 1, left, f_send.at[j], f_recv.at[j])

    def across(j, dx):
        return ring_copies(j, dx, sibling, c_send.at[j, dx], c_recv.at[j, dx])

    def arrived(j, dx, core, sem):
        gs = plane(j)
        at = block_at(dx, core)
        for i, ref in enumerate((lat_all, rope_all)):
            remote(
                ref.at[at, gs], ref.at[at, gs], sem.at[i], sem.at[i], {"head": sibling}
            ).wait_recv()

    def serve_own(j):
        if j > 0:
            arrived(j, 0, c, z_recv.at[j - 1])
        start(to_right(j))
        start(to_left(j))
        start(across(j, 0))

    def serve_near(j):
        arrived(j, 3, c, x_recv.at[j, 0])
        if j in (0, 3):
            start(onward(j))
        start(across(j, 3))
        arrived(j, 1, c, x_recv.at[j, 1])
        if j in (1, 2):
            start(onward(j))
        start(across(j, 1))

    def serve_far(j):
        arrived(j, 2, c, f_recv.at[j])
        start(across(j, 2))

    def from_sibling(j, places):
        for dx in places:
            arrived(j, dx, other, c_recv.at[j, dx])

    for j in (1, 2, 3):
        start(z_copies(j))
    own = [
        pltpu.make_async_copy(zlat.at[0], lat_all.at[b, g], own_sem.at[0]),
        pltpu.make_async_copy(zrope.at[0], rope_all.at[b, g], own_sem.at[1]),
    ]
    start(own)
    serve_own(0)

    new_lat[...] = norm_rows(acc[tokens : tokens + 64, 0:LAT], kv_gain[...], LAT).astype(BF16)
    new_r = acc[tokens : tokens + 64, LAT : LAT + ROPE]
    new_r = rotate_pairs(jnp.concatenate([new_r, new_r], axis=1), new_cos[...], new_sin[...])
    lane = lax.broadcasted_iota(jnp.int32, new_r.shape, 1)
    new_rope[...] = jnp.where(lane < ROPE, new_r, 0.0).astype(BF16)

    @pl.loop(1, N_HEAD)
    def _(o):
        src = (h + o) % N_HEAD
        remote(
            red, qlat.at[q_block(src)], g_send.at[src], g_recv.at[src], {"head": src}
        ).wait_recv()

    uq_copy.wait()
    uk_copy.wait()
    query_norm = norm_rows(qlat[...], q_gain[...], QL).astype(BF16)
    queries = dot(query_norm, uq_buf[...])
    parts = []
    ropes = []
    for n in range(NH):
        at = n * (NOPE + ROPE)
        parts.append(dot(queries[:, at : at + NOPE].astype(BF16), uk_buf[n]).astype(BF16))
        one = queries[:, at + NOPE : at + NOPE + ROPE]
        one = jnp.concatenate([one, one], axis=1)
        ropes.append(rotate_pairs(one, new_cos[...], new_sin[...]).astype(BF16))
    order = rows_by_request(False)
    qmine[...] = dot(order, jnp.concatenate(parts, axis=0)).astype(BF16)
    qrmine[...] = dot(order, jnp.concatenate(ropes, axis=0)).astype(BF16)

    def y_copies(o):
        to = ((y + o) % NY) * NB + b
        return [
            remote(src, dst.at[y], y_send.at[o - 1, i], y_recv.at[o - 1, i], {"head": to})
            for i, (src, dst) in enumerate(((qmine, q_lat), (qrmine, q_rope)))
        ]

    for o in (2, 1, 3):
        start(y_copies(o))
    q_lat[y] = qmine[...]
    q_rope[y] = qrmine[...]

    serve_near(0)
    serve_own(1)
    serve_own(2)
    serve_far(0)
    serve_own(3)

    s = (dot_t(qmine[...], new_lat[...]) + dot_t(qrmine[...], new_rope[...])) * scale
    i = lax.broadcasted_iota(jnp.int32, s.shape, 0)
    j = lax.broadcasted_iota(jnp.int32, s.shape, 1)
    live = ((i >> 3) == (j >> 1)) & ((j & 1) <= (i & 1))
    s = jnp.where(live, s, LOW)
    top = jnp.max(s, axis=1, keepdims=True)
    p = jnp.where(live, jnp.exp(s - top), 0.0)
    total = jnp.sum(p, axis=1, keepdims=True)
    new_o[...] = dot(p.astype(BF16), new_lat[...]) / total
    new_lse[...] = jnp.broadcast_to(top + jnp.log(total), new_lse.shape)

    serve_near(1)

    for o in (1, 3, 2):
        src = (y + NY - o) % NY
        for n, ref in enumerate((q_lat, q_rope)):
            remote(
                ref.at[src],
                ref.at[src],
                y_send.at[o - 1, n],
                y_recv.at[o - 1, n],
                {"head": src * NB + b},
            ).wait_recv()
    requests = 32
    for yb in range(NY):
        qf[:, yb * 8 : (yb + 1) * 8, 0:LAT] = q_lat[yb].astype(F32).reshape(requests, 8, LAT)
        qf[:, yb * 8 : (yb + 1) * 8, LAT:] = q_rope[yb].astype(F32).reshape(requests, 8, 128)
    qb[0:requests] = qf[...].astype(BF16)
    qb[requests] = jnp.zeros((32, LAT + 128), BF16)

    row = lax.broadcasted_iota(jnp.int32, (SLOT * 32, ROWS), 0)
    col = lax.broadcasted_iota(jnp.int32, (SLOT * 32, ROWS), 1)
    own_page = (row >> 5) == (col >> 6)
    low_lane = lax.broadcasted_iota(jnp.int32, (32, 128), 1) < ROPE

    def attend(at, gs):
        first = (at * NG + gs) * SLOT
        keys = lat_all[at, gs]
        pairs = rope_all[at, gs]
        zero = jnp.zeros((32, 128), BF16)
        ropes = []
        for k in range(SLOT):
            pair = pairs[k * 32 : (k + 1) * 32, :]
            ropes += [jnp.where(low_lane, pair, zero), jnp.where(low_lane, zero, pair)]
        q = jnp.concatenate([qb[owner[first + k]] for k in range(SLOT)], axis=0)
        s = dot_t(q[:, 0:LAT], keys) + dot_t(q[:, LAT:], jnp.concatenate(ropes, axis=0))
        s = jnp.where(own_page, s * scale, LOW)
        top = jnp.max(s, axis=1, keepdims=True)
        p = jnp.where(own_page, jnp.exp(s - top), 0.0)
        total = jnp.sum(p, axis=1, keepdims=True)
        o = dot(p.astype(BF16), keys)
        top = jnp.broadcast_to(top, (SLOT * 32, 128))
        total = jnp.broadcast_to(total, (SLOT * 32, 128))
        o_slot[pl.ds(first, SLOT)] = o.astype(BF16).reshape(SLOT, 32, LAT)
        m_slot[pl.ds(first, SLOT)] = top.reshape(SLOT, 32, 128)
        l_slot[pl.ds(first, SLOT)] = total.reshape(SLOT, 32, 128)

    def gray(j):
        return j ^ (j >> 1)

    def attend_own(n, core, dx, j0):
        @pl.loop(0, n // 2)
        def _(i):
            for u in range(2):
                attend(block_at(dx, core), (g + NG - gray(j0 + 2 * i + u)) % NG)

    def attend_places(j, core, places):
        for dx in places:
            attend(block_at(dx, core), plane(j))

    def attend_ring(j, core):
        @pl.loop(0, 2)
        def _(i):
            for u in range(2):
                attend(block_at(2 * i + u, core), plane(j))

    for one in own:
        one.wait()
    o_slot[96] = jnp.zeros((32, LAT), BF16)
    m_slot[96] = jnp.full((32, 128), LOW, F32)
    l_slot[96] = jnp.zeros((32, 128), F32)
    attend_own(4, c, 0, 0)
    serve_near(2)
    attend_places(0, c, (1, 3))
    serve_far(1)
    attend_places(0, c, (2,))
    attend_places(1, c, (1, 3))
    serve_far(2)
    from_sibling(0, (0, 1, 2, 3))
    attend_ring(0, other)
    serve_near(3)
    attend_places(2, c, (1, 3))
    attend_places(1, c, (2,))
    from_sibling(1, (0, 1, 2, 3))
    attend_ring(1, other)
    serve_far(3)
    attend_places(2, c, (2,))
    attend_places(3, c, (1, 3))
    from_sibling(2, (0, 1, 2, 3))
    attend_ring(2, other)
    attend_places(3, c, (2,))
    from_sibling(3, (0, 1, 2, 3))
    attend_ring(3, other)

    @pl.loop(0, requests // 2)
    def _(pair):
        mixes = []
        for u in range(2):
            r = pair * 2 + u
            at = [listed[r * MAXP + k] for k in range(MAXP)]
            tops = [m_slot[one] for one in at]
            top = tops[0]
            for one in tops[1:]:
                top = jnp.maximum(top, one)
            total = jnp.zeros((32, 128), F32)
            mixed = jnp.zeros((32, LAT), F32)
            for one, its_top in zip(at, tops):
                e = jnp.exp(its_top - top)
                total += l_slot[one] * e
                mixed += o_slot[one].astype(F32) * e[:, 0:1]
            some = total > 0.0
            safe = jnp.where(some, total, 1.0)
            lse = jnp.where(some, top + jnp.log(safe), LOW)
            mixed = mixed * (1.0 / safe)[:, 0:1]
            mixes.append(mixed)
            for yb in range(NY):
                lse_rows[yb, pl.ds(pl.multiple_of(r * 8, 8), 8), :] = lse[yb * 8 : (yb + 1) * 8]
        for yb in range(NY):
            rows = slice(yb * 8, (yb + 1) * 8)
            both = jnp.concatenate([mixes[0][rows], mixes[1][rows]], axis=0)
            part[yb, pl.ds(pl.multiple_of(pair * 16, 16), 16), :] = both.astype(BF16)

    for yb in range(NY):
        stats[yb] = jnp.transpose(lse_rows[yb])[0:8, :]

    def o_copies(o):
        ty = (y + o) % NY
        return [
            remote(
                src.at[ty],
                dst.at[o - 1],
                o_send.at[o - 1, i],
                o_recv.at[o - 1, i],
                {"head": ty * NB + b},
            )
            for i, (src, dst) in enumerate(((part, o_land), (stats, s_land)))
        ]

    for o in (2, 1, 3):
        start(o_copies(o))

    def column(block):
        t_buf[0:8, :] = block
        return jnp.transpose(t_buf[...])[:, 0:1]

    t_buf[...] = jnp.zeros_like(t_buf)
    lses = [new_lse[:, 0:1], column(stats[y])]
    mixes = [new_o[...], part[y].astype(F32)]
    for o in (1, 3, 2):
        wait_recv(o_copies(o))
        lses.append(column(s_land[o - 1]))
        mixes.append(o_land[o - 1].astype(F32))
    top = lses[0]
    for one in lses[1:]:
        top = jnp.maximum(top, one)
    weights = [jnp.exp(one - top) for one in lses]
    total = weights[0]
    for one in weights[1:]:
        total = total + one
    mixed = mixes[0] * (weights[0] / total)
    for one, weight in zip(mixes[1:], weights[1:]):
        mixed += one * (weight / total)
    by_head = dot(rows_by_request(True), mixed.astype(BF16)).astype(BF16)
    uv_copy.wait()
    for n in range(NH):
        vals[:, n * 128 : (n + 1) * 128] = dot(
            by_head[n * 64 : (n + 1) * 64, :], uv_buf[n]
        ).astype(BF16)

    wo_copy.wait()
    width = out.shape[1]
    span = width * NB
    chip = y * 4 + x

    def pair_copy(ty):
        chips = pl.ds(ty * 4, 4)
        return remote(
            sbuf.at[other, chips], sib_land.at[chips], p_send.at[ty], p_recv.at[ty], {"head": sibling}
        )

    for n in range(NY):
        ty = (y + n) % NY
        cols = pl.ds(pl.multiple_of(ty * span, 128), span)
        piece = dot(vals[...], wbuf[0 : w_o.shape[0], cols])
        for k in range(NB):
            sbuf[k % 2, ty * 4 + k // 2] = piece[:, k * width : (k + 1) * width].astype(BF16)
        pair_copy(ty).start()

    def out_copy(t):
        return remote(
            tbuf.at[t], rbuf.at[chip], d_send.at[t], d_recv.at[chip], {"head": t * 2 + c}
        )

    for n in (1, 2, 3, 0):
        ty = (y + n) % NY
        pair_copy(ty).wait_recv()
        for k in range(4):
            t = ty * 4 + k
            tbuf[t] = (sbuf[c, t].astype(F32) + sib_land[t].astype(F32)).astype(BF16)

            @pl.when(t != chip)
            def _():
                out_copy(t).start()

    def body(o, total):
        src = (chip + o) % 16
        remote(
            rbuf.at[src], rbuf.at[src], d_send.at[src], d_recv.at[src], {"head": src * 2 + c}
        ).wait_recv()
        return total + rbuf[src].astype(F32)

    result = lax.fori_loop(1, 16, body, tbuf[chip].astype(F32))
    out[...] = result.astype(BF16)

    for j in (1, 2, 3):
        wait_send(z_copies(j))
    for j in range(4):
        wait_send(to_right(j))
        wait_send(to_left(j))
        wait_send(onward(j))
        for dx in range(4):
            wait_send(across(j, dx))
    for o in (1, 2, 3):
        wait_send(y_copies(o))
        wait_send(o_copies(o))
    for ty in range(NY):
        pair_copy(ty).wait_send()

    @pl.loop(1, 16)
    def _(o):
        out_copy((chip + o) % 16).wait_send()

    @pl.loop(1, N_HEAD)
    def _(o):
        to = (h + o) % N_HEAD
        share_copy(to).wait_send()
        sum_copy(to).wait_send()


def spec(space):
    return pl.BlockSpec(memory_space=space)


VM, SM, ANY = pltpu.VMEM, pltpu.SMEM, pl.ANY


def page_plan(block_table, ctx_pages, g, y, b, per_rank, pages_dev):
    flat = jnp.where(
        jnp.arange(MAXP, dtype=jnp.int32)[None, :] < ctx_pages[:, None], block_table, -1
    ).reshape(1, -1)
    at = jnp.arange(NG * NB * pages_dev, dtype=jnp.int32)
    per_plane = NB * pages_dev
    ids = (at // per_plane) * (N_HEAD * pages_dev) + y * per_plane + at % per_plane
    codes = jnp.arange(flat.shape[1], dtype=jnp.int32)[None, :]
    code = jnp.sum(jnp.where(flat == ids[:, None], codes, 0), axis=1)
    code = code.reshape(NG, NB, pages_dev)
    target = code // (per_rank * MAXP)
    within = jnp.arange(pages_dev, dtype=jnp.int32)
    alike = (target[..., :, None] == target[..., None, :]) & (within[None, :] < within[:, None])
    slot = jnp.sum(alike.astype(jnp.int32), axis=-1)
    places = jnp.arange(SLOT, dtype=jnp.int32)
    here = (target == g)[..., None, :] & (slot[..., None, :] == places[:, None])
    local = code % (per_rank * MAXP)
    held = jnp.sum(jnp.where(here, local[..., None, :] + 1, 0), axis=-1) - 1
    held = held.transpose(1, 0, 2).reshape(-1)
    owner = jnp.where(held >= 0, held // MAXP, per_rank)
    wanted = jnp.arange(per_rank * MAXP, dtype=jnp.int32)
    total = held.shape[0]
    spare = jnp.arange(total, dtype=jnp.int32) - total
    listed = total + jnp.sum(jnp.where(held[None, :] == wanted[:, None], spare[None, :], 0), axis=1)
    mine = lax.dynamic_slice(code, (g, b, 0), (1, 1, pages_dev)).reshape(-1)
    my_target = lax.dynamic_slice(target, (g, b, 0), (1, 1, pages_dev)).reshape(-1)
    my_slot = lax.dynamic_slice(slot, (g, b, 0), (1, 1, pages_dev)).reshape(-1)
    sends = (my_target[None, :] * SLOT + my_slot[None, :]) == jnp.arange(
        NG * SLOT, dtype=jnp.int32
    )[:, None]
    send_idx = jnp.sum(jnp.where(sends, within[None, :], 0), axis=1)
    return owner, listed, send_idx, mine % MAXP


def angle_tables(positions):
    lane = jnp.arange(2 * ROPE, dtype=jnp.int32)
    inverse_freq = 10000.0 ** (-2.0 * (lane % 32).astype(F32) / ROPE)
    angles = jnp.repeat(positions.astype(F32), ROPE, axis=1) * inverse_freq[None, :]
    sign = jnp.where((lane % ROPE) < 32, -1.0, 1.0).astype(F32)
    return jnp.cos(angles), jnp.sin(angles) * sign[None, :]


def on_device(
    prompt, w_dkv, kv_gain, block_table, ctx_pages, dec_hidden, w_dq, q_gain, w_uq, w_uk, w_uv, w_o
):
    g = lax.axis_index("grp")
    h = lax.axis_index("head")
    y, b = h // NB, h % NB
    tokens, depth = prompt.shape
    pages_dev = tokens // PAGE
    per_rank = dec_hidden.shape[0]
    owner, listed, send_idx, my_depth = page_plan(
        block_table, ctx_pages, g, y, b, per_rank, pages_dev
    )
    lengths = lax.dynamic_slice_in_dim(ctx_pages, g * per_rank, per_rank, 0)
    t = jnp.arange(32, dtype=jnp.int32)
    page_pos = my_depth[:, None, None] * PAGE + t[None, :, None] + jnp.array([0, 32], jnp.int32)
    page_cos, page_sin = angle_tables(page_pos.reshape(-1, 2))
    new_pos = (lengths[:, None] * PAGE + jnp.arange(2, dtype=jnp.int32)[None, :]).reshape(-1, 1)
    new_cos, new_sin = angle_tables(jnp.concatenate([new_pos, new_pos], axis=1))
    share = w_dq.shape[0]
    hpart = lax.dynamic_slice_in_dim(dec_hidden, h * share, share, 2).reshape(-1, share)

    dma = pltpu.SemaphoreType.DMA
    width = depth // N_HEAD
    slots = NB * NG * SLOT
    out = pl.pallas_call(
        fused_kernel,
        out_shape=jax.ShapeDtypeStruct((64, width), BF16),
        in_specs=[spec(SM)] * 3 + [spec(VM)] * 8 + [spec(ANY)] * 7,
        out_specs=spec(VM),
        scratch_shapes=[
            pltpu.VMEM((tokens + 64, depth), BF16),
            pltpu.VMEM((per_rank, 2, depth), BF16),
            pltpu.VMEM((LAT + ROPE, depth), BF16),
            pltpu.VMEM((tokens + 64, LAT + ROPE), F32),
            pltpu.VMEM(w_uq.shape, BF16),
            pltpu.VMEM(w_uk.shape, BF16),
            pltpu.VMEM(w_uv.shape, BF16),
            pltpu.VMEM((pages_dev, PAGE, LAT), BF16),
            pltpu.VMEM((pages_dev, 32, 128), BF16),
            pltpu.VMEM((NG, ROWS, LAT), BF16),
            pltpu.VMEM((NG, RROWS, 128), BF16),
            pltpu.VMEM((64, QL), F32),
            pltpu.VMEM((N_HEAD, 8, 384), F32),
            pltpu.VMEM((8, 384), F32),
            pltpu.VMEM((64, QL), F32),
            pltpu.VMEM((256, LAT), BF16),
            pltpu.VMEM((256, 128), BF16),
            pltpu.VMEM((64, LAT), BF16),
            pltpu.VMEM((64, 128), BF16),
            pltpu.VMEM((256, LAT), F32),
            pltpu.VMEM((256, 128), F32),
            pltpu.VMEM((NB, NG, ROWS, LAT), BF16),
            pltpu.VMEM((NB, NG, RROWS, 128), BF16),
            pltpu.VMEM((NY, 256, LAT), BF16),
            pltpu.VMEM((NY, 256, 128), BF16),
            pltpu.VMEM((32, 32, LAT + 128), F32),
            pltpu.VMEM((33, 32, LAT + 128), BF16),
            pltpu.VMEM((slots + 1, 32, LAT), BF16),
            pltpu.VMEM((slots + 1, 32, 128), F32),
            pltpu.VMEM((slots + 1, 32, 128), F32),
            pltpu.VMEM((NY, 256, LAT), BF16),
            pltpu.VMEM((NY, 256, 128), F32),
            pltpu.VMEM((NY, 8, 256), F32),
            pltpu.VMEM((3, 256, LAT), BF16),
            pltpu.VMEM((3, 8, 256), F32),
            pltpu.VMEM((128, 256), F32),
            pltpu.VMEM((64, LAT), BF16),
            pltpu.VMEM((2, 16, 64, width), BF16),
            pltpu.VMEM((16, 64, width), BF16),
            pltpu.VMEM((16, 64, width), BF16),
            pltpu.VMEM((16, 64, width), BF16),
            dma((depth // KCHUNK, 3)),
            dma((4,)),
            dma((2,)),
            dma((3, 2)),
            dma((3, 2)),
            dma((4, 2, 2)),
            dma((4, 2, 2)),
            dma((4, 2)),
            dma((4, 2)),
            dma((4, 4, 2)),
            dma((4, 4, 2)),
            dma((N_HEAD,)),
            dma((N_HEAD,)),
            dma((N_HEAD,)),
            dma((N_HEAD,)),
            dma((3, 2)),
            dma((3, 2)),
            dma((3, 2)),
            dma((3, 2)),
            dma((4,)),
            dma((4,)),
            dma((16,)),
            dma((16,)),
        ],
        compiler_params=pltpu.CompilerParams(
            collective_id=0, has_side_effects=True, vmem_limit_bytes=58 * 1024 * 1024
        ),
    )(
        send_idx,
        owner,
        listed,
        hpart,
        w_dq,
        kv_gain.reshape(1, -1),
        q_gain.reshape(1, -1),
        page_cos,
        page_sin,
        new_cos,
        new_sin,
        prompt,
        dec_hidden,
        w_dkv.T,
        w_uq,
        w_uk,
        w_uv,
        w_o,
    )
    return out.reshape(per_rank, 2, width)


def solution(mesh):
    return jax.shard_map(
        on_device,
        mesh=mesh,
        in_specs=(
            P(("grp", "head"), None),
            P(),
            P(),
            P(),
            P(),
            P("grp", None, None),
            P("head", None),
            P(),
            P(None, "head"),
            P("head", None, None),
            P("head", None, None),
            P("head", None),
        ),
        out_specs=P("grp", None, "head"),
        check_vma=False,
    )
```

```python
import jax
import jax.numpy as jnp
import numpy as np
from jax import lax
from jax.experimental import pallas as pl
from jax.experimental.pallas import tpu as pltpu
from jax.sharding import PartitionSpec as P

PAGE = 64
SLOT = 3
MAXP = 16
LAT = 512
ROPE = 64
NOPE = 128
QL = 1536
NH = 4
NG = 4
NY = 4
NB = 8
N_HEAD = 32
ROWS = SLOT * PAGE
RROWS = SLOT * PAGE // 2
KCHUNK = 1024
AHEAD = 3
OFFS = (0, 1, 3, 2)
MESH = pl.DeviceIdType.MESH
F32 = jnp.float32
BF16 = jnp.bfloat16
LOW = -1e30


def dot(a, b):
    return jnp.dot(a, b, preferred_element_type=F32)


def dot_t(a, b):
    return lax.dot_general(a, b, (((1,), (1,)), ((), ())), preferred_element_type=F32)


def norm_rows(values, gain_row, width):
    mean = jnp.sum(values * values, axis=-1, keepdims=True) * (1.0 / width)
    return values * lax.rsqrt(mean + 1e-06) * gain_row


def rotate_pairs(x, cosine, signed_sine):
    lane = lax.broadcasted_iota(jnp.int32, x.shape, 1)
    swapped = jnp.where((lane & 63) < 32, pltpu.roll(x, 96, 1), pltpu.roll(x, 32, 1))
    return x * cosine + swapped * signed_sine


def rows_by_request(transposed):
    i = lax.broadcasted_iota(jnp.int32, (256, 256), 1 if transposed else 0)
    j = lax.broadcasted_iota(jnp.int32, (256, 256), 0 if transposed else 1)
    place = ((i >> 1) & 3) * 64 + (i >> 3) * 2 + (i & 1)
    return jnp.where(j == place, 1.0, 0.0).astype(BF16)


def fused_kernel(
    send_idx,
    owner,
    listed,
    depths,
    lengths,
    kv_gain,
    q_gain,
    cos_far,
    sin_far,
    cos_near,
    sin_near,
    prompt,
    hidden,
    w_dq,
    w_dkv,
    w_uq,
    w_uk,
    w_uv,
    w_o,
    out,
    pbuf,
    hbuf,
    wbuf,
    acc,
    uq_buf,
    uk_buf,
    uv_buf,
    lat_own,
    rope_own,
    zlat,
    zrope,
    wdq_buf,
    new_cos,
    new_sin,
    qpart,
    pair_land,
    half,
    rq_land,
    red,
    qlat,
    qmine,
    qr_dup,
    qrmine,
    new_lat,
    new_rope,
    new_o,
    new_lse,
    lat_all,
    rope_all,
    q_lat,
    q_rope,
    qf,
    qb,
    o_slot,
    m_slot,
    l_slot,
    part,
    lse_rows,
    stats,
    o_land,
    s_land,
    t_buf,
    vals,
    sbuf,
    sib_land,
    tbuf,
    rbuf,
    load_sem,
    w_sem,
    own_sem,
    z_send,
    z_recv,
    x_send,
    x_recv,
    f_send,
    f_recv,
    c_send,
    c_recv,
    q_sem,
    r_send,
    r_recv,
    g_send,
    g_recv,
    y_send,
    y_recv,
    o_send,
    o_recv,
    s_send,
    s_recv,
    p_send,
    p_recv,
    d_send,
    d_recv,
):
    g = lax.axis_index("grp")
    h = lax.axis_index("head")
    y = h // NB
    b = h % NB
    x = b // 2
    c = b % 2
    other = 1 - c
    sibling = y * NB + x * 2 + other
    right = y * NB + ((x + 1) % 4) * 2 + c
    left = y * NB + ((x + 3) % 4) * 2 + c
    scale = (NOPE + ROPE) ** (-0.5)

    def start(copies):
        for one in copies:
            one.start()

    def wait_recv(copies):
        for one in copies:
            one.wait_recv()

    def wait_send(copies):
        for one in copies:
            one.wait_send()

    def remote(src, dst, send, recv, to):
        return pltpu.make_async_remote_copy(
            src_ref=src,
            dst_ref=dst,
            send_sem=send,
            recv_sem=recv,
            device_id=to,
            device_id_type=MESH,
        )

    barrier = pltpu.get_barrier_semaphore()

    @pl.loop(1, N_HEAD)
    def _(o):
        pl.semaphore_signal(
            barrier, inc=1, device_id={"head": (h + o) % N_HEAD}, device_id_type=MESH
        )

    for o in (1, 2, 3):
        pl.semaphore_signal(barrier, inc=1, device_id={"grp": (g + o) % NG}, device_id_type=MESH)

    depth = prompt.shape[1]
    tokens = prompt.shape[0]
    chunks = depth // KCHUNK
    loads = []
    for k in range(chunks):
        cols = pl.ds(k * KCHUNK, KCHUNK)
        loads.append(
            [
                pltpu.make_async_copy(
                    prompt.at[:, cols], pbuf.at[pl.ds(0, tokens), cols], load_sem.at[k, 0]
                ),
                pltpu.make_async_copy(w_dkv.at[:, cols], wbuf.at[:, cols], load_sem.at[k, 1]),
            ]
        )
    share = w_dq.shape[0]
    window = 384
    first_col = jnp.minimum((h * share) // 128 * 128, depth - window)
    at_row = pl.multiple_of(h * share - first_col, 32)
    hidden_copy = pltpu.make_async_copy(hidden, hbuf, w_sem.at[4])
    hidden_copy.start()
    wdq_buf[...] = jnp.zeros_like(wdq_buf)
    dq_copy = pltpu.make_async_copy(w_dq, wdq_buf.at[pl.ds(at_row, share), :], w_sem.at[5])
    dq_copy.start()
    for group in loads[:AHEAD]:
        start(group)
    uq_copy = pltpu.make_async_copy(w_uq, uq_buf, w_sem.at[0])
    uk_copy = pltpu.make_async_copy(w_uk, uk_buf, w_sem.at[1])
    uv_copy = pltpu.make_async_copy(w_uv, uv_buf, w_sem.at[2])
    wo_copy = pltpu.make_async_copy(w_o, wbuf.at[pl.ds(0, w_o.shape[0])], w_sem.at[3])

    requests = hidden.shape[0]
    for r in range(requests):
        far = lengths[g * requests + r]
        new_cos[2 * r : 2 * r + 2, :] = jnp.broadcast_to(cos_far[pl.ds(far, 1), :], (2, 128))
        new_sin[2 * r : 2 * r + 2, :] = jnp.broadcast_to(sin_far[pl.ds(far, 1), :], (2, 128))
    odd = (lax.broadcasted_iota(jnp.int32, (64, 128), 0) & 1) == 1
    step_cos = jnp.where(odd, cos_far[18:19, :], cos_far[17:18, :])
    step_sin = jnp.where(odd, sin_far[18:19, :], sin_far[17:18, :])
    far_cos, far_sin = new_cos[...], new_sin[...]
    sign = jnp.where(
        (lax.broadcasted_iota(jnp.int32, (1, 128), 1) & 63) < 32, -1.0, 1.0
    ).astype(F32)
    new_cos[...] = far_cos * step_cos - far_sin * step_sin
    new_sin[...] = (far_sin * step_cos + far_cos * step_sin) * sign

    hidden_copy.wait()
    dq_copy.wait()
    part_of_hidden = hbuf[:, :, pl.ds(pl.multiple_of(first_col, 128), window)].reshape(64, window)
    qpart[...] = dot(part_of_hidden, wdq_buf[...])

    chip = y * 4 + x
    half_width = QL // 2

    def half_cols(core):
        return pl.ds(pl.multiple_of(core * half_width, 128), half_width)

    def block_in(t, first):
        return (
            pl.ds(pl.multiple_of((t // 2) * 8, 8), 8),
            pl.ds(pl.multiple_of(first + (t % 2) * 384, 128), 384),
        )

    def halves_copy():
        return remote(
            qpart.at[:, half_cols(other)], pair_land, q_sem.at[0], q_sem.at[1], {"head": sibling}
        )

    def share_copy(t):
        return remote(
            half.at[block_in(t, 0)], rq_land.at[chip], r_send.at[t], r_recv.at[chip], {"head": t * 2 + c}
        )

    def sum_copy(t):
        return remote(
            red,
            qlat.at[block_in(chip, c * half_width)],
            g_send.at[t],
            g_recv.at[chip],
            {"head": t * 2 + c},
        )

    def back_copy():
        return remote(
            qlat.at[:, half_cols(c)],
            qlat.at[:, half_cols(c)],
            q_sem.at[2],
            q_sem.at[3],
            {"head": sibling},
        )

    def share_sums():
        halves_copy().wait_recv()
        half[...] = qpart[:, half_cols(c)] + pair_land[...]
        rq_land[chip] = half[block_in(chip, 0)]

        @pl.loop(1, 16)
        def _(o):
            share_copy((chip + o) % 16).start()

    def send_sums():
        @pl.loop(1, 16)
        def _(o):
            src = (chip + o) % 16
            remote(
                rq_land.at[src], rq_land.at[src], r_send.at[src], r_recv.at[src], {"head": src * 2 + c}
            ).wait_recv()

        red[...] = jnp.sum(rq_land[...], axis=0)
        qlat[block_in(chip, c * half_width)] = red[...]

        @pl.loop(1, 16)
        def _(o):
            sum_copy((chip + o) % 16).start()

    for k in range(chunks):
        if k == 2:
            pl.semaphore_wait(barrier, N_HEAD - 1 + 3)
            halves_copy().start()
        if k == 3:
            share_sums()
        for one in loads[k]:
            one.wait()
        if k + AHEAD < chunks:
            start(loads[k + AHEAD])
        elif k + AHEAD == chunks:
            start([uq_copy, uk_copy, uv_copy])
        cols = slice(k * KCHUNK, (k + 1) * KCHUNK)
        pbuf[tokens:, cols] = hbuf[:, :, cols].reshape(64, KCHUNK)
        piece = dot_t(pbuf[:, cols], wbuf[:, cols])
        if k == 0:
            acc[...] = piece
        else:
            acc[...] += piece
    send_sums()
    wo_copy.start()

    pages = tokens // PAGE
    lat_own[...] = (
        norm_rows(acc[0:tokens, 0:LAT], kv_gain[...].reshape(1, LAT), LAT).astype(BF16).reshape(pages, PAGE, LAT)
    )
    halves = []
    for p in range(pages):
        first = acc[p * PAGE : p * PAGE + 32, LAT : LAT + ROPE]
        second = acc[p * PAGE + 32 : p * PAGE + 64, LAT : LAT + ROPE]
        halves.append(jnp.concatenate([first, second], axis=1))
    packed = jnp.concatenate(halves, axis=0)
    page_cos = []
    page_sin = []
    for p in range(pages):
        far = pl.ds(depths[p], 1)
        far_cos, far_sin = cos_far[far, :], sin_far[far, :]
        page_cos.append(far_cos * cos_near[...] - far_sin * sin_near[...])
        page_sin.append((far_sin * cos_near[...] + far_cos * sin_near[...]) * sign)
    page_cos = jnp.concatenate(page_cos, axis=0)
    page_sin = jnp.concatenate(page_sin, axis=0)
    rope_own[...] = (
        rotate_pairs(packed, page_cos, page_sin).astype(BF16).reshape(pages, 32, 128)
    )

    for j in range(4):
        rank = (g + OFFS[j]) % NG
        for k in range(SLOT):
            page = send_idx[rank * SLOT + k]
            zlat[j, k * PAGE : (k + 1) * PAGE, :] = lat_own[page]
            zrope[j, k * 32 : (k + 1) * 32, :] = rope_own[page]

    def z_copies(j):
        rank = (g + OFFS[j]) % NG
        return [
            remote(
                src.at[j], dst.at[b, g], z_send.at[j - 1, i], z_recv.at[j - 1, i], {"grp": rank}
            )
            for i, (src, dst) in enumerate(((zlat, lat_all), (zrope, rope_all)))
        ]

    def plane(j):
        return (g + NG - OFFS[j]) % NG

    def block_at(dx, core):
        return ((x + dx) % 4) * 2 + core

    def ring_copies(j, dx, to, send, recv):
        gs = plane(j)
        at = block_at(dx, c)
        res = []
        for i, (mine, ref) in enumerate(((zlat, lat_all), (zrope, rope_all))):
            src = mine.at[0] if (j == 0 and dx == 0) else ref.at[at, gs]
            res.append(remote(src, ref.at[at, gs], send.at[i], recv.at[i], {"head": to}))
        return res

    def to_right(j):
        return ring_copies(j, 0, right, x_send.at[j, 0], x_recv.at[j, 0])

    def to_left(j):
        return ring_copies(j, 0, left, x_send.at[j, 1], x_recv.at[j, 1])

    def onward(j):
        if j in (0, 3):
            return ring_copies(j, 3, right, f_send.at[j], f_recv.at[j])
        return ring_copies(j, 1, left, f_send.at[j], f_recv.at[j])

    def across(j, dx):
        return ring_copies(j, dx, sibling, c_send.at[j, dx], c_recv.at[j, dx])

    def arrived(j, dx, core, sem):
        gs = plane(j)
        at = block_at(dx, core)
        for i, ref in enumerate((lat_all, rope_all)):
            remote(
                ref.at[at, gs], ref.at[at, gs], sem.at[i], sem.at[i], {"head": sibling}
            ).wait_recv()

    def serve_own(j):
        if j > 0:
            arrived(j, 0, c, z_recv.at[j - 1])
        start(to_right(j))
        start(to_left(j))
        start(across(j, 0))

    def serve_near(j):
        arrived(j, 3, c, x_recv.at[j, 0])
        if j in (0, 3):
            start(onward(j))
        start(across(j, 3))
        arrived(j, 1, c, x_recv.at[j, 1])
        if j in (1, 2):
            start(onward(j))
        start(across(j, 1))

    def serve_far(j):
        arrived(j, 2, c, f_recv.at[j])
        start(across(j, 2))

    def from_sibling(j, places):
        for dx in places:
            arrived(j, dx, other, c_recv.at[j, dx])

    for j in (1, 2, 3):
        start(z_copies(j))
    own = [
        pltpu.make_async_copy(zlat.at[0], lat_all.at[b, g], own_sem.at[0]),
        pltpu.make_async_copy(zrope.at[0], rope_all.at[b, g], own_sem.at[1]),
    ]
    start(own)
    serve_own(0)

    new_lat[...] = norm_rows(acc[tokens : tokens + 64, 0:LAT], kv_gain[...].reshape(1, LAT), LAT).astype(BF16)
    new_r = acc[tokens : tokens + 64, LAT : LAT + ROPE]
    new_r = rotate_pairs(jnp.concatenate([new_r, new_r], axis=1), new_cos[...], new_sin[...])
    lane = lax.broadcasted_iota(jnp.int32, new_r.shape, 1)
    new_rope[...] = jnp.where(lane < ROPE, new_r, 0.0).astype(BF16)

    @pl.loop(1, 16)
    def _(o):
        src = (chip + o) % 16
        remote(
            red,
            qlat.at[block_in(src, c * half_width)],
            g_send.at[src],
            g_recv.at[src],
            {"head": src * 2 + c},
        ).wait_recv()

    back_copy().start()
    serve_own(1)
    remote(
        qlat.at[:, half_cols(other)],
        qlat.at[:, half_cols(other)],
        q_sem.at[2],
        q_sem.at[3],
        {"head": sibling},
    ).wait_recv()
    uq_copy.wait()
    uk_copy.wait()
    query_norm = norm_rows(qlat[...], q_gain[...].reshape(1, QL), QL).astype(BF16)
    queries = dot(query_norm, uq_buf[...])
    serve_own(2)
    parts = []
    ropes = []
    for n in range(NH):
        at = n * (NOPE + ROPE)
        parts.append(dot(queries[:, at : at + NOPE].astype(BF16), uk_buf[n]).astype(BF16))
        one = queries[:, at + NOPE : at + NOPE + ROPE]
        one = jnp.concatenate([one, one], axis=1)
        ropes.append(rotate_pairs(one, new_cos[...], new_sin[...]).astype(BF16))
    order = rows_by_request(False)
    qmine[...] = dot(order, jnp.concatenate(parts, axis=0)).astype(BF16)
    rotated = dot(order, jnp.concatenate(ropes, axis=0))
    qr_dup[...] = rotated.astype(BF16)
    first_lanes = lax.broadcasted_iota(jnp.int32, (128, 128), 1) < ROPE
    qrmine[...] = jnp.where(first_lanes, rotated[0:128], rotated[128:256]).astype(BF16)

    def y_copies(o):
        to = ((y + o) % NY) * NB + b
        return [
            remote(src, dst.at[y], y_send.at[o - 1, i], y_recv.at[o - 1, i], {"head": to})
            for i, (src, dst) in enumerate(((qmine, q_lat), (qrmine, q_rope)))
        ]

    for o in (2, 1, 3):
        start(y_copies(o))
    q_lat[y] = qmine[...]
    q_rope[y] = qrmine[...]

    serve_near(0)
    serve_own(3)
    serve_near(1)

    s = (dot_t(qmine[...], new_lat[...]) + dot_t(qr_dup[...], new_rope[...])) * scale
    i = lax.broadcasted_iota(jnp.int32, s.shape, 0)
    j = lax.broadcasted_iota(jnp.int32, s.shape, 1)
    live = ((i >> 3) == (j >> 1)) & ((j & 1) <= (i & 1))
    s = jnp.where(live, s, LOW)
    top = jnp.max(s, axis=1, keepdims=True)
    p = jnp.where(live, jnp.exp(s - top), 0.0)
    total = jnp.sum(p, axis=1, keepdims=True)
    new_o[...] = dot(p.astype(BF16), new_lat[...]) / total
    new_lse[...] = jnp.broadcast_to(top + jnp.log(total), new_lse.shape)

    serve_far(0)
    serve_near(2)

    for o in (1, 3, 2):
        src = (y + NY - o) % NY
        for n, ref in enumerate((q_lat, q_rope)):
            remote(
                ref.at[src],
                ref.at[src],
                y_send.at[o - 1, n],
                y_recv.at[o - 1, n],
                {"head": src * NB + b},
            ).wait_recv()
    serve_near(3)
    for yb in range(NY):
        qf[:, yb * 8 : (yb + 1) * 8, 0:LAT] = q_lat[yb].astype(F32).reshape(requests, 8, LAT)
        both = q_rope[yb].astype(F32)
        turned = pltpu.roll(both, 64, 1)
        rows = slice(yb * 8, (yb + 1) * 8)
        qf[0:16, rows, LAT:] = jnp.where(first_lanes, both, turned).reshape(16, 8, 128)
        qf[16:32, rows, LAT:] = jnp.where(first_lanes, turned, both).reshape(16, 8, 128)
    qb[0:requests] = qf[...].astype(BF16)
    qb[requests] = jnp.zeros((32, LAT + 128), BF16)

    row = lax.broadcasted_iota(jnp.int32, (SLOT * 32, ROWS), 0)
    col = lax.broadcasted_iota(jnp.int32, (SLOT * 32, ROWS), 1)
    own_page = (row >> 5) == (col >> 6)
    low_lane = lax.broadcasted_iota(jnp.int32, (32, 128), 1) < ROPE

    def attend(at, gs):
        first = (at * NG + gs) * SLOT
        keys = lat_all[at, gs]
        pairs = rope_all[at, gs]
        zero = jnp.zeros((32, 128), BF16)
        ropes = []
        for k in range(SLOT):
            pair = pairs[k * 32 : (k + 1) * 32, :]
            ropes += [jnp.where(low_lane, pair, zero), jnp.where(low_lane, zero, pair)]
        q = jnp.concatenate([qb[owner[first + k]] for k in range(SLOT)], axis=0)
        s = dot_t(q[:, 0:LAT], keys) + dot_t(q[:, LAT:], jnp.concatenate(ropes, axis=0))
        s = jnp.where(own_page, s * scale, LOW)
        top = jnp.max(s, axis=1, keepdims=True)
        p = jnp.where(own_page, jnp.exp(s - top), 0.0)
        total = jnp.sum(p, axis=1, keepdims=True)
        o = dot(p.astype(BF16), keys)
        top = jnp.broadcast_to(top, (SLOT * 32, 128))
        total = jnp.broadcast_to(total, (SLOT * 32, 128))
        o_slot[pl.ds(first, SLOT)] = o.astype(BF16).reshape(SLOT, 32, LAT)
        m_slot[pl.ds(first, SLOT)] = top.reshape(SLOT, 32, 128)
        l_slot[pl.ds(first, SLOT)] = total.reshape(SLOT, 32, 128)

    def gray(j):
        return j ^ (j >> 1)

    def attend_own(n, core, dx, j0):
        @pl.loop(0, n // 2)
        def _(i):
            for u in range(2):
                attend(block_at(dx, core), (g + NG - gray(j0 + 2 * i + u)) % NG)

    def attend_places(j, core, places):
        for dx in places:
            attend(block_at(dx, core), plane(j))

    for one in own:
        one.wait()
    o_slot[96] = jnp.zeros((32, LAT), BF16)
    m_slot[96] = jnp.full((32, 128), LOW, F32)
    l_slot[96] = jnp.zeros((32, 128), F32)
    attend_own(4, c, 0, 0)
    for j in range(4):
        from_sibling(j, (0,))
    attend_own(4, other, 0, 0)
    attend_places(0, c, (1, 3))
    serve_far(1)
    attend_places(1, c, (1, 3))
    from_sibling(0, (1, 3))
    attend_places(0, other, (1, 3))
    serve_far(2)
    from_sibling(1, (1, 3))
    attend_places(1, other, (1, 3))
    attend_places(2, c, (1, 3))
    serve_far(3)
    attend_places(3, c, (1, 3))
    for j in (2, 3):
        from_sibling(j, (1, 3))
        attend_places(j, other, (1, 3))
    attend_own(4, c, 2, 0)
    for j in range(4):
        from_sibling(j, (2,))
    attend_own(4, other, 2, 0)

    def o_copy(o, n):
        ty = (y + o) % NY
        rows = pl.ds(n * 64, 64)
        return remote(
            part.at[ty, rows],
            o_land.at[o - 1, rows],
            o_send.at[o - 1, n],
            o_recv.at[o - 1, n],
            {"head": ty * NB + b},
        )

    def s_copy(o):
        ty = (y + o) % NY
        return remote(
            stats.at[ty], s_land.at[o - 1], s_send.at[o - 1], s_recv.at[o - 1], {"head": ty * NB + b}
        )

    def merge_pair(pair):
        mixes = []
        for u in range(2):
            r = pair * 2 + u
            at = [listed[r * MAXP + k] for k in range(MAXP)]
            tops = [m_slot[one] for one in at]
            top = tops[0]
            for one in tops[1:]:
                top = jnp.maximum(top, one)
            total = jnp.zeros((32, 128), F32)
            mixed = jnp.zeros((32, LAT), F32)
            for one, its_top in zip(at, tops):
                e = jnp.exp(its_top - top)
                total += l_slot[one] * e
                mixed += o_slot[one].astype(F32) * e[:, 0:1]
            some = total > 0.0
            safe = jnp.where(some, total, 1.0)
            lse = jnp.where(some, top + jnp.log(safe), LOW)
            mixed = mixed * (1.0 / safe)[:, 0:1]
            mixes.append(mixed)
            for yb in range(NY):
                lse_rows[yb, pl.ds(pl.multiple_of(r * 8, 8), 8), :] = lse[yb * 8 : (yb + 1) * 8]
        for yb in range(NY):
            rows = slice(yb * 8, (yb + 1) * 8)
            both = jnp.concatenate([mixes[0][rows], mixes[1][rows]], axis=0)
            part[yb, pl.ds(pl.multiple_of(pair * 16, 16), 16), :] = both.astype(BF16)

    for n in range(4):

        @pl.loop(0, 4)
        def _(i):
            merge_pair(n * 4 + i)

        if n == 3:
            for yb in range(NY):
                stats[yb] = jnp.transpose(lse_rows[yb])[0:8, :]
            for o in (2, 1, 3):
                s_copy(o).start()
        for o in (2, 1, 3):
            o_copy(o, n).start()

    def column(block):
        t_buf[0:8, :] = block
        return jnp.transpose(t_buf[...])[:, 0:1]

    t_buf[...] = jnp.zeros_like(t_buf)
    lses = [new_lse[:, 0:1], column(stats[y])]
    mixes = [new_o[...], part[y].astype(F32)]
    for o in (1, 3, 2):
        s_copy(o).wait_recv()
        for n in range(4):
            o_copy(o, n).wait_recv()
        lses.append(column(s_land[o - 1]))
        mixes.append(o_land[o - 1].astype(F32))
    top = lses[0]
    for one in lses[1:]:
        top = jnp.maximum(top, one)
    weights = [jnp.exp(one - top) for one in lses]
    total = weights[0]
    for one in weights[1:]:
        total = total + one
    mixed = mixes[0] * (weights[0] / total)
    for one, weight in zip(mixes[1:], weights[1:]):
        mixed += one * (weight / total)
    by_head = dot(rows_by_request(True), mixed.astype(BF16)).astype(BF16)
    uv_copy.wait()
    for n in range(NH):
        vals[:, n * 128 : (n + 1) * 128] = dot(
            by_head[n * 64 : (n + 1) * 64, :], uv_buf[n]
        ).astype(BF16)

    wo_copy.wait()
    width = out.shape[2]
    span = width * NB
    def pair_copy(ty):
        chips = pl.ds(ty * 4, 4)
        return remote(
            sbuf.at[other, chips], sib_land.at[chips], p_send.at[ty], p_recv.at[ty], {"head": sibling}
        )

    for n in (1, 2, 3, 0):
        ty = (y + n) % NY
        cols = pl.ds(pl.multiple_of(ty * span, 128), span)
        piece = dot(vals[...], wbuf[0 : w_o.shape[0], cols])
        for k in range(NB):
            sbuf[k % 2, ty * 4 + k // 2] = piece[:, k * width : (k + 1) * width].astype(BF16)
        pair_copy(ty).start()

    def out_copy(t):
        return remote(
            tbuf.at[t], rbuf.at[chip], d_send.at[t], d_recv.at[chip], {"head": t * 2 + c}
        )

    for n in (1, 2, 3, 0):
        ty = (y + n) % NY
        pair_copy(ty).wait_recv()
        for k in range(4):
            t = ty * 4 + k
            tbuf[t] = (sbuf[c, t].astype(F32) + sib_land[t].astype(F32)).astype(BF16)

            @pl.when(t != chip)
            def _():
                out_copy(t).start()

    def body(o, total):
        src = (chip + o) % 16
        remote(
            rbuf.at[src], rbuf.at[src], d_send.at[src], d_recv.at[src], {"head": src * 2 + c}
        ).wait_recv()
        return total + rbuf[src].astype(F32)

    result = lax.fori_loop(1, 16, body, tbuf[chip].astype(F32))
    out[...] = result.reshape(out.shape).astype(BF16)

    for j in (1, 2, 3):
        wait_send(z_copies(j))
    for j in range(4):
        wait_send(to_right(j))
        wait_send(to_left(j))
        wait_send(onward(j))
        for dx in range(4):
            wait_send(across(j, dx))
    for o in (1, 2, 3):
        wait_send(y_copies(o))
        s_copy(o).wait_send()
        for n in range(4):
            o_copy(o, n).wait_send()
    for ty in range(NY):
        pair_copy(ty).wait_send()

    @pl.loop(1, 16)
    def _(o):
        out_copy((chip + o) % 16).wait_send()

    @pl.loop(1, 16)
    def _(o):
        to = (chip + o) % 16
        share_copy(to).wait_send()
        sum_copy(to).wait_send()

    halves_copy().wait_send()
    back_copy().wait_send()


def spec(space):
    return pl.BlockSpec(memory_space=space)


VM, SM, ANY = pltpu.VMEM, pltpu.SMEM, pl.ANY


def page_plan(block_table, ctx_pages, g, y, b, per_rank, pages_dev):
    flat = jnp.where(
        jnp.arange(MAXP, dtype=jnp.int32)[None, :] < ctx_pages[:, None], block_table, -1
    ).reshape(1, -1)
    at = jnp.arange(NG * NB * pages_dev, dtype=jnp.int32)
    per_plane = NB * pages_dev
    ids = (at // per_plane) * (N_HEAD * pages_dev) + y * per_plane + at % per_plane
    codes = jnp.arange(flat.shape[1], dtype=jnp.int32)[None, :]
    code = jnp.sum(jnp.where(flat == ids[:, None], codes, 0), axis=1)
    code = code.reshape(NG, NB, pages_dev)
    target = code // (per_rank * MAXP)
    within = jnp.arange(pages_dev, dtype=jnp.int32)
    alike = (target[..., :, None] == target[..., None, :]) & (within[None, :] < within[:, None])
    slot = jnp.sum(alike.astype(jnp.int32), axis=-1)
    places = jnp.arange(SLOT, dtype=jnp.int32)
    here = (target == g)[..., None, :] & (slot[..., None, :] == places[:, None])
    local = code % (per_rank * MAXP)
    held = jnp.sum(jnp.where(here, local[..., None, :] + 1, 0), axis=-1) - 1
    held = held.transpose(1, 0, 2).reshape(-1)
    owner = jnp.where(held >= 0, held // MAXP, per_rank)
    wanted = jnp.arange(per_rank * MAXP, dtype=jnp.int32)
    total = held.shape[0]
    spare = jnp.arange(total, dtype=jnp.int32) - total
    listed = total + jnp.sum(jnp.where(held[None, :] == wanted[:, None], spare[None, :], 0), axis=1)
    mine = lax.dynamic_slice(code, (g, b, 0), (1, 1, pages_dev)).reshape(-1)
    my_target = lax.dynamic_slice(target, (g, b, 0), (1, 1, pages_dev)).reshape(-1)
    my_slot = lax.dynamic_slice(slot, (g, b, 0), (1, 1, pages_dev)).reshape(-1)
    sends = (my_target[None, :] * SLOT + my_slot[None, :]) == jnp.arange(
        NG * SLOT, dtype=jnp.int32
    )[:, None]
    send_idx = jnp.sum(jnp.where(sends, within[None, :], 0), axis=1)
    return owner, listed, send_idx, mine % MAXP


def angle_tables():
    lane = np.arange(2 * ROPE)
    inverse_freq = 10000.0 ** (-2.0 * (lane % 32) / ROPE)
    steps = np.concatenate([np.arange(17) * PAGE, np.arange(2), np.zeros(5)])
    far = steps[:, None] * inverse_freq[None, :]
    near = (np.arange(32)[:, None] + 32 * (lane // ROPE)[None, :]) * inverse_freq[None, :]
    return [jnp.asarray(t, F32) for t in (np.cos(far), np.sin(far), np.cos(near), np.sin(near))]


def on_device(
    prompt, w_dkv, kv_gain, block_table, ctx_pages, dec_hidden, w_dq, q_gain, w_uq, w_uk, w_uv, w_o
):
    g = lax.axis_index("grp")
    h = lax.axis_index("head")
    y, b = h // NB, h % NB
    tokens, depth = prompt.shape
    pages_dev = tokens // PAGE
    per_rank = dec_hidden.shape[0]
    owner, listed, send_idx, my_depth = page_plan(
        block_table, ctx_pages, g, y, b, per_rank, pages_dev
    )
    dma = pltpu.SemaphoreType.DMA
    width = depth // N_HEAD
    slots = NB * NG * SLOT
    out = pl.pallas_call(
        fused_kernel,
        out_shape=jax.ShapeDtypeStruct((per_rank, 2, width), BF16),
        in_specs=[spec(SM)] * 5 + [spec(VM)] * 6 + [spec(ANY)] * 8,
        out_specs=spec(VM),
        scratch_shapes=[
            pltpu.VMEM((tokens + 64, depth), BF16),
            pltpu.VMEM((per_rank, 2, depth), BF16),
            pltpu.VMEM((LAT + ROPE, depth), BF16),
            pltpu.VMEM((tokens + 64, LAT + ROPE), F32),
            pltpu.VMEM(w_uq.shape, BF16),
            pltpu.VMEM(w_uk.shape, BF16),
            pltpu.VMEM(w_uv.shape, BF16),
            pltpu.VMEM((pages_dev, PAGE, LAT), BF16),
            pltpu.VMEM((pages_dev, 32, 128), BF16),
            pltpu.VMEM((NG, ROWS, LAT), BF16),
            pltpu.VMEM((NG, RROWS, 128), BF16),
            pltpu.VMEM((384, QL), BF16),
            pltpu.VMEM((64, 128), F32),
            pltpu.VMEM((64, 128), F32),
            pltpu.VMEM((64, QL), F32),
            pltpu.VMEM((64, QL // 2), F32),
            pltpu.VMEM((64, QL // 2), F32),
            pltpu.VMEM((16, 8, 384), F32),
            pltpu.VMEM((8, 384), F32),
            pltpu.VMEM((64, QL), F32),
            pltpu.VMEM((256, LAT), BF16),
            pltpu.VMEM((256, 128), BF16),
            pltpu.VMEM((128, 128), BF16),
            pltpu.VMEM((64, LAT), BF16),
            pltpu.VMEM((64, 128), BF16),
            pltpu.VMEM((256, LAT), F32),
            pltpu.VMEM((256, 128), F32),
            pltpu.VMEM((NB, NG, ROWS, LAT), BF16),
            pltpu.VMEM((NB, NG, RROWS, 128), BF16),
            pltpu.VMEM((NY, 256, LAT), BF16),
            pltpu.VMEM((NY, 128, 128), BF16),
            pltpu.VMEM((32, 32, LAT + 128), F32),
            pltpu.VMEM((33, 32, LAT + 128), BF16),
            pltpu.VMEM((slots + 1, 32, LAT), BF16),
            pltpu.VMEM((slots + 1, 32, 128), F32),
            pltpu.VMEM((slots + 1, 32, 128), F32),
            pltpu.VMEM((NY, 256, LAT), BF16),
            pltpu.VMEM((NY, 256, 128), F32),
            pltpu.VMEM((NY, 8, 256), F32),
            pltpu.VMEM((3, 256, LAT), BF16),
            pltpu.VMEM((3, 8, 256), F32),
            pltpu.VMEM((128, 256), F32),
            pltpu.VMEM((64, LAT), BF16),
            pltpu.VMEM((2, 16, 64, width), BF16),
            pltpu.VMEM((16, 64, width), BF16),
            pltpu.VMEM((16, 64, width), BF16),
            pltpu.VMEM((16, 64, width), BF16),
            dma((depth // KCHUNK, 2)),
            dma((6,)),
            dma((2,)),
            dma((3, 2)),
            dma((3, 2)),
            dma((4, 2, 2)),
            dma((4, 2, 2)),
            dma((4, 2)),
            dma((4, 2)),
            dma((4, 4, 2)),
            dma((4, 4, 2)),
            dma((4,)),
            dma((16,)),
            dma((16,)),
            dma((16,)),
            dma((16,)),
            dma((3, 2)),
            dma((3, 2)),
            dma((3, 4)),
            dma((3, 4)),
            dma((3,)),
            dma((3,)),
            dma((4,)),
            dma((4,)),
            dma((16,)),
            dma((16,)),
        ],
        compiler_params=pltpu.CompilerParams(
            collective_id=0, has_side_effects=True, vmem_limit_bytes=58 * 1024 * 1024
        ),
    )(
        send_idx,
        owner,
        listed,
        my_depth,
        ctx_pages,
        kv_gain,
        q_gain,
        *angle_tables(),
        prompt,
        dec_hidden,
        w_dq,
        w_dkv.T,
        w_uq,
        w_uk,
        w_uv,
        w_o,
    )
    return out


def solution(mesh):
    return jax.shard_map(
        on_device,
        mesh=mesh,
        in_specs=(
            P(("grp", "head"), None),
            P(),
            P(),
            P(),
            P(),
            P("grp", None, None),
            P("head", None),
            P(),
            P(None, "head"),
            P("head", None, None),
            P("head", None, None),
            P("head", None),
        ),
        out_specs=P("grp", None, "head"),
        check_vma=False,
    )
```

```python
import jax
import jax.numpy as jnp
import numpy as np
from jax import lax
from jax.experimental import pallas as pl
from jax.experimental.pallas import tpu as pltpu
from jax.sharding import PartitionSpec as P

PAGE = 64
SLOT = 3
MAXP = 16
LAT = 512
ROPE = 64
NOPE = 128
QL = 1536
NH = 4
NG = 4
NY = 4
NB = 8
N_HEAD = 32
ROWS = SLOT * PAGE
RROWS = SLOT * PAGE // 2
FOUR = 4
KCHUNK = 1024
AHEAD = 3
OFFS = (0, 1, 3, 2)
MESH = pl.DeviceIdType.MESH
F32 = jnp.float32
BF16 = jnp.bfloat16
LOW = -1e30


def dot(a, b):
    return jnp.dot(a, b, preferred_element_type=F32)


def dot_t(a, b):
    return lax.dot_general(a, b, (((1,), (1,)), ((), ())), preferred_element_type=F32)


def norm_rows(values, gain_row, width):
    mean = jnp.sum(values * values, axis=-1, keepdims=True) * (1.0 / width)
    return values * lax.rsqrt(mean + 1e-06) * gain_row


def rotate_pairs(x, cosine, signed_sine):
    lane = lax.broadcasted_iota(jnp.int32, x.shape, 1)
    swapped = jnp.where((lane & 63) < 32, pltpu.roll(x, 96, 1), pltpu.roll(x, 32, 1))
    return x * cosine + swapped * signed_sine


def rows_by_request(transposed):
    i = lax.broadcasted_iota(jnp.int32, (256, 256), 1 if transposed else 0)
    j = lax.broadcasted_iota(jnp.int32, (256, 256), 0 if transposed else 1)
    place = ((i >> 1) & 3) * 64 + (i >> 3) * 2 + (i & 1)
    return jnp.where(j == place, 1.0, 0.0).astype(BF16)


def fused_kernel(
    send_idx,
    owner,
    listed,
    depths,
    lengths,
    kv_gain,
    q_gain,
    cos_far,
    sin_far,
    cos_near,
    sin_near,
    prompt,
    hidden,
    w_dq,
    w_dkv,
    w_uq,
    w_uk,
    w_uv,
    w_o,
    out,
    pbuf,
    hbuf,
    wbuf,
    acc,
    uq_buf,
    uk_buf,
    uv_buf,
    lat_own,
    rope_own,
    zlat,
    zrope,
    wdq_buf,
    new_cos,
    new_sin,
    qpart,
    pair_land,
    half,
    rq_land,
    red,
    qlat,
    qmine,
    qr_dup,
    qrmine,
    new_lat,
    new_rope,
    new_o,
    new_lse,
    lat_all,
    rope_all,
    q_lat,
    q_rope,
    qf,
    qb,
    o_slot,
    m_slot,
    l_slot,
    part,
    lse_rows,
    stats,
    o_land,
    s_land,
    t_buf,
    vals,
    sbuf,
    sib_land,
    tbuf,
    rbuf,
    load_sem,
    w_sem,
    own_sem,
    z_send,
    z_recv,
    x_send,
    x_recv,
    f_send,
    f_recv,
    c_send,
    c_recv,
    q_sem,
    r_send,
    r_recv,
    g_send,
    g_recv,
    y_send,
    y_recv,
    o_send,
    o_recv,
    s_send,
    s_recv,
    p_send,
    p_recv,
    d_send,
    d_recv,
):
    g = lax.axis_index("grp")
    h = lax.axis_index("head")
    y = h // NB
    b = h % NB
    x = b // 2
    c = b % 2
    other = 1 - c
    sibling = y * NB + x * 2 + other
    right = y * NB + ((x + 1) % 4) * 2 + c
    left = y * NB + ((x + 3) % 4) * 2 + c
    scale = (NOPE + ROPE) ** (-0.5)

    def start(copies):
        for one in copies:
            one.start()

    def wait_recv(copies):
        for one in copies:
            one.wait_recv()

    def wait_send(copies):
        for one in copies:
            one.wait_send()

    def remote(src, dst, send, recv, to):
        return pltpu.make_async_remote_copy(
            src_ref=src,
            dst_ref=dst,
            send_sem=send,
            recv_sem=recv,
            device_id=to,
            device_id_type=MESH,
        )

    barrier = pltpu.get_barrier_semaphore()

    @pl.loop(1, N_HEAD)
    def _(o):
        pl.semaphore_signal(
            barrier, inc=1, device_id={"head": (h + o) % N_HEAD}, device_id_type=MESH
        )

    for o in (1, 2, 3):
        pl.semaphore_signal(barrier, inc=1, device_id={"grp": (g + o) % NG}, device_id_type=MESH)

    depth = prompt.shape[1]
    tokens = prompt.shape[0]
    chunks = depth // KCHUNK
    loads = []
    for k in range(chunks):
        cols = pl.ds(k * KCHUNK, KCHUNK)
        loads.append(
            [
                pltpu.make_async_copy(
                    prompt.at[:, cols], pbuf.at[pl.ds(0, tokens), cols], load_sem.at[k, 0]
                ),
                pltpu.make_async_copy(w_dkv.at[:, cols], wbuf.at[:, cols], load_sem.at[k, 1]),
            ]
        )
    share = w_dq.shape[0]
    window = 384
    first_col = jnp.minimum((h * share) // 128 * 128, depth - window)
    at_row = pl.multiple_of(h * share - first_col, 32)
    hidden_copy = pltpu.make_async_copy(hidden, hbuf, w_sem.at[4])
    hidden_copy.start()
    wdq_buf[...] = jnp.zeros_like(wdq_buf)
    dq_copy = pltpu.make_async_copy(w_dq, wdq_buf.at[pl.ds(at_row, share), :], w_sem.at[5])
    dq_copy.start()
    for group in loads[:AHEAD]:
        start(group)
    uq_copy = pltpu.make_async_copy(w_uq, uq_buf, w_sem.at[0])
    uk_copy = pltpu.make_async_copy(w_uk, uk_buf, w_sem.at[1])
    uv_copy = pltpu.make_async_copy(w_uv, uv_buf, w_sem.at[2])
    wo_copy = pltpu.make_async_copy(w_o, wbuf.at[pl.ds(0, w_o.shape[0])], w_sem.at[3])

    requests = hidden.shape[0]
    for r in range(requests):
        far = lengths[g * requests + r]
        new_cos[2 * r : 2 * r + 2, :] = jnp.broadcast_to(cos_far[pl.ds(far, 1), :], (2, 128))
        new_sin[2 * r : 2 * r + 2, :] = jnp.broadcast_to(sin_far[pl.ds(far, 1), :], (2, 128))
    odd = (lax.broadcasted_iota(jnp.int32, (64, 128), 0) & 1) == 1
    step_cos = jnp.where(odd, cos_far[18:19, :], cos_far[17:18, :])
    step_sin = jnp.where(odd, sin_far[18:19, :], sin_far[17:18, :])
    far_cos, far_sin = new_cos[...], new_sin[...]
    sign = jnp.where(
        (lax.broadcasted_iota(jnp.int32, (1, 128), 1) & 63) < 32, -1.0, 1.0
    ).astype(F32)
    new_cos[...] = far_cos * step_cos - far_sin * step_sin
    new_sin[...] = (far_sin * step_cos + far_cos * step_sin) * sign

    hidden_copy.wait()
    dq_copy.wait()
    part_of_hidden = hbuf[:, :, pl.ds(pl.multiple_of(first_col, 128), window)].reshape(64, window)
    qpart[...] = dot(part_of_hidden, wdq_buf[...])

    chip = y * 4 + x
    half_width = QL // 2

    def half_cols(core):
        return pl.ds(pl.multiple_of(core * half_width, 128), half_width)

    def block_in(t, first):
        return (
            pl.ds(pl.multiple_of((t // 2) * 8, 8), 8),
            pl.ds(pl.multiple_of(first + (t % 2) * 384, 128), 384),
        )

    def halves_copy():
        return remote(
            qpart.at[:, half_cols(other)], pair_land, q_sem.at[0], q_sem.at[1], {"head": sibling}
        )

    def share_copy(t):
        return remote(
            half.at[block_in(t, 0)], rq_land.at[chip], r_send.at[t], r_recv.at[chip], {"head": t * 2 + c}
        )

    def sum_copy(t):
        return remote(
            red,
            qlat.at[block_in(chip, c * half_width)],
            g_send.at[t],
            g_recv.at[chip],
            {"head": t * 2 + c},
        )

    def back_copy():
        return remote(
            qlat.at[:, half_cols(c)],
            qlat.at[:, half_cols(c)],
            q_sem.at[2],
            q_sem.at[3],
            {"head": sibling},
        )

    def share_sums():
        halves_copy().wait_recv()
        half[...] = qpart[:, half_cols(c)] + pair_land[...]
        rq_land[chip] = half[block_in(chip, 0)]

        @pl.loop(1, 16)
        def _(o):
            share_copy((chip + o) % 16).start()

    def send_sums():
        @pl.loop(1, 16)
        def _(o):
            src = (chip + o) % 16
            remote(
                rq_land.at[src], rq_land.at[src], r_send.at[src], r_recv.at[src], {"head": src * 2 + c}
            ).wait_recv()

        red[...] = jnp.sum(rq_land[...], axis=0)
        qlat[block_in(chip, c * half_width)] = red[...]

        @pl.loop(1, 16)
        def _(o):
            sum_copy((chip + o) % 16).start()

    for k in range(chunks):
        if k == 2:
            pl.semaphore_wait(barrier, N_HEAD - 1 + 3)
            halves_copy().start()
        if k == 3:
            share_sums()
        for one in loads[k]:
            one.wait()
        if k + AHEAD < chunks:
            start(loads[k + AHEAD])
        elif k + AHEAD == chunks:
            start([uq_copy, uk_copy, uv_copy])
        cols = slice(k * KCHUNK, (k + 1) * KCHUNK)
        pbuf[tokens:, cols] = hbuf[:, :, cols].reshape(64, KCHUNK)
        piece = dot_t(pbuf[:, cols], wbuf[:, cols])
        if k == 0:
            acc[...] = piece
        else:
            acc[...] += piece
    send_sums()
    wo_copy.start()

    pages = tokens // PAGE
    lat_own[...] = (
        norm_rows(acc[0:tokens, 0:LAT], kv_gain[...].reshape(1, LAT), LAT).astype(BF16).reshape(pages, PAGE, LAT)
    )
    halves = []
    for p in range(pages):
        first = acc[p * PAGE : p * PAGE + 32, LAT : LAT + ROPE]
        second = acc[p * PAGE + 32 : p * PAGE + 64, LAT : LAT + ROPE]
        halves.append(jnp.concatenate([first, second], axis=1))
    packed = jnp.concatenate(halves, axis=0)
    page_cos = []
    page_sin = []
    for p in range(pages):
        far = pl.ds(depths[p], 1)
        far_cos, far_sin = cos_far[far, :], sin_far[far, :]
        page_cos.append(far_cos * cos_near[...] - far_sin * sin_near[...])
        page_sin.append((far_sin * cos_near[...] + far_cos * sin_near[...]) * sign)
    page_cos = jnp.concatenate(page_cos, axis=0)
    page_sin = jnp.concatenate(page_sin, axis=0)
    rope_own[...] = (
        rotate_pairs(packed, page_cos, page_sin).astype(BF16).reshape(pages, 32, 128)
    )

    for j in range(4):
        rank = (g + OFFS[j]) % NG
        for k in range(SLOT):
            page = send_idx[rank * SLOT + k]
            zlat[j, k * PAGE : (k + 1) * PAGE, :] = lat_own[page]
            zrope[j, k * 32 : (k + 1) * 32, :] = rope_own[page]

    def place(ref, at, j):
        rows = ref.shape[1] // NG
        return ref.at[at, pl.ds(j * rows, rows)]

    def half_place(ref, at, j, side):
        rows = ref.shape[1] // NG // 2
        return ref.at[at, pl.ds((j * 2 + side) * rows, rows)]

    def z_copies(j):
        rank = (g + OFFS[j]) % NG
        return [
            remote(
                src.at[j], place(dst, b, j), z_send.at[j - 1, i], z_recv.at[j - 1, i], {"grp": rank}
            )
            for i, (src, dst) in enumerate(((zlat, lat_all), (zrope, rope_all)))
        ]

    def block_at(dx, core):
        return ((x + dx) % 4) * 2 + core

    def ring_copies(j, dx, to, send, recv):
        at = block_at(dx, c)
        res = []
        for i, (mine, ref) in enumerate(((zlat, lat_all), (zrope, rope_all))):
            src = mine.at[0] if (j == 0 and dx == 0) else place(ref, at, j)
            res.append(remote(src, place(ref, at, j), send.at[i], recv.at[i], {"head": to}))
        return res

    def to_right(j):
        return ring_copies(j, 0, right, x_send.at[j, 0], x_recv.at[j, 0])

    def to_left(j):
        return ring_copies(j, 0, left, x_send.at[j, 1], x_recv.at[j, 1])

    def onward(j, side):
        at = block_at(1 if side else 3, c)
        return [
            remote(
                half_place(ref, at, j, side),
                half_place(ref, at, j, side),
                f_send.at[j, side, i],
                f_recv.at[j, side, i],
                {"head": left if side else right},
            )
            for i, ref in enumerate((lat_all, rope_all))
        ]

    def across(j, dx):
        return ring_copies(j, dx, sibling, c_send.at[j, dx], c_recv.at[j, dx])

    def arrived(j, dx, core, sem):
        at = block_at(dx, core)
        for i, ref in enumerate((lat_all, rope_all)):
            remote(
                place(ref, at, j), place(ref, at, j), sem.at[i], sem.at[i], {"head": sibling}
            ).wait_recv()

    def serve_own(j):
        if j > 0:
            arrived(j, 0, c, z_recv.at[j - 1])
        start(to_right(j))
        start(to_left(j))
        start(across(j, 0))

    def serve_near(j):
        arrived(j, 3, c, x_recv.at[j, 0])
        start(onward(j, 0))
        start(across(j, 3))
        arrived(j, 1, c, x_recv.at[j, 1])
        start(onward(j, 1))
        start(across(j, 1))

    def serve_far(j):
        at = block_at(2, c)
        for side in range(2):
            for i, ref in enumerate((lat_all, rope_all)):
                there = half_place(ref, at, j, side)
                sem = f_recv.at[j, side, i]
                remote(there, there, sem, sem, {"head": sibling}).wait_recv()
        start(across(j, 2))

    def from_sibling(j, places):
        for dx in places:
            arrived(j, dx, other, c_recv.at[j, dx])

    for j in (1, 2, 3):
        start(z_copies(j))
    own = [
        pltpu.make_async_copy(zlat.at[0], place(lat_all, b, 0), own_sem.at[0]),
        pltpu.make_async_copy(zrope.at[0], place(rope_all, b, 0), own_sem.at[1]),
    ]
    start(own)
    serve_own(0)

    new_lat[...] = norm_rows(acc[tokens : tokens + 64, 0:LAT], kv_gain[...].reshape(1, LAT), LAT).astype(BF16)
    new_r = acc[tokens : tokens + 64, LAT : LAT + ROPE]
    new_r = rotate_pairs(jnp.concatenate([new_r, new_r], axis=1), new_cos[...], new_sin[...])
    lane = lax.broadcasted_iota(jnp.int32, new_r.shape, 1)
    new_rope[...] = jnp.where(lane < ROPE, new_r, 0.0).astype(BF16)

    @pl.loop(1, 16)
    def _(o):
        src = (chip + o) % 16
        remote(
            red,
            qlat.at[block_in(src, c * half_width)],
            g_send.at[src],
            g_recv.at[src],
            {"head": src * 2 + c},
        ).wait_recv()

    back_copy().start()
    serve_own(1)
    remote(
        qlat.at[:, half_cols(other)],
        qlat.at[:, half_cols(other)],
        q_sem.at[2],
        q_sem.at[3],
        {"head": sibling},
    ).wait_recv()
    uq_copy.wait()
    uk_copy.wait()
    query_norm = norm_rows(qlat[...], q_gain[...].reshape(1, QL), QL).astype(BF16)
    queries = dot(query_norm, uq_buf[...])
    serve_own(2)
    parts = []
    ropes = []
    for n in range(NH):
        at = n * (NOPE + ROPE)
        parts.append(dot(queries[:, at : at + NOPE].astype(BF16), uk_buf[n]).astype(BF16))
        one = queries[:, at + NOPE : at + NOPE + ROPE]
        one = jnp.concatenate([one, one], axis=1)
        ropes.append(rotate_pairs(one, new_cos[...], new_sin[...]).astype(BF16))
    order = rows_by_request(False)
    qmine[...] = dot(order, jnp.concatenate(parts, axis=0)).astype(BF16)
    rotated = dot(order, jnp.concatenate(ropes, axis=0))
    qr_dup[...] = rotated.astype(BF16)
    first_lanes = lax.broadcasted_iota(jnp.int32, (128, 128), 1) < ROPE
    qrmine[...] = jnp.where(first_lanes, rotated[0:128], rotated[128:256]).astype(BF16)

    def y_copies(o):
        to = ((y + o) % NY) * NB + b
        return [
            remote(src, dst.at[y], y_send.at[o - 1, i], y_recv.at[o - 1, i], {"head": to})
            for i, (src, dst) in enumerate(((qmine, q_lat), (qrmine, q_rope)))
        ]

    for o in (2, 1, 3):
        start(y_copies(o))
    q_lat[y] = qmine[...]
    q_rope[y] = qrmine[...]

    serve_near(0)
    serve_own(3)
    serve_near(1)

    s = (dot_t(qmine[...], new_lat[...]) + dot_t(qr_dup[...], new_rope[...])) * scale
    i = lax.broadcasted_iota(jnp.int32, s.shape, 0)
    j = lax.broadcasted_iota(jnp.int32, s.shape, 1)
    live = ((i >> 3) == (j >> 1)) & ((j & 1) <= (i & 1))
    s = jnp.where(live, s, LOW)
    top = jnp.max(s, axis=1, keepdims=True)
    p = jnp.where(live, jnp.exp(s - top), 0.0)
    total = jnp.sum(p, axis=1, keepdims=True)
    new_o[...] = dot(p.astype(BF16), new_lat[...]) / total
    new_lse[...] = jnp.broadcast_to(top + jnp.log(total), new_lse.shape)

    serve_far(0)
    serve_near(2)

    for o in (1, 3, 2):
        src = (y + NY - o) % NY
        for n, ref in enumerate((q_lat, q_rope)):
            remote(
                ref.at[src],
                ref.at[src],
                y_send.at[o - 1, n],
                y_recv.at[o - 1, n],
                {"head": src * NB + b},
            ).wait_recv()
    for yb in range(NY):
        qf[:, yb * 8 : (yb + 1) * 8, 0:LAT] = q_lat[yb].astype(F32).reshape(requests, 8, LAT)
        both = q_rope[yb].astype(F32)
        turned = pltpu.roll(both, 64, 1)
        rows = slice(yb * 8, (yb + 1) * 8)
        qf[0:16, rows, LAT:] = jnp.where(first_lanes, both, turned).reshape(16, 8, 128)
        qf[16:32, rows, LAT:] = jnp.where(first_lanes, turned, both).reshape(16, 8, 128)
    qb[0:requests] = qf[...].astype(BF16)
    qb[requests] = jnp.zeros((32, LAT + 128), BF16)

    row = lax.broadcasted_iota(jnp.int32, (FOUR * 32, FOUR * PAGE), 0)
    col = lax.broadcasted_iota(jnp.int32, (FOUR * 32, FOUR * PAGE), 1)
    own_page = (row >> 5) == (col >> 6)
    low_lane = lax.broadcasted_iota(jnp.int32, (32, 128), 1) < ROPE

    def attend(at, t):
        first = at * NG * SLOT + t * FOUR
        keys = lat_all[at, pl.ds(pl.multiple_of(t * FOUR * PAGE, 256), FOUR * PAGE), :]
        pairs = rope_all[at, pl.ds(pl.multiple_of(t * FOUR * 32, 128), FOUR * 32), :]
        zero = jnp.zeros((32, 128), BF16)
        ropes = []
        for k in range(FOUR):
            pair = pairs[k * 32 : (k + 1) * 32, :]
            ropes += [jnp.where(low_lane, pair, zero), jnp.where(low_lane, zero, pair)]
        q = jnp.concatenate([qb[owner[first + k]] for k in range(FOUR)], axis=0)
        s = dot_t(q[:, 0:LAT], keys) + dot_t(q[:, LAT:], jnp.concatenate(ropes, axis=0))
        s = jnp.where(own_page, s * scale, LOW)
        top = jnp.max(s, axis=1, keepdims=True)
        p = jnp.where(own_page, jnp.exp(s - top), 0.0)
        total = jnp.sum(p, axis=1, keepdims=True)
        o = dot(p.astype(BF16), keys)
        top = jnp.broadcast_to(top, (FOUR * 32, 128))
        total = jnp.broadcast_to(total, (FOUR * 32, 128))
        o_slot[pl.ds(first, FOUR)] = o.astype(BF16).reshape(FOUR, 32, LAT)
        m_slot[pl.ds(first, FOUR)] = top.reshape(FOUR, 32, 128)
        l_slot[pl.ds(first, FOUR)] = total.reshape(FOUR, 32, 128)

    def attend_blocks(core, places, first, last):
        if last - first == 1:
            for dx in places:
                attend(block_at(dx, core), first)
            return

        @pl.loop(first, last)
        def _(t):
            for dx in places:
                attend(block_at(dx, core), t)

    for one in own:
        one.wait()
    o_slot[96] = jnp.zeros((32, LAT), BF16)
    m_slot[96] = jnp.full((32, 128), LOW, F32)
    l_slot[96] = jnp.zeros((32, 128), F32)
    for j in range(4):
        from_sibling(j, (0,))

    @pl.loop(0, NG * SLOT // FOUR)
    def _(t):
        attend(block_at(0, c), t)
        attend(block_at(0, other), t)

    serve_near(3)
    attend_blocks(c, (1, 3), 0, 2)
    serve_far(1)
    for j in range(3):
        from_sibling(j, (1, 3))
    attend_blocks(other, (1, 3), 0, 2)
    serve_far(2)
    attend_blocks(c, (1, 3), 2, 3)
    attend_blocks(c, (2,), 0, 2)
    from_sibling(3, (1, 3))
    serve_far(3)
    attend_blocks(other, (1, 3), 2, 3)
    for j in range(3):
        from_sibling(j, (2,))
    attend_blocks(other, (2,), 0, 2)
    attend_blocks(c, (2,), 2, 3)
    from_sibling(3, (2,))
    attend_blocks(other, (2,), 2, 3)

    def o_copy(o, n):
        ty = (y + o) % NY
        rows = pl.ds(n * 64, 64)
        return remote(
            part.at[ty, rows],
            o_land.at[o - 1, rows],
            o_send.at[o - 1, n],
            o_recv.at[o - 1, n],
            {"head": ty * NB + b},
        )

    def s_copy(o):
        ty = (y + o) % NY
        return remote(
            stats.at[ty], s_land.at[o - 1], s_send.at[o - 1], s_recv.at[o - 1], {"head": ty * NB + b}
        )

    def merge_pair(pair):
        mixes = []
        for u in range(2):
            r = pair * 2 + u
            at = [listed[r * MAXP + k] for k in range(MAXP)]
            tops = [m_slot[one] for one in at]
            top = tops[0]
            for one in tops[1:]:
                top = jnp.maximum(top, one)
            total = jnp.zeros((32, 128), F32)
            mixed = jnp.zeros((32, LAT), F32)
            for one, its_top in zip(at, tops):
                e = jnp.exp(its_top - top)
                total += l_slot[one] * e
                mixed += o_slot[one].astype(F32) * e[:, 0:1]
            some = total > 0.0
            safe = jnp.where(some, total, 1.0)
            lse = jnp.where(some, top + jnp.log(safe), LOW)
            mixed = mixed * (1.0 / safe)[:, 0:1]
            mixes.append(mixed)
            for yb in range(NY):
                lse_rows[yb, pl.ds(pl.multiple_of(r * 8, 8), 8), :] = lse[yb * 8 : (yb + 1) * 8]
        for yb in range(NY):
            rows = slice(yb * 8, (yb + 1) * 8)
            both = jnp.concatenate([mixes[0][rows], mixes[1][rows]], axis=0)
            part[yb, pl.ds(pl.multiple_of(pair * 16, 16), 16), :] = both.astype(BF16)

    for n in range(4):

        @pl.loop(0, 4)
        def _(i):
            merge_pair(n * 4 + i)

        if n == 3:
            for yb in range(NY):
                stats[yb] = jnp.transpose(lse_rows[yb])[0:8, :]
            for o in (2, 1, 3):
                s_copy(o).start()
        for o in (2, 1, 3):
            o_copy(o, n).start()

    def column(block):
        t_buf[0:8, :] = block
        return jnp.transpose(t_buf[...])[:, 0:1]

    t_buf[...] = jnp.zeros_like(t_buf)
    lses = [new_lse[:, 0:1], column(stats[y])]
    mixes = [new_o[...], part[y].astype(F32)]
    for o in (1, 3, 2):
        s_copy(o).wait_recv()
        for n in range(4):
            o_copy(o, n).wait_recv()
        lses.append(column(s_land[o - 1]))
        mixes.append(o_land[o - 1].astype(F32))
    top = lses[0]
    for one in lses[1:]:
        top = jnp.maximum(top, one)
    weights = [jnp.exp(one - top) for one in lses]
    total = weights[0]
    for one in weights[1:]:
        total = total + one
    mixed = mixes[0] * (weights[0] / total)
    for one, weight in zip(mixes[1:], weights[1:]):
        mixed += one * (weight / total)
    by_head = dot(rows_by_request(True), mixed.astype(BF16)).astype(BF16)
    uv_copy.wait()
    for n in range(NH):
        vals[:, n * 128 : (n + 1) * 128] = dot(
            by_head[n * 64 : (n + 1) * 64, :], uv_buf[n]
        ).astype(BF16)

    wo_copy.wait()
    width = out.shape[2]
    span = width * NB
    def pair_copy(ty):
        chips = pl.ds(ty * 4, 4)
        return remote(
            sbuf.at[other, chips], sib_land.at[chips], p_send.at[ty], p_recv.at[ty], {"head": sibling}
        )

    for n in (1, 2, 3, 0):
        ty = (y + n) % NY
        cols = pl.ds(pl.multiple_of(ty * span, 128), span)
        piece = dot(vals[...], wbuf[0 : w_o.shape[0], cols])
        for k in range(NB):
            sbuf[k % 2, ty * 4 + k // 2] = piece[:, k * width : (k + 1) * width].astype(BF16)
        pair_copy(ty).start()

    def out_copy(t):
        return remote(
            tbuf.at[t], rbuf.at[chip], d_send.at[t], d_recv.at[chip], {"head": t * 2 + c}
        )

    for n in (1, 2, 3, 0):
        ty = (y + n) % NY
        pair_copy(ty).wait_recv()
        for k in range(4):
            t = ty * 4 + k
            tbuf[t] = (sbuf[c, t].astype(F32) + sib_land[t].astype(F32)).astype(BF16)

            @pl.when(t != chip)
            def _():
                out_copy(t).start()

    def body(o, total):
        src = (chip + o) % 16
        remote(
            rbuf.at[src], rbuf.at[src], d_send.at[src], d_recv.at[src], {"head": src * 2 + c}
        ).wait_recv()
        return total + rbuf[src].astype(F32)

    result = lax.fori_loop(1, 16, body, tbuf[chip].astype(F32))
    out[...] = result.reshape(out.shape).astype(BF16)

    for j in (1, 2, 3):
        wait_send(z_copies(j))
    for j in range(4):
        wait_send(to_right(j))
        wait_send(to_left(j))
        wait_send(onward(j, 0))
        wait_send(onward(j, 1))
        for dx in range(4):
            wait_send(across(j, dx))
    for o in (1, 2, 3):
        wait_send(y_copies(o))
        s_copy(o).wait_send()
        for n in range(4):
            o_copy(o, n).wait_send()
    for ty in range(NY):
        pair_copy(ty).wait_send()

    @pl.loop(1, 16)
    def _(o):
        out_copy((chip + o) % 16).wait_send()

    @pl.loop(1, 16)
    def _(o):
        to = (chip + o) % 16
        share_copy(to).wait_send()
        sum_copy(to).wait_send()

    halves_copy().wait_send()
    back_copy().wait_send()


def spec(space):
    return pl.BlockSpec(memory_space=space)


VM, SM, ANY = pltpu.VMEM, pltpu.SMEM, pl.ANY


def page_plan(block_table, ctx_pages, g, y, b, per_rank, pages_dev):
    flat = jnp.where(
        jnp.arange(MAXP, dtype=jnp.int32)[None, :] < ctx_pages[:, None], block_table, -1
    ).reshape(1, -1)
    at = jnp.arange(NG * NB * pages_dev, dtype=jnp.int32)
    per_plane = NB * pages_dev
    behind = at // per_plane
    plane = (g + NG - (behind ^ (behind >> 1))) % NG
    ids = plane * (N_HEAD * pages_dev) + y * per_plane + at % per_plane
    codes = jnp.arange(flat.shape[1], dtype=jnp.int32)[None, :]
    code = jnp.sum(jnp.where(flat == ids[:, None], codes, 0), axis=1)
    code = code.reshape(NG, NB, pages_dev)
    target = code // (per_rank * MAXP)
    within = jnp.arange(pages_dev, dtype=jnp.int32)
    alike = (target[..., :, None] == target[..., None, :]) & (within[None, :] < within[:, None])
    slot = jnp.sum(alike.astype(jnp.int32), axis=-1)
    places = jnp.arange(SLOT, dtype=jnp.int32)
    here = (target == g)[..., None, :] & (slot[..., None, :] == places[:, None])
    local = code % (per_rank * MAXP)
    held = jnp.sum(jnp.where(here, local[..., None, :] + 1, 0), axis=-1) - 1
    held = held.transpose(1, 0, 2).reshape(-1)
    owner = jnp.where(held >= 0, held // MAXP, per_rank)
    wanted = jnp.arange(per_rank * MAXP, dtype=jnp.int32)
    total = held.shape[0]
    spare = jnp.arange(total, dtype=jnp.int32) - total
    listed = total + jnp.sum(jnp.where(held[None, :] == wanted[:, None], spare[None, :], 0), axis=1)
    mine = lax.dynamic_slice(code, (0, b, 0), (1, 1, pages_dev)).reshape(-1)
    my_target = lax.dynamic_slice(target, (0, b, 0), (1, 1, pages_dev)).reshape(-1)
    my_slot = lax.dynamic_slice(slot, (0, b, 0), (1, 1, pages_dev)).reshape(-1)
    sends = (my_target[None, :] * SLOT + my_slot[None, :]) == jnp.arange(
        NG * SLOT, dtype=jnp.int32
    )[:, None]
    send_idx = jnp.sum(jnp.where(sends, within[None, :], 0), axis=1)
    return owner, listed, send_idx, mine % MAXP


def angle_tables():
    lane = np.arange(2 * ROPE)
    inverse_freq = 10000.0 ** (-2.0 * (lane % 32) / ROPE)
    steps = np.concatenate([np.arange(17) * PAGE, np.arange(2), np.zeros(5)])
    far = steps[:, None] * inverse_freq[None, :]
    near = (np.arange(32)[:, None] + 32 * (lane // ROPE)[None, :]) * inverse_freq[None, :]
    return [jnp.asarray(t, F32) for t in (np.cos(far), np.sin(far), np.cos(near), np.sin(near))]


def on_device(
    prompt, w_dkv, kv_gain, block_table, ctx_pages, dec_hidden, w_dq, q_gain, w_uq, w_uk, w_uv, w_o
):
    g = lax.axis_index("grp")
    h = lax.axis_index("head")
    y, b = h // NB, h % NB
    tokens, depth = prompt.shape
    pages_dev = tokens // PAGE
    per_rank = dec_hidden.shape[0]
    owner, listed, send_idx, my_depth = page_plan(
        block_table, ctx_pages, g, y, b, per_rank, pages_dev
    )
    dma = pltpu.SemaphoreType.DMA
    width = depth // N_HEAD
    slots = NB * NG * SLOT
    out = pl.pallas_call(
        fused_kernel,
        out_shape=jax.ShapeDtypeStruct((per_rank, 2, width), BF16),
        in_specs=[spec(SM)] * 5 + [spec(VM)] * 6 + [spec(ANY)] * 8,
        out_specs=spec(VM),
        scratch_shapes=[
            pltpu.VMEM((tokens + 64, depth), BF16),
            pltpu.VMEM((per_rank, 2, depth), BF16),
            pltpu.VMEM((LAT + ROPE, depth), BF16),
            pltpu.VMEM((tokens + 64, LAT + ROPE), F32),
            pltpu.VMEM(w_uq.shape, BF16),
            pltpu.VMEM(w_uk.shape, BF16),
            pltpu.VMEM(w_uv.shape, BF16),
            pltpu.VMEM((pages_dev, PAGE, LAT), BF16),
            pltpu.VMEM((pages_dev, 32, 128), BF16),
            pltpu.VMEM((NG, ROWS, LAT), BF16),
            pltpu.VMEM((NG, RROWS, 128), BF16),
            pltpu.VMEM((384, QL), BF16),
            pltpu.VMEM((64, 128), F32),
            pltpu.VMEM((64, 128), F32),
            pltpu.VMEM((64, QL), F32),
            pltpu.VMEM((64, QL // 2), F32),
            pltpu.VMEM((64, QL // 2), F32),
            pltpu.VMEM((16, 8, 384), F32),
            pltpu.VMEM((8, 384), F32),
            pltpu.VMEM((64, QL), F32),
            pltpu.VMEM((256, LAT), BF16),
            pltpu.VMEM((256, 128), BF16),
            pltpu.VMEM((128, 128), BF16),
            pltpu.VMEM((64, LAT), BF16),
            pltpu.VMEM((64, 128), BF16),
            pltpu.VMEM((256, LAT), F32),
            pltpu.VMEM((256, 128), F32),
            pltpu.VMEM((NB, NG * ROWS, LAT), BF16),
            pltpu.VMEM((NB, NG * RROWS, 128), BF16),
            pltpu.VMEM((NY, 256, LAT), BF16),
            pltpu.VMEM((NY, 128, 128), BF16),
            pltpu.VMEM((32, 32, LAT + 128), F32),
            pltpu.VMEM((33, 32, LAT + 128), BF16),
            pltpu.VMEM((slots + 1, 32, LAT), BF16),
            pltpu.VMEM((slots + 1, 32, 128), F32),
            pltpu.VMEM((slots + 1, 32, 128), F32),
            pltpu.VMEM((NY, 256, LAT), BF16),
            pltpu.VMEM((NY, 256, 128), F32),
            pltpu.VMEM((NY, 8, 256), F32),
            pltpu.VMEM((3, 256, LAT), BF16),
            pltpu.VMEM((3, 8, 256), F32),
            pltpu.VMEM((128, 256), F32),
            pltpu.VMEM((64, LAT), BF16),
            pltpu.VMEM((2, 16, 64, width), BF16),
            pltpu.VMEM((16, 64, width), BF16),
            pltpu.VMEM((16, 64, width), BF16),
            pltpu.VMEM((16, 64, width), BF16),
            dma((depth // KCHUNK, 2)),
            dma((6,)),
            dma((2,)),
            dma((3, 2)),
            dma((3, 2)),
            dma((4, 2, 2)),
            dma((4, 2, 2)),
            dma((4, 2, 2)),
            dma((4, 2, 2)),
            dma((4, 4, 2)),
            dma((4, 4, 2)),
            dma((4,)),
            dma((16,)),
            dma((16,)),
            dma((16,)),
            dma((16,)),
            dma((3, 2)),
            dma((3, 2)),
            dma((3, 4)),
            dma((3, 4)),
            dma((3,)),
            dma((3,)),
            dma((4,)),
            dma((4,)),
            dma((16,)),
            dma((16,)),
        ],
        compiler_params=pltpu.CompilerParams(
            collective_id=0, has_side_effects=True, vmem_limit_bytes=58 * 1024 * 1024
        ),
    )(
        send_idx,
        owner,
        listed,
        my_depth,
        ctx_pages,
        kv_gain,
        q_gain,
        *angle_tables(),
        prompt,
        dec_hidden,
        w_dq,
        w_dkv.T,
        w_uq,
        w_uk,
        w_uv,
        w_o,
    )
    return out


def solution(mesh):
    return jax.shard_map(
        on_device,
        mesh=mesh,
        in_specs=(
            P(("grp", "head"), None),
            P(),
            P(),
            P(),
            P(),
            P("grp", None, None),
            P("head", None),
            P(),
            P(None, "head"),
            P("head", None, None),
            P("head", None, None),
            P("head", None),
        ),
        out_specs=P("grp", None, "head"),
        check_vma=False,
    )
```

```python
import jax
import jax.numpy as jnp
import numpy as np
from jax import lax
from jax.experimental import pallas as pl
from jax.experimental.pallas import tpu as pltpu
from jax.sharding import PartitionSpec as P

PAGE = 64
SLOT = 3
MAXP = 16
LAT = 512
ROPE = 64
NOPE = 128
QL = 1536
NH = 4
NG = 4
NY = 4
NB = 8
N_HEAD = 32
ROWS = SLOT * PAGE
RROWS = SLOT * PAGE // 2
AT_DEPTH = NG * SLOT
AT_OWNER = 32
AT_LIST = AT_OWNER + NB * NG * SLOT
GROUPS = 8
FOUR = 4
KCHUNK = 1024
AHEAD = 3
OFFS = (0, 1, 3, 2)
MESH = pl.DeviceIdType.MESH
F32 = jnp.float32
BF16 = jnp.bfloat16
LOW = -1e30


def dot(a, b):
    return jnp.dot(a, b, preferred_element_type=F32)


def dot_t(a, b):
    return lax.dot_general(a, b, (((1,), (1,)), ((), ())), preferred_element_type=F32)


def norm_rows(values, gain_row, width):
    mean = jnp.sum(values * values, axis=-1, keepdims=True) * (1.0 / width)
    return values * lax.rsqrt(mean + 1e-06) * gain_row


def rotate_pairs(x, cosine, signed_sine):
    lane = lax.broadcasted_iota(jnp.int32, x.shape, 1)
    swapped = jnp.where((lane & 63) < 32, pltpu.roll(x, 96, 1), pltpu.roll(x, 32, 1))
    return x * cosine + swapped * signed_sine


def rows_by_request(transposed):
    i = lax.broadcasted_iota(jnp.int32, (256, 256), 1 if transposed else 0)
    j = lax.broadcasted_iota(jnp.int32, (256, 256), 0 if transposed else 1)
    place = ((i >> 1) & 3) * 64 + (i >> 3) * 2 + (i & 1)
    return jnp.where(j == place, 1.0, 0.0).astype(BF16)


def fused_kernel(
    plan,
    lengths,
    kv_gain,
    q_gain,
    cos_far,
    sin_far,
    cos_near,
    sin_near,
    prompt,
    hidden,
    w_dq,
    w_dkv,
    w_uq,
    w_uk,
    w_uv,
    w_o,
    out,
    pbuf,
    hbuf,
    wbuf,
    acc,
    uq_buf,
    uk_buf,
    uv_buf,
    lat_own,
    rope_own,
    zlat,
    zrope,
    wdq_buf,
    new_cos,
    new_sin,
    qpart,
    pair_land,
    half,
    rq_land,
    red,
    qlat,
    qmine,
    qr_dup,
    qrmine,
    new_lat,
    new_rope,
    new_o,
    new_lse,
    lat_all,
    rope_all,
    q_lat,
    q_rope,
    qf,
    qb,
    o_slot,
    m_slot,
    l_slot,
    part,
    lse_rows,
    stats,
    o_land,
    s_land,
    t_buf,
    vals,
    sbuf,
    sib_land,
    tbuf,
    rbuf,
    load_sem,
    w_sem,
    own_sem,
    z_send,
    z_recv,
    x_send,
    x_recv,
    f_send,
    f_recv,
    c_send,
    c_recv,
    q_sem,
    r_send,
    r_recv,
    g_send,
    g_recv,
    y_send,
    y_recv,
    o_send,
    o_recv,
    s_send,
    s_recv,
    p_send,
    p_recv,
    d_send,
    d_recv,
):
    g = lax.axis_index("grp")
    h = lax.axis_index("head")
    y = h // NB
    b = h % NB
    x = b // 2
    c = b % 2
    other = 1 - c
    sibling = y * NB + x * 2 + other
    right = y * NB + ((x + 1) % 4) * 2 + c
    left = y * NB + ((x + 3) % 4) * 2 + c
    scale = (NOPE + ROPE) ** (-0.5)

    def start(copies):
        for one in copies:
            one.start()

    def wait_recv(copies):
        for one in copies:
            one.wait_recv()

    def wait_send(copies):
        for one in copies:
            one.wait_send()

    def remote(src, dst, send, recv, to):
        return pltpu.make_async_remote_copy(
            src_ref=src,
            dst_ref=dst,
            send_sem=send,
            recv_sem=recv,
            device_id=to,
            device_id_type=MESH,
        )

    barrier = pltpu.get_barrier_semaphore()

    @pl.loop(1, N_HEAD)
    def _(o):
        pl.semaphore_signal(
            barrier, inc=1, device_id={"head": (h + o) % N_HEAD}, device_id_type=MESH
        )

    for o in (1, 2, 3):
        pl.semaphore_signal(barrier, inc=1, device_id={"grp": (g + o) % NG}, device_id_type=MESH)

    depth = prompt.shape[1]
    tokens = prompt.shape[0]
    chunks = depth // KCHUNK
    loads = []
    for k in range(chunks):
        cols = pl.ds(k * KCHUNK, KCHUNK)
        loads.append(
            [
                pltpu.make_async_copy(
                    prompt.at[:, cols], pbuf.at[pl.ds(0, tokens), cols], load_sem.at[k, 0]
                ),
                pltpu.make_async_copy(w_dkv.at[:, cols], wbuf.at[:, cols], load_sem.at[k, 1]),
            ]
        )
    share = w_dq.shape[0]
    window = 384
    first_col = jnp.minimum((h * share) // 128 * 128, depth - window)
    at_row = pl.multiple_of(h * share - first_col, 32)
    hidden_copy = pltpu.make_async_copy(hidden, hbuf, w_sem.at[4])
    hidden_copy.start()
    wdq_buf[...] = jnp.zeros_like(wdq_buf)
    dq_copy = pltpu.make_async_copy(w_dq, wdq_buf.at[pl.ds(at_row, share), :], w_sem.at[5])
    dq_copy.start()
    for group in loads[:AHEAD]:
        start(group)
    uq_copy = pltpu.make_async_copy(w_uq, uq_buf, w_sem.at[0])
    uk_copy = pltpu.make_async_copy(w_uk, uk_buf, w_sem.at[1])
    uv_copy = pltpu.make_async_copy(w_uv, uv_buf, w_sem.at[2])
    wo_copy = pltpu.make_async_copy(w_o, wbuf.at[pl.ds(0, w_o.shape[0])], w_sem.at[3])

    requests = hidden.shape[0]
    for r in range(requests):
        far = lengths[g * requests + r]
        new_cos[2 * r : 2 * r + 2, :] = jnp.broadcast_to(cos_far[pl.ds(far, 1), :], (2, 128))
        new_sin[2 * r : 2 * r + 2, :] = jnp.broadcast_to(sin_far[pl.ds(far, 1), :], (2, 128))
    odd = (lax.broadcasted_iota(jnp.int32, (64, 128), 0) & 1) == 1
    step_cos = jnp.where(odd, cos_far[18:19, :], cos_far[17:18, :])
    step_sin = jnp.where(odd, sin_far[18:19, :], sin_far[17:18, :])
    far_cos, far_sin = new_cos[...], new_sin[...]
    sign = jnp.where(
        (lax.broadcasted_iota(jnp.int32, (1, 128), 1) & 63) < 32, -1.0, 1.0
    ).astype(F32)
    new_cos[...] = far_cos * step_cos - far_sin * step_sin
    new_sin[...] = (far_sin * step_cos + far_cos * step_sin) * sign

    hidden_copy.wait()
    dq_copy.wait()
    part_of_hidden = hbuf[:, :, pl.ds(pl.multiple_of(first_col, 128), window)].reshape(64, window)
    qpart[...] = dot(part_of_hidden, wdq_buf[...])

    chip = y * 4 + x
    half_width = QL // 2

    def half_cols(core):
        return pl.ds(pl.multiple_of(core * half_width, 128), half_width)

    def block_in(t, first):
        return (
            pl.ds(pl.multiple_of((t // 2) * 8, 8), 8),
            pl.ds(pl.multiple_of(first + (t % 2) * 384, 128), 384),
        )

    def halves_copy():
        return remote(
            qpart.at[:, half_cols(other)], pair_land, q_sem.at[0], q_sem.at[1], {"head": sibling}
        )

    def share_copy(t):
        return remote(
            half.at[block_in(t, 0)], rq_land.at[chip], r_send.at[t], r_recv.at[chip], {"head": t * 2 + c}
        )

    def sum_copy(t):
        return remote(
            red,
            qlat.at[block_in(chip, c * half_width)],
            g_send.at[t],
            g_recv.at[chip],
            {"head": t * 2 + c},
        )

    def back_copy():
        return remote(
            qlat.at[:, half_cols(c)],
            qlat.at[:, half_cols(c)],
            q_sem.at[2],
            q_sem.at[3],
            {"head": sibling},
        )

    def share_sums():
        halves_copy().wait_recv()
        half[...] = qpart[:, half_cols(c)] + pair_land[...]
        rq_land[chip] = half[block_in(chip, 0)]

        @pl.loop(1, 16)
        def _(o):
            share_copy((chip + o) % 16).start()

    def send_sums():
        @pl.loop(1, 16)
        def _(o):
            src = (chip + o) % 16
            remote(
                rq_land.at[src], rq_land.at[src], r_send.at[src], r_recv.at[src], {"head": src * 2 + c}
            ).wait_recv()

        red[...] = jnp.sum(rq_land[...], axis=0)
        qlat[block_in(chip, c * half_width)] = red[...]

        @pl.loop(1, 16)
        def _(o):
            sum_copy((chip + o) % 16).start()

    for k in range(chunks):
        if k == 2:
            pl.semaphore_wait(barrier, N_HEAD - 1 + 3)
            halves_copy().start()
        if k == 3:
            share_sums()
        for one in loads[k]:
            one.wait()
        if k + AHEAD < chunks:
            start(loads[k + AHEAD])
        elif k + AHEAD == chunks:
            start([uq_copy, uk_copy, uv_copy])
        cols = slice(k * KCHUNK, (k + 1) * KCHUNK)
        pbuf[tokens:, cols] = hbuf[:, :, cols].reshape(64, KCHUNK)
        piece = dot_t(pbuf[:, cols], wbuf[:, cols])
        if k == 0:
            acc[...] = piece
        else:
            acc[...] += piece
    send_sums()
    wo_copy.start()

    pages = tokens // PAGE
    lat_own[...] = (
        norm_rows(acc[0:tokens, 0:LAT], kv_gain[...].reshape(1, LAT), LAT).astype(BF16).reshape(pages, PAGE, LAT)
    )
    halves = []
    for p in range(pages):
        first = acc[p * PAGE : p * PAGE + 32, LAT : LAT + ROPE]
        second = acc[p * PAGE + 32 : p * PAGE + 64, LAT : LAT + ROPE]
        halves.append(jnp.concatenate([first, second], axis=1))
    packed = jnp.concatenate(halves, axis=0)
    page_cos = []
    page_sin = []
    for p in range(pages):
        far = pl.ds(plan[AT_DEPTH + p], 1)
        far_cos, far_sin = cos_far[far, :], sin_far[far, :]
        page_cos.append(far_cos * cos_near[...] - far_sin * sin_near[...])
        page_sin.append((far_sin * cos_near[...] + far_cos * sin_near[...]) * sign)
    page_cos = jnp.concatenate(page_cos, axis=0)
    page_sin = jnp.concatenate(page_sin, axis=0)
    rope_own[...] = (
        rotate_pairs(packed, page_cos, page_sin).astype(BF16).reshape(pages, 32, 128)
    )

    for j in range(4):
        rank = (g + OFFS[j]) % NG
        for k in range(SLOT):
            page = plan[rank * SLOT + k]
            zlat[j, k * PAGE : (k + 1) * PAGE, :] = lat_own[page]
            zrope[j, k * 32 : (k + 1) * 32, :] = rope_own[page]

    def place(ref, at, j):
        rows = ref.shape[1] // NG
        return ref.at[at, pl.ds(j * rows, rows)]

    def half_place(ref, at, j, side):
        rows = ref.shape[1] // NG // 2
        return ref.at[at, pl.ds((j * 2 + side) * rows, rows)]

    def z_copies(j):
        rank = (g + OFFS[j]) % NG
        return [
            remote(
                src.at[j], place(dst, b, j), z_send.at[j - 1, i], z_recv.at[j - 1, i], {"grp": rank}
            )
            for i, (src, dst) in enumerate(((zlat, lat_all), (zrope, rope_all)))
        ]

    def block_at(dx, core):
        return ((x + dx) % 4) * 2 + core

    def ring_copies(j, dx, to, send, recv):
        at = block_at(dx, c)
        res = []
        for i, (mine, ref) in enumerate(((zlat, lat_all), (zrope, rope_all))):
            src = mine.at[0] if (j == 0 and dx == 0) else place(ref, at, j)
            res.append(remote(src, place(ref, at, j), send.at[i], recv.at[i], {"head": to}))
        return res

    def to_right(j):
        return ring_copies(j, 0, right, x_send.at[j, 0], x_recv.at[j, 0])

    def to_left(j):
        return ring_copies(j, 0, left, x_send.at[j, 1], x_recv.at[j, 1])

    def onward(j, side):
        at = block_at(1 if side else 3, c)
        return [
            remote(
                half_place(ref, at, j, side),
                half_place(ref, at, j, side),
                f_send.at[j, side, i],
                f_recv.at[j, side, i],
                {"head": left if side else right},
            )
            for i, ref in enumerate((lat_all, rope_all))
        ]

    def across(j, dx):
        return ring_copies(j, dx, sibling, c_send.at[j, dx], c_recv.at[j, dx])

    def arrived(j, dx, core, sem):
        at = block_at(dx, core)
        for i, ref in enumerate((lat_all, rope_all)):
            remote(
                place(ref, at, j), place(ref, at, j), sem.at[i], sem.at[i], {"head": sibling}
            ).wait_recv()

    def serve_own(j):
        if j > 0:
            arrived(j, 0, c, z_recv.at[j - 1])
        start(to_right(j))
        start(to_left(j))
        start(across(j, 0))

    def serve_near(j):
        arrived(j, 3, c, x_recv.at[j, 0])
        start(onward(j, 0))
        start(across(j, 3))
        arrived(j, 1, c, x_recv.at[j, 1])
        start(onward(j, 1))
        start(across(j, 1))

    def serve_far(j):
        at = block_at(2, c)
        for side in range(2):
            for i, ref in enumerate((lat_all, rope_all)):
                there = half_place(ref, at, j, side)
                sem = f_recv.at[j, side, i]
                remote(there, there, sem, sem, {"head": sibling}).wait_recv()
        start(across(j, 2))

    def from_sibling(j, places):
        for dx in places:
            arrived(j, dx, other, c_recv.at[j, dx])

    for j in (1, 2, 3):
        start(z_copies(j))
    own = [
        pltpu.make_async_copy(zlat.at[0], place(lat_all, b, 0), own_sem.at[0]),
        pltpu.make_async_copy(zrope.at[0], place(rope_all, b, 0), own_sem.at[1]),
    ]
    start(own)
    serve_own(0)

    new_lat[...] = norm_rows(acc[tokens : tokens + 64, 0:LAT], kv_gain[...].reshape(1, LAT), LAT).astype(BF16)
    new_r = acc[tokens : tokens + 64, LAT : LAT + ROPE]
    new_r = rotate_pairs(jnp.concatenate([new_r, new_r], axis=1), new_cos[...], new_sin[...])
    lane = lax.broadcasted_iota(jnp.int32, new_r.shape, 1)
    new_rope[...] = jnp.where(lane < ROPE, new_r, 0.0).astype(BF16)

    @pl.loop(1, 16)
    def _(o):
        src = (chip + o) % 16
        remote(
            red,
            qlat.at[block_in(src, c * half_width)],
            g_send.at[src],
            g_recv.at[src],
            {"head": src * 2 + c},
        ).wait_recv()

    back_copy().start()
    serve_own(1)
    remote(
        qlat.at[:, half_cols(other)],
        qlat.at[:, half_cols(other)],
        q_sem.at[2],
        q_sem.at[3],
        {"head": sibling},
    ).wait_recv()
    uq_copy.wait()
    uk_copy.wait()
    query_norm = norm_rows(qlat[...], q_gain[...].reshape(1, QL), QL).astype(BF16)
    queries = dot(query_norm, uq_buf[...])
    serve_own(2)
    parts = []
    ropes = []
    for n in range(NH):
        at = n * (NOPE + ROPE)
        parts.append(dot(queries[:, at : at + NOPE].astype(BF16), uk_buf[n]).astype(BF16))
        one = queries[:, at + NOPE : at + NOPE + ROPE]
        one = jnp.concatenate([one, one], axis=1)
        ropes.append(rotate_pairs(one, new_cos[...], new_sin[...]).astype(BF16))
    order = rows_by_request(False)
    qmine[...] = dot(order, jnp.concatenate(parts, axis=0)).astype(BF16)
    rotated = dot(order, jnp.concatenate(ropes, axis=0))
    qr_dup[...] = rotated.astype(BF16)
    first_lanes = lax.broadcasted_iota(jnp.int32, (128, 128), 1) < ROPE
    qrmine[...] = jnp.where(first_lanes, rotated[0:128], rotated[128:256]).astype(BF16)

    def y_copies(o):
        to = ((y + o) % NY) * NB + b
        return [
            remote(src, dst.at[y], y_send.at[o - 1, i], y_recv.at[o - 1, i], {"head": to})
            for i, (src, dst) in enumerate(((qmine, q_lat), (qrmine, q_rope)))
        ]

    for o in (2, 1, 3):
        start(y_copies(o))
    q_lat[y] = qmine[...]
    q_rope[y] = qrmine[...]

    serve_near(0)
    serve_own(3)
    serve_near(1)

    s = (dot_t(qmine[...], new_lat[...]) + dot_t(qr_dup[...], new_rope[...])) * scale
    i = lax.broadcasted_iota(jnp.int32, s.shape, 0)
    j = lax.broadcasted_iota(jnp.int32, s.shape, 1)
    live = ((i >> 3) == (j >> 1)) & ((j & 1) <= (i & 1))
    s = jnp.where(live, s, LOW)
    top = jnp.max(s, axis=1, keepdims=True)
    p = jnp.where(live, jnp.exp(s - top), 0.0)
    total = jnp.sum(p, axis=1, keepdims=True)
    new_o[...] = dot(p.astype(BF16), new_lat[...]) / total
    new_lse[...] = jnp.broadcast_to(top + jnp.log(total), new_lse.shape)

    serve_far(0)
    serve_near(2)

    for o in (1, 3, 2):
        src = (y + NY - o) % NY
        for n, ref in enumerate((q_lat, q_rope)):
            remote(
                ref.at[src],
                ref.at[src],
                y_send.at[o - 1, n],
                y_recv.at[o - 1, n],
                {"head": src * NB + b},
            ).wait_recv()
    for yb in range(NY):
        qf[:, yb * 8 : (yb + 1) * 8, 0:LAT] = q_lat[yb].astype(F32).reshape(requests, 8, LAT)
        both = q_rope[yb].astype(F32)
        turned = pltpu.roll(both, 64, 1)
        rows = slice(yb * 8, (yb + 1) * 8)
        qf[0:16, rows, LAT:] = jnp.where(first_lanes, both, turned).reshape(16, 8, 128)
        qf[16:32, rows, LAT:] = jnp.where(first_lanes, turned, both).reshape(16, 8, 128)
    qb[0:requests] = qf[...].astype(BF16)
    qb[requests] = jnp.zeros((32, LAT + 128), BF16)

    row = lax.broadcasted_iota(jnp.int32, (FOUR * 32, FOUR * PAGE), 0)
    col = lax.broadcasted_iota(jnp.int32, (FOUR * 32, FOUR * PAGE), 1)
    own_page = (row >> 5) == (col >> 6)
    low_lane = lax.broadcasted_iota(jnp.int32, (32, 128), 1) < ROPE

    def attend(at, t):
        first = at * NG * SLOT + t * FOUR
        keys = lat_all[at, pl.ds(pl.multiple_of(t * FOUR * PAGE, 256), FOUR * PAGE), :]
        pairs = rope_all[at, pl.ds(pl.multiple_of(t * FOUR * 32, 128), FOUR * 32), :]
        zero = jnp.zeros((32, 128), BF16)
        ropes = []
        for k in range(FOUR):
            pair = pairs[k * 32 : (k + 1) * 32, :]
            ropes += [jnp.where(low_lane, pair, zero), jnp.where(low_lane, zero, pair)]
        q = jnp.concatenate([qb[plan[AT_OWNER + first + k]] for k in range(FOUR)], axis=0)
        s = dot_t(q[:, 0:LAT], keys) + dot_t(q[:, LAT:], jnp.concatenate(ropes, axis=0))
        s = jnp.where(own_page, s * scale, LOW)
        top = jnp.max(s, axis=1, keepdims=True)
        p = jnp.where(own_page, jnp.exp(s - top), 0.0)
        total = jnp.sum(p, axis=1, keepdims=True)
        o = dot(p.astype(BF16), keys)
        top = jnp.broadcast_to(top, (FOUR * 32, 128))
        total = jnp.broadcast_to(total, (FOUR * 32, 128))
        o_slot[pl.ds(first, FOUR)] = o.astype(BF16).reshape(FOUR, 32, LAT)
        m_slot[pl.ds(first, FOUR)] = top.reshape(FOUR, 32, 128)
        l_slot[pl.ds(first, FOUR)] = total.reshape(FOUR, 32, 128)

    def attend_blocks(core, places, first, last):
        if last - first == 1:
            for dx in places:
                attend(block_at(dx, core), first)
            return

        @pl.loop(first, last)
        def _(t):
            for dx in places:
                attend(block_at(dx, core), t)

    for one in own:
        one.wait()
    o_slot[96] = jnp.zeros((32, LAT), BF16)
    m_slot[96] = jnp.full((32, 128), LOW, F32)
    l_slot[96] = jnp.zeros((32, 128), F32)
    for j in range(4):
        from_sibling(j, (0,))

    @pl.loop(0, NG * SLOT // FOUR)
    def _(t):
        attend(block_at(0, c), t)
        attend(block_at(0, other), t)

    serve_near(3)
    attend_blocks(c, (1, 3), 0, 2)
    serve_far(1)
    for j in range(3):
        from_sibling(j, (1, 3))
    attend_blocks(other, (1, 3), 0, 2)
    serve_far(2)
    attend_blocks(c, (1, 3), 2, 3)
    attend_blocks(c, (2,), 0, 2)
    from_sibling(3, (1, 3))
    serve_far(3)
    attend_blocks(other, (1, 3), 2, 3)
    for j in range(3):
        from_sibling(j, (2,))
    attend_blocks(other, (2,), 0, 2)
    attend_blocks(c, (2,), 2, 3)
    from_sibling(3, (2,))
    attend_blocks(other, (2,), 2, 3)

    def o_copy(o, n):
        ty = (y + o) % NY
        size = 256 // GROUPS
        rows = pl.ds(pl.multiple_of(n * size, size), size)
        return remote(
            part.at[ty, rows],
            o_land.at[o - 1, rows],
            o_send.at[o - 1, n],
            o_recv.at[o - 1, n],
            {"head": ty * NB + b},
        )

    def s_copy(o):
        ty = (y + o) % NY
        return remote(
            stats.at[ty], s_land.at[o - 1], s_send.at[o - 1], s_recv.at[o - 1], {"head": ty * NB + b}
        )

    def merge_pair(pair):
        mixes = []
        for u in range(2):
            r = pair * 2 + u
            at = [plan[AT_LIST + r * MAXP + k] for k in range(MAXP)]
            tops = [m_slot[one] for one in at]
            top = tops[0]
            for one in tops[1:]:
                top = jnp.maximum(top, one)
            total = jnp.zeros((32, 128), F32)
            mixed = jnp.zeros((32, LAT), F32)
            for one, its_top in zip(at, tops):
                e = jnp.exp(its_top - top)
                total += l_slot[one] * e
                mixed += o_slot[one].astype(F32) * e[:, 0:1]
            some = total > 0.0
            safe = jnp.where(some, total, 1.0)
            lse = jnp.where(some, top + jnp.log(safe), LOW)
            mixed = mixed * (1.0 / safe)[:, 0:1]
            mixes.append(mixed)
            for yb in range(NY):
                lse_rows[yb, pl.ds(pl.multiple_of(r * 8, 8), 8), :] = lse[yb * 8 : (yb + 1) * 8]
        for yb in range(NY):
            rows = slice(yb * 8, (yb + 1) * 8)
            both = jnp.concatenate([mixes[0][rows], mixes[1][rows]], axis=0)
            part[yb, pl.ds(pl.multiple_of(pair * 16, 16), 16), :] = both.astype(BF16)

    @pl.loop(0, GROUPS)
    def _(n):
        @pl.loop(0, 16 // GROUPS)
        def _(i):
            merge_pair(n * (16 // GROUPS) + i)

        for o in (2, 1, 3):
            o_copy(o, n).start()

    for yb in range(NY):
        stats[yb] = jnp.transpose(lse_rows[yb])[0:8, :]
    for o in (2, 1, 3):
        s_copy(o).start()

    for j in (1, 2, 3):
        wait_send(z_copies(j))
    for j in range(4):
        wait_send(to_right(j))
        wait_send(to_left(j))
        wait_send(onward(j, 0))
        wait_send(onward(j, 1))
        for dx in range(4):
            wait_send(across(j, dx))
    for o in (1, 2, 3):
        wait_send(y_copies(o))

    @pl.loop(1, 16)
    def _(o):
        to = (chip + o) % 16
        share_copy(to).wait_send()
        sum_copy(to).wait_send()

    halves_copy().wait_send()
    back_copy().wait_send()

    def column(block):
        t_buf[0:8, :] = block
        return jnp.transpose(t_buf[...])[:, 0:1]

    t_buf[...] = jnp.zeros_like(t_buf)
    lses = [new_lse[:, 0:1], column(stats[y])]
    mixes = [new_o[...], part[y].astype(F32)]
    for o in (1, 3, 2):
        s_copy(o).wait_recv()
        for n in range(GROUPS):
            o_copy(o, n).wait_recv()
        lses.append(column(s_land[o - 1]))
        mixes.append(o_land[o - 1].astype(F32))
    top = lses[0]
    for one in lses[1:]:
        top = jnp.maximum(top, one)
    weights = [jnp.exp(one - top) for one in lses]
    total = weights[0]
    for one in weights[1:]:
        total = total + one
    mixed = mixes[0] * (weights[0] / total)
    for one, weight in zip(mixes[1:], weights[1:]):
        mixed += one * (weight / total)
    by_head = dot(rows_by_request(True), mixed.astype(BF16)).astype(BF16)
    uv_copy.wait()
    for n in range(NH):
        vals[:, n * 128 : (n + 1) * 128] = dot(
            by_head[n * 64 : (n + 1) * 64, :], uv_buf[n]
        ).astype(BF16)

    wo_copy.wait()
    width = out.shape[2]
    span = width * NB
    def pair_copy(ty):
        chips = pl.ds(ty * 4, 4)
        return remote(
            sbuf.at[other, chips], sib_land.at[chips], p_send.at[ty], p_recv.at[ty], {"head": sibling}
        )

    for n in (1, 2, 3, 0):
        ty = (y + n) % NY
        cols = pl.ds(pl.multiple_of(ty * span, 128), span)
        piece = dot(vals[...], wbuf[0 : w_o.shape[0], cols])
        for k in range(NB):
            sbuf[k % 2, ty * 4 + k // 2] = piece[:, k * width : (k + 1) * width].astype(BF16)
        pair_copy(ty).start()

    def out_copy(t):
        return remote(
            tbuf.at[t], rbuf.at[chip], d_send.at[t], d_recv.at[chip], {"head": t * 2 + c}
        )

    for n in (1, 2, 3, 0):
        ty = (y + n) % NY
        pair_copy(ty).wait_recv()
        for k in range(4):
            t = ty * 4 + k
            tbuf[t] = (sbuf[c, t].astype(F32) + sib_land[t].astype(F32)).astype(BF16)

            @pl.when(t != chip)
            def _():
                out_copy(t).start()

    def body(o, total):
        src = (chip + o) % 16
        remote(
            rbuf.at[src], rbuf.at[src], d_send.at[src], d_recv.at[src], {"head": src * 2 + c}
        ).wait_recv()
        return total + rbuf[src].astype(F32)

    result = lax.fori_loop(1, 16, body, tbuf[chip].astype(F32))
    out[...] = result.reshape(out.shape).astype(BF16)

    for o in (1, 2, 3):
        s_copy(o).wait_send()
        for n in range(GROUPS):
            o_copy(o, n).wait_send()
    for ty in range(NY):
        pair_copy(ty).wait_send()

    @pl.loop(1, 16)
    def _(o):
        out_copy((chip + o) % 16).wait_send()


def spec(space):
    return pl.BlockSpec(memory_space=space)


VM, SM, ANY = pltpu.VMEM, pltpu.SMEM, pl.ANY


def page_plan(block_table, ctx_pages, g, y, b, per_rank, pages_dev):
    flat = jnp.where(
        jnp.arange(MAXP, dtype=jnp.int32)[None, :] < ctx_pages[:, None], block_table, -1
    ).reshape(1, -1)
    at = jnp.arange(NG * NB * pages_dev, dtype=jnp.int32)
    per_plane = NB * pages_dev
    behind = at // per_plane
    plane = (g + NG - (behind ^ (behind >> 1))) % NG
    ids = plane * (N_HEAD * pages_dev) + y * per_plane + at % per_plane
    codes = jnp.arange(flat.shape[1], dtype=jnp.int32)[None, :]
    code = jnp.sum(jnp.where(flat == ids[:, None], codes, 0), axis=1)
    code = code.reshape(NG, NB, pages_dev)
    target = code // (per_rank * MAXP)
    within = jnp.arange(pages_dev, dtype=jnp.int32)
    alike = (target[..., :, None] == target[..., None, :]) & (within[None, :] < within[:, None])
    slot = jnp.sum(alike.astype(jnp.int32), axis=-1)
    places = jnp.arange(SLOT, dtype=jnp.int32)
    here = (target == g)[..., None, :] & (slot[..., None, :] == places[:, None])
    local = code % (per_rank * MAXP)
    held = jnp.sum(jnp.where(here, local[..., None, :] + 1, 0), axis=-1) - 1
    held = held.transpose(1, 0, 2).reshape(-1)
    owner = jnp.where(held >= 0, held // MAXP, per_rank)
    wanted = jnp.arange(per_rank * MAXP, dtype=jnp.int32)
    total = held.shape[0]
    spare = jnp.arange(total, dtype=jnp.int32) - total
    listed = total + jnp.sum(jnp.where(held[None, :] == wanted[:, None], spare[None, :], 0), axis=1)
    mine = lax.dynamic_slice(code, (0, b, 0), (1, 1, pages_dev)).reshape(-1)
    my_target = lax.dynamic_slice(target, (0, b, 0), (1, 1, pages_dev)).reshape(-1)
    my_slot = lax.dynamic_slice(slot, (0, b, 0), (1, 1, pages_dev)).reshape(-1)
    sends = (my_target[None, :] * SLOT + my_slot[None, :]) == jnp.arange(
        NG * SLOT, dtype=jnp.int32
    )[:, None]
    send_idx = jnp.sum(jnp.where(sends, within[None, :], 0), axis=1)
    spare = jnp.zeros(AT_OWNER - AT_DEPTH - pages_dev, jnp.int32)
    return jnp.concatenate([send_idx, mine % MAXP, spare, owner, listed])


def angle_tables():
    lane = np.arange(2 * ROPE)
    inverse_freq = 10000.0 ** (-2.0 * (lane % 32) / ROPE)
    steps = np.concatenate([np.arange(17) * PAGE, np.arange(2), np.zeros(5)])
    far = steps[:, None] * inverse_freq[None, :]
    near = (np.arange(32)[:, None] + 32 * (lane // ROPE)[None, :]) * inverse_freq[None, :]
    return [jnp.asarray(t, F32) for t in (np.cos(far), np.sin(far), np.cos(near), np.sin(near))]


def on_device(
    prompt, w_dkv, kv_gain, block_table, ctx_pages, dec_hidden, w_dq, q_gain, w_uq, w_uk, w_uv, w_o
):
    g = lax.axis_index("grp")
    h = lax.axis_index("head")
    y, b = h // NB, h % NB
    tokens, depth = prompt.shape
    pages_dev = tokens // PAGE
    per_rank = dec_hidden.shape[0]
    plan = page_plan(
        block_table, ctx_pages, g, y, b, per_rank, pages_dev
    )
    dma = pltpu.SemaphoreType.DMA
    width = depth // N_HEAD
    slots = NB * NG * SLOT
    out = pl.pallas_call(
        fused_kernel,
        out_shape=jax.ShapeDtypeStruct((per_rank, 2, width), BF16),
        in_specs=[spec(SM)] * 2 + [spec(VM)] * 6 + [spec(ANY)] * 8,
        out_specs=spec(VM),
        scratch_shapes=[
            pltpu.VMEM((tokens + 64, depth), BF16),
            pltpu.VMEM((per_rank, 2, depth), BF16),
            pltpu.VMEM((LAT + ROPE, depth), BF16),
            pltpu.VMEM((tokens + 64, LAT + ROPE), F32),
            pltpu.VMEM(w_uq.shape, BF16),
            pltpu.VMEM(w_uk.shape, BF16),
            pltpu.VMEM(w_uv.shape, BF16),
            pltpu.VMEM((pages_dev, PAGE, LAT), BF16),
            pltpu.VMEM((pages_dev, 32, 128), BF16),
            pltpu.VMEM((NG, ROWS, LAT), BF16),
            pltpu.VMEM((NG, RROWS, 128), BF16),
            pltpu.VMEM((384, QL), BF16),
            pltpu.VMEM((64, 128), F32),
            pltpu.VMEM((64, 128), F32),
            pltpu.VMEM((64, QL), F32),
            pltpu.VMEM((64, QL // 2), F32),
            pltpu.VMEM((64, QL // 2), F32),
            pltpu.VMEM((16, 8, 384), F32),
            pltpu.VMEM((8, 384), F32),
            pltpu.VMEM((64, QL), F32),
            pltpu.VMEM((256, LAT), BF16),
            pltpu.VMEM((256, 128), BF16),
            pltpu.VMEM((128, 128), BF16),
            pltpu.VMEM((64, LAT), BF16),
            pltpu.VMEM((64, 128), BF16),
            pltpu.VMEM((256, LAT), F32),
            pltpu.VMEM((256, 128), F32),
            pltpu.VMEM((NB, NG * ROWS, LAT), BF16),
            pltpu.VMEM((NB, NG * RROWS, 128), BF16),
            pltpu.VMEM((NY, 256, LAT), BF16),
            pltpu.VMEM((NY, 128, 128), BF16),
            pltpu.VMEM((32, 32, LAT + 128), F32),
            pltpu.VMEM((33, 32, LAT + 128), BF16),
            pltpu.VMEM((slots + 1, 32, LAT), BF16),
            pltpu.VMEM((slots + 1, 32, 128), F32),
            pltpu.VMEM((slots + 1, 32, 128), F32),
            pltpu.VMEM((NY, 256, LAT), BF16),
            pltpu.VMEM((NY, 256, 128), F32),
            pltpu.VMEM((NY, 8, 256), F32),
            pltpu.VMEM((3, 256, LAT), BF16),
            pltpu.VMEM((3, 8, 256), F32),
            pltpu.VMEM((128, 256), F32),
            pltpu.VMEM((64, LAT), BF16),
            pltpu.VMEM((2, 16, 64, width), BF16),
            pltpu.VMEM((16, 64, width), BF16),
            pltpu.VMEM((16, 64, width), BF16),
            pltpu.VMEM((16, 64, width), BF16),
            dma((depth // KCHUNK, 2)),
            dma((6,)),
            dma((2,)),
            dma((3, 2)),
            dma((3, 2)),
            dma((4, 2, 2)),
            dma((4, 2, 2)),
            dma((4, 2, 2)),
            dma((4, 2, 2)),
            dma((4, 4, 2)),
            dma((4, 4, 2)),
            dma((4,)),
            dma((16,)),
            dma((16,)),
            dma((16,)),
            dma((16,)),
            dma((3, 2)),
            dma((3, 2)),
            dma((3, GROUPS)),
            dma((3, GROUPS)),
            dma((3,)),
            dma((3,)),
            dma((4,)),
            dma((4,)),
            dma((16,)),
            dma((16,)),
        ],
        compiler_params=pltpu.CompilerParams(
            collective_id=0, has_side_effects=True, vmem_limit_bytes=58 * 1024 * 1024
        ),
    )(
        plan,
        ctx_pages,
        kv_gain,
        q_gain,
        *angle_tables(),
        prompt,
        dec_hidden,
        w_dq,
        w_dkv.T,
        w_uq,
        w_uk,
        w_uv,
        w_o,
    )
    return out


def solution(mesh):
    return jax.shard_map(
        on_device,
        mesh=mesh,
        in_specs=(
            P(("grp", "head"), None),
            P(),
            P(),
            P(),
            P(),
            P("grp", None, None),
            P("head", None),
            P(),
            P(None, "head"),
            P("head", None, None),
            P("head", None, None),
            P("head", None),
        ),
        out_specs=P("grp", None, "head"),
        check_vma=False,
    )
```

```python
import jax
import jax.numpy as jnp
import numpy as np
from jax import lax
from jax.experimental import pallas as pl
from jax.experimental.pallas import tpu as pltpu
from jax.sharding import PartitionSpec as P

PAGE = 64
SLOT = 3
MAXP = 16
LAT = 512
ROPE = 64
NOPE = 128
QL = 1536
NH = 4
NG = 4
NY = 4
NB = 8
N_HEAD = 32
ROWS = SLOT * PAGE
RROWS = SLOT * PAGE // 2
AT_DEPTH = NG * SLOT
AT_OWNER = 32
AT_LIST = AT_OWNER + NB * NG * SLOT
GROUPS = 8
FOUR = 4
KCHUNK = 1024
AHEAD = 3
OFFS = (0, 1, 3, 2)
MESH = pl.DeviceIdType.MESH
F32 = jnp.float32
BF16 = jnp.bfloat16
LOW = -1e30


def dot(a, b):
    return jnp.dot(a, b, preferred_element_type=F32)


def dot_t(a, b):
    return lax.dot_general(a, b, (((1,), (1,)), ((), ())), preferred_element_type=F32)


def norm_rows(values, gain_row, width):
    mean = jnp.sum(values * values, axis=-1, keepdims=True) * (1.0 / width)
    return values * lax.rsqrt(mean + 1e-06) * gain_row


def rotate_pairs(x, cosine, signed_sine):
    lane = lax.broadcasted_iota(jnp.int32, x.shape, 1)
    swapped = jnp.where((lane & 63) < 32, pltpu.roll(x, 96, 1), pltpu.roll(x, 32, 1))
    return x * cosine + swapped * signed_sine


def rows_by_request(transposed):
    i = lax.broadcasted_iota(jnp.int32, (256, 256), 1 if transposed else 0)
    j = lax.broadcasted_iota(jnp.int32, (256, 256), 0 if transposed else 1)
    place = ((i >> 1) & 3) * 64 + (i >> 3) * 2 + (i & 1)
    return jnp.where(j == place, 1.0, 0.0).astype(BF16)


def fused_kernel(
    plan,
    lengths,
    kv_gain,
    q_gain,
    cos_far,
    sin_far,
    cos_near,
    sin_near,
    prompt,
    hidden,
    w_dq,
    w_dkv,
    w_uq,
    w_uk,
    w_uv,
    w_o,
    out,
    pbuf,
    hbuf,
    wbuf,
    acc,
    uq_buf,
    uk_buf,
    uv_buf,
    lat_own,
    rope_own,
    zlat,
    zrope,
    wdq_buf,
    new_cos,
    new_sin,
    qpart,
    pair_land,
    half,
    rq_land,
    red,
    qlat,
    qmine,
    qr_dup,
    qrmine,
    new_lat,
    new_rope,
    new_o,
    new_lse,
    lat_all,
    rope_all,
    q_lat,
    q_rope,
    qf,
    qb,
    o_slot,
    m_slot,
    l_slot,
    part,
    lse_rows,
    stats,
    o_land,
    s_land,
    t_buf,
    vals,
    sbuf,
    sib_land,
    tbuf,
    rbuf,
    load_sem,
    w_sem,
    own_sem,
    z_send,
    z_recv,
    x_send,
    x_recv,
    f_send,
    f_recv,
    c_send,
    c_recv,
    q_sem,
    r_send,
    r_recv,
    g_send,
    g_recv,
    y_send,
    y_recv,
    o_send,
    o_recv,
    s_send,
    s_recv,
    p_send,
    p_recv,
    d_send,
    d_recv,
):
    g = lax.axis_index("grp")
    h = lax.axis_index("head")
    y = h // NB
    b = h % NB
    x = b // 2
    c = b % 2
    other = 1 - c
    sibling = y * NB + x * 2 + other
    right = y * NB + ((x + 1) % 4) * 2 + c
    left = y * NB + ((x + 3) % 4) * 2 + c
    scale = (NOPE + ROPE) ** (-0.5)

    def start(copies):
        for one in copies:
            one.start()

    def wait_recv(copies):
        for one in copies:
            one.wait_recv()

    def wait_send(copies):
        for one in copies:
            one.wait_send()

    def remote(src, dst, send, recv, to):
        return pltpu.make_async_remote_copy(
            src_ref=src,
            dst_ref=dst,
            send_sem=send,
            recv_sem=recv,
            device_id=to,
            device_id_type=MESH,
        )

    barrier = pltpu.get_barrier_semaphore()

    @pl.loop(1, N_HEAD)
    def _(o):
        pl.semaphore_signal(
            barrier, inc=1, device_id={"head": (h + o) % N_HEAD}, device_id_type=MESH
        )

    for o in (1, 2, 3):
        pl.semaphore_signal(barrier, inc=1, device_id={"grp": (g + o) % NG}, device_id_type=MESH)

    depth = prompt.shape[1]
    tokens = prompt.shape[0]
    chunks = depth // KCHUNK
    loads = []
    for k in range(chunks):
        cols = pl.ds(k * KCHUNK, KCHUNK)
        loads.append(
            [
                pltpu.make_async_copy(
                    prompt.at[:, cols], pbuf.at[pl.ds(0, tokens), cols], load_sem.at[k, 0]
                ),
                pltpu.make_async_copy(w_dkv.at[:, cols], wbuf.at[:, cols], load_sem.at[k, 1]),
            ]
        )
    share = w_dq.shape[0]
    window = 384
    first_col = jnp.minimum((h * share) // 128 * 128, depth - window)
    at_row = pl.multiple_of(h * share - first_col, 32)
    hidden_copy = pltpu.make_async_copy(hidden, hbuf, w_sem.at[4])
    hidden_copy.start()
    wdq_buf[...] = jnp.zeros_like(wdq_buf)
    dq_copy = pltpu.make_async_copy(w_dq, wdq_buf.at[pl.ds(at_row, share), :], w_sem.at[5])
    dq_copy.start()
    for group in loads[:AHEAD]:
        start(group)
    uq_copy = pltpu.make_async_copy(w_uq, uq_buf, w_sem.at[0])
    uk_copy = pltpu.make_async_copy(w_uk, uk_buf, w_sem.at[1])
    uv_copy = pltpu.make_async_copy(w_uv, uv_buf, w_sem.at[2])
    wo_copy = pltpu.make_async_copy(w_o, wbuf.at[pl.ds(0, w_o.shape[0])], w_sem.at[3])

    requests = hidden.shape[0]
    for r in range(requests):
        far = lengths[g * requests + r]
        new_cos[2 * r : 2 * r + 2, :] = jnp.broadcast_to(cos_far[pl.ds(far, 1), :], (2, 128))
        new_sin[2 * r : 2 * r + 2, :] = jnp.broadcast_to(sin_far[pl.ds(far, 1), :], (2, 128))
    odd = (lax.broadcasted_iota(jnp.int32, (64, 128), 0) & 1) == 1
    step_cos = jnp.where(odd, cos_far[18:19, :], cos_far[17:18, :])
    step_sin = jnp.where(odd, sin_far[18:19, :], sin_far[17:18, :])
    far_cos, far_sin = new_cos[...], new_sin[...]
    sign = jnp.where(
        (lax.broadcasted_iota(jnp.int32, (1, 128), 1) & 63) < 32, -1.0, 1.0
    ).astype(F32)
    new_cos[...] = far_cos * step_cos - far_sin * step_sin
    new_sin[...] = (far_sin * step_cos + far_cos * step_sin) * sign

    hidden_copy.wait()
    dq_copy.wait()
    part_of_hidden = hbuf[:, :, pl.ds(pl.multiple_of(first_col, 128), window)].reshape(64, window)
    qpart[...] = dot(part_of_hidden, wdq_buf[...])

    chip = y * 4 + x
    half_width = QL // 2

    def half_cols(core):
        return pl.ds(pl.multiple_of(core * half_width, 128), half_width)

    def block_in(t, first):
        return (
            pl.ds(pl.multiple_of((t // 2) * 8, 8), 8),
            pl.ds(pl.multiple_of(first + (t % 2) * 384, 128), 384),
        )

    def halves_copy():
        return remote(
            qpart.at[:, half_cols(other)], pair_land, q_sem.at[0], q_sem.at[1], {"head": sibling}
        )

    def share_copy(t):
        return remote(
            half.at[block_in(t, 0)], rq_land.at[chip], r_send.at[t], r_recv.at[chip], {"head": t * 2 + c}
        )

    def sum_copy(t):
        return remote(
            red,
            qlat.at[block_in(chip, c * half_width)],
            g_send.at[t],
            g_recv.at[chip],
            {"head": t * 2 + c},
        )

    def back_copy():
        return remote(
            qlat.at[:, half_cols(c)],
            qlat.at[:, half_cols(c)],
            q_sem.at[2],
            q_sem.at[3],
            {"head": sibling},
        )

    def share_sums():
        halves_copy().wait_recv()
        half[...] = qpart[:, half_cols(c)] + pair_land[...]
        rq_land[chip] = half[block_in(chip, 0)]

        @pl.loop(1, 16)
        def _(o):
            share_copy((chip + o) % 16).start()

    def send_sums():
        @pl.loop(1, 16)
        def _(o):
            src = (chip + o) % 16
            remote(
                rq_land.at[src], rq_land.at[src], r_send.at[src], r_recv.at[src], {"head": src * 2 + c}
            ).wait_recv()

        red[...] = jnp.sum(rq_land[...], axis=0)
        qlat[block_in(chip, c * half_width)] = red[...]

        @pl.loop(1, 16)
        def _(o):
            sum_copy((chip + o) % 16).start()

    for k in range(chunks):
        if k == 2:
            pl.semaphore_wait(barrier, N_HEAD - 1 + 3)
            halves_copy().start()
        if k == 3:
            share_sums()
        for one in loads[k]:
            one.wait()
        if k + AHEAD < chunks:
            start(loads[k + AHEAD])
        elif k + AHEAD == chunks:
            start([uq_copy, uk_copy, uv_copy])
        cols = slice(k * KCHUNK, (k + 1) * KCHUNK)
        pbuf[tokens:, cols] = hbuf[:, :, cols].reshape(64, KCHUNK)
        piece = dot_t(pbuf[:, cols], wbuf[:, cols])
        if k == 0:
            acc[...] = piece
        else:
            acc[...] += piece
    wo_copy.start()

    pages = tokens // PAGE
    lat_own[...] = (
        norm_rows(acc[0:tokens, 0:LAT], kv_gain[...].reshape(1, LAT), LAT).astype(BF16).reshape(pages, PAGE, LAT)
    )
    halves = []
    for p in range(pages):
        first = acc[p * PAGE : p * PAGE + 32, LAT : LAT + ROPE]
        second = acc[p * PAGE + 32 : p * PAGE + 64, LAT : LAT + ROPE]
        halves.append(jnp.concatenate([first, second], axis=1))
    packed = jnp.concatenate(halves, axis=0)
    page_cos = []
    page_sin = []
    for p in range(pages):
        far = pl.ds(plan[AT_DEPTH + p], 1)
        far_cos, far_sin = cos_far[far, :], sin_far[far, :]
        page_cos.append(far_cos * cos_near[...] - far_sin * sin_near[...])
        page_sin.append((far_sin * cos_near[...] + far_cos * sin_near[...]) * sign)
    page_cos = jnp.concatenate(page_cos, axis=0)
    page_sin = jnp.concatenate(page_sin, axis=0)
    rope_own[...] = (
        rotate_pairs(packed, page_cos, page_sin).astype(BF16).reshape(pages, 32, 128)
    )

    for j in range(4):
        rank = (g + OFFS[j]) % NG
        for k in range(SLOT):
            page = plan[rank * SLOT + k]
            zlat[j, k * PAGE : (k + 1) * PAGE, :] = lat_own[page]
            zrope[j, k * 32 : (k + 1) * 32, :] = rope_own[page]

    def place(ref, at, j):
        rows = ref.shape[1] // NG
        return ref.at[at, pl.ds(j * rows, rows)]

    def half_place(ref, at, j, side):
        rows = ref.shape[1] // NG // 2
        return ref.at[at, pl.ds((j * 2 + side) * rows, rows)]

    def z_copies(j):
        rank = (g + OFFS[j]) % NG
        return [
            remote(
                src.at[j], place(dst, b, j), z_send.at[j - 1, i], z_recv.at[j - 1, i], {"grp": rank}
            )
            for i, (src, dst) in enumerate(((zlat, lat_all), (zrope, rope_all)))
        ]

    def block_at(dx, core):
        return ((x + dx) % 4) * 2 + core

    def ring_copies(j, dx, to, send, recv):
        at = block_at(dx, c)
        res = []
        for i, (mine, ref) in enumerate(((zlat, lat_all), (zrope, rope_all))):
            src = mine.at[0] if (j == 0 and dx == 0) else place(ref, at, j)
            res.append(remote(src, place(ref, at, j), send.at[i], recv.at[i], {"head": to}))
        return res

    def to_right(j):
        return ring_copies(j, 0, right, x_send.at[j, 0], x_recv.at[j, 0])

    def to_left(j):
        return ring_copies(j, 0, left, x_send.at[j, 1], x_recv.at[j, 1])

    def onward(j, side):
        at = block_at(1 if side else 3, c)
        return [
            remote(
                half_place(ref, at, j, side),
                half_place(ref, at, j, side),
                f_send.at[j, side, i],
                f_recv.at[j, side, i],
                {"head": left if side else right},
            )
            for i, ref in enumerate((lat_all, rope_all))
        ]

    def across(j, dx):
        return ring_copies(j, dx, sibling, c_send.at[j, dx], c_recv.at[j, dx])

    def arrived(j, dx, core, sem):
        at = block_at(dx, core)
        for i, ref in enumerate((lat_all, rope_all)):
            remote(
                place(ref, at, j), place(ref, at, j), sem.at[i], sem.at[i], {"head": sibling}
            ).wait_recv()

    def serve_own(j):
        if j > 0:
            arrived(j, 0, c, z_recv.at[j - 1])
        start(to_right(j))
        start(to_left(j))
        start(across(j, 0))

    def serve_near(j):
        arrived(j, 3, c, x_recv.at[j, 0])
        start(onward(j, 0))
        start(across(j, 3))
        arrived(j, 1, c, x_recv.at[j, 1])
        start(onward(j, 1))
        start(across(j, 1))

    def serve_far(j):
        at = block_at(2, c)
        for side in range(2):
            for i, ref in enumerate((lat_all, rope_all)):
                there = half_place(ref, at, j, side)
                sem = f_recv.at[j, side, i]
                remote(there, there, sem, sem, {"head": sibling}).wait_recv()
        start(across(j, 2))

    def from_sibling(j, places):
        for dx in places:
            arrived(j, dx, other, c_recv.at[j, dx])

    for j in (1, 2, 3):
        start(z_copies(j))
    own = [
        pltpu.make_async_copy(zlat.at[0], place(lat_all, b, 0), own_sem.at[0]),
        pltpu.make_async_copy(zrope.at[0], place(rope_all, b, 0), own_sem.at[1]),
    ]
    start(own)
    serve_own(0)
    send_sums()

    new_lat[...] = norm_rows(acc[tokens : tokens + 64, 0:LAT], kv_gain[...].reshape(1, LAT), LAT).astype(BF16)
    new_r = acc[tokens : tokens + 64, LAT : LAT + ROPE]
    new_r = rotate_pairs(jnp.concatenate([new_r, new_r], axis=1), new_cos[...], new_sin[...])
    lane = lax.broadcasted_iota(jnp.int32, new_r.shape, 1)
    new_rope[...] = jnp.where(lane < ROPE, new_r, 0.0).astype(BF16)

    @pl.loop(1, 16)
    def _(o):
        src = (chip + o) % 16
        remote(
            red,
            qlat.at[block_in(src, c * half_width)],
            g_send.at[src],
            g_recv.at[src],
            {"head": src * 2 + c},
        ).wait_recv()

    back_copy().start()
    serve_own(1)
    remote(
        qlat.at[:, half_cols(other)],
        qlat.at[:, half_cols(other)],
        q_sem.at[2],
        q_sem.at[3],
        {"head": sibling},
    ).wait_recv()
    uq_copy.wait()
    uk_copy.wait()
    query_norm = norm_rows(qlat[...], q_gain[...].reshape(1, QL), QL).astype(BF16)
    queries = dot(query_norm, uq_buf[...])
    serve_own(2)
    parts = []
    ropes = []
    for n in range(NH):
        at = n * (NOPE + ROPE)
        parts.append(dot(queries[:, at : at + NOPE].astype(BF16), uk_buf[n]).astype(BF16))
        one = queries[:, at + NOPE : at + NOPE + ROPE]
        one = jnp.concatenate([one, one], axis=1)
        ropes.append(rotate_pairs(one, new_cos[...], new_sin[...]).astype(BF16))
    order = rows_by_request(False)
    qmine[...] = dot(order, jnp.concatenate(parts, axis=0)).astype(BF16)
    rotated = dot(order, jnp.concatenate(ropes, axis=0))
    qr_dup[...] = rotated.astype(BF16)
    first_lanes = lax.broadcasted_iota(jnp.int32, (128, 128), 1) < ROPE
    qrmine[...] = jnp.where(first_lanes, rotated[0:128], rotated[128:256]).astype(BF16)

    def y_copies(o):
        to = ((y + o) % NY) * NB + b
        return [
            remote(src, dst.at[y], y_send.at[o - 1, i], y_recv.at[o - 1, i], {"head": to})
            for i, (src, dst) in enumerate(((qmine, q_lat), (qrmine, q_rope)))
        ]

    for o in (2, 1, 3):
        start(y_copies(o))
    q_lat[y] = qmine[...]
    q_rope[y] = qrmine[...]

    serve_near(0)
    serve_own(3)
    serve_near(1)

    s = (dot_t(qmine[...], new_lat[...]) + dot_t(qr_dup[...], new_rope[...])) * scale
    i = lax.broadcasted_iota(jnp.int32, s.shape, 0)
    j = lax.broadcasted_iota(jnp.int32, s.shape, 1)
    live = ((i >> 3) == (j >> 1)) & ((j & 1) <= (i & 1))
    s = jnp.where(live, s, LOW)
    top = jnp.max(s, axis=1, keepdims=True)
    p = jnp.where(live, jnp.exp(s - top), 0.0)
    total = jnp.sum(p, axis=1, keepdims=True)
    new_o[...] = dot(p.astype(BF16), new_lat[...]) / total
    new_lse[...] = jnp.broadcast_to(top + jnp.log(total), new_lse.shape)

    serve_far(0)
    serve_near(2)

    for o in (1, 3, 2):
        src = (y + NY - o) % NY
        for n, ref in enumerate((q_lat, q_rope)):
            remote(
                ref.at[src],
                ref.at[src],
                y_send.at[o - 1, n],
                y_recv.at[o - 1, n],
                {"head": src * NB + b},
            ).wait_recv()
    for yb in range(NY):
        qf[:, yb * 8 : (yb + 1) * 8, 0:LAT] = q_lat[yb].astype(F32).reshape(requests, 8, LAT)
        both = q_rope[yb].astype(F32)
        turned = pltpu.roll(both, 64, 1)
        rows = slice(yb * 8, (yb + 1) * 8)
        qf[0:16, rows, LAT:] = jnp.where(first_lanes, both, turned).reshape(16, 8, 128)
        qf[16:32, rows, LAT:] = jnp.where(first_lanes, turned, both).reshape(16, 8, 128)
    qb[0:requests] = qf[...].astype(BF16)
    qb[requests] = jnp.zeros((32, LAT + 128), BF16)

    row = lax.broadcasted_iota(jnp.int32, (FOUR * 32, FOUR * PAGE), 0)
    col = lax.broadcasted_iota(jnp.int32, (FOUR * 32, FOUR * PAGE), 1)
    own_page = (row >> 5) == (col >> 6)
    low_lane = lax.broadcasted_iota(jnp.int32, (32, 128), 1) < ROPE

    def attend(at, t):
        first = at * NG * SLOT + t * FOUR
        keys = lat_all[at, pl.ds(pl.multiple_of(t * FOUR * PAGE, 256), FOUR * PAGE), :]
        pairs = rope_all[at, pl.ds(pl.multiple_of(t * FOUR * 32, 128), FOUR * 32), :]
        zero = jnp.zeros((32, 128), BF16)
        ropes = []
        for k in range(FOUR):
            pair = pairs[k * 32 : (k + 1) * 32, :]
            ropes += [jnp.where(low_lane, pair, zero), jnp.where(low_lane, zero, pair)]
        q = jnp.concatenate([qb[plan[AT_OWNER + first + k]] for k in range(FOUR)], axis=0)
        s = dot_t(q[:, 0:LAT], keys) + dot_t(q[:, LAT:], jnp.concatenate(ropes, axis=0))
        s = jnp.where(own_page, s * scale, LOW)
        top = jnp.max(s, axis=1, keepdims=True)
        p = jnp.where(own_page, jnp.exp(s - top), 0.0)
        total = jnp.sum(p, axis=1, keepdims=True)
        o = dot(p.astype(BF16), keys)
        top = jnp.broadcast_to(top, (FOUR * 32, 128))
        total = jnp.broadcast_to(total, (FOUR * 32, 128))
        o_slot[pl.ds(first, FOUR)] = o.astype(BF16).reshape(FOUR, 32, LAT)
        m_slot[pl.ds(first, FOUR)] = top.reshape(FOUR, 32, 128)
        l_slot[pl.ds(first, FOUR)] = total.reshape(FOUR, 32, 128)

    def attend_blocks(core, places, first, last):
        if last - first == 1:
            for dx in places:
                attend(block_at(dx, core), first)
            return

        @pl.loop(first, last)
        def _(t):
            for dx in places:
                attend(block_at(dx, core), t)

    for one in own:
        one.wait()
    o_slot[96] = jnp.zeros((32, LAT), BF16)
    m_slot[96] = jnp.full((32, 128), LOW, F32)
    l_slot[96] = jnp.zeros((32, 128), F32)
    for j in range(4):
        from_sibling(j, (0,))

    @pl.loop(0, NG * SLOT // FOUR)
    def _(t):
        attend(block_at(0, c), t)
        attend(block_at(0, other), t)

    serve_near(3)
    attend_blocks(c, (1, 3), 0, 2)
    serve_far(1)
    for j in range(3):
        from_sibling(j, (1, 3))
    attend_blocks(other, (1, 3), 0, 2)
    serve_far(2)
    attend_blocks(c, (1, 3), 2, 3)
    attend_blocks(c, (2,), 0, 2)
    from_sibling(3, (1, 3))
    serve_far(3)
    attend_blocks(other, (1, 3), 2, 3)
    for j in range(3):
        from_sibling(j, (2,))
    attend_blocks(other, (2,), 0, 2)
    attend_blocks(c, (2,), 2, 3)
    from_sibling(3, (2,))
    attend_blocks(other, (2,), 2, 3)

    def o_copy(o, n):
        ty = (y + o) % NY
        size = 256 // GROUPS
        rows = pl.ds(pl.multiple_of(n * size, size), size)
        return remote(
            part.at[ty, rows],
            o_land.at[o - 1, rows],
            o_send.at[o - 1, n],
            o_recv.at[o - 1, n],
            {"head": ty * NB + b},
        )

    def s_copy(o):
        ty = (y + o) % NY
        return remote(
            stats.at[ty], s_land.at[o - 1], s_send.at[o - 1], s_recv.at[o - 1], {"head": ty * NB + b}
        )

    def merge_pair(pair):
        mixes = []
        for u in range(2):
            r = pair * 2 + u
            at = [plan[AT_LIST + r * MAXP + k] for k in range(MAXP)]
            tops = [m_slot[one] for one in at]
            top = tops[0]
            for one in tops[1:]:
                top = jnp.maximum(top, one)
            total = jnp.zeros((32, 128), F32)
            mixed = jnp.zeros((32, LAT), F32)
            for one, its_top in zip(at, tops):
                e = jnp.exp(its_top - top)
                total += l_slot[one] * e
                mixed += o_slot[one].astype(F32) * e[:, 0:1]
            some = total > 0.0
            safe = jnp.where(some, total, 1.0)
            lse = jnp.where(some, top + jnp.log(safe), LOW)
            mixed = mixed * (1.0 / safe)[:, 0:1]
            mixes.append(mixed)
            for yb in range(NY):
                lse_rows[yb, pl.ds(pl.multiple_of(r * 8, 8), 8), :] = lse[yb * 8 : (yb + 1) * 8]
        for yb in range(NY):
            rows = slice(yb * 8, (yb + 1) * 8)
            both = jnp.concatenate([mixes[0][rows], mixes[1][rows]], axis=0)
            part[yb, pl.ds(pl.multiple_of(pair * 16, 16), 16), :] = both.astype(BF16)

    @pl.loop(0, GROUPS)
    def _(n):
        @pl.loop(0, 16 // GROUPS)
        def _(i):
            merge_pair(n * (16 // GROUPS) + i)

        for o in (2, 1, 3):
            o_copy(o, n).start()

    for yb in range(NY):
        stats[yb] = jnp.transpose(lse_rows[yb])[0:8, :]
    for o in (2, 1, 3):
        s_copy(o).start()

    for j in (1, 2, 3):
        wait_send(z_copies(j))
    for j in range(4):
        wait_send(to_right(j))
        wait_send(to_left(j))
        wait_send(onward(j, 0))
        wait_send(onward(j, 1))
        for dx in range(4):
            wait_send(across(j, dx))
    for o in (1, 2, 3):
        wait_send(y_copies(o))

    @pl.loop(1, 16)
    def _(o):
        to = (chip + o) % 16
        share_copy(to).wait_send()
        sum_copy(to).wait_send()

    halves_copy().wait_send()
    back_copy().wait_send()

    def column(block):
        t_buf[0:8, :] = block
        return jnp.transpose(t_buf[...])[:, 0:1]

    t_buf[...] = jnp.zeros_like(t_buf)
    lses = [new_lse[:, 0:1], column(stats[y])]
    mixes = [new_o[...], part[y].astype(F32)]
    for o in (1, 3, 2):
        s_copy(o).wait_recv()
        for n in range(GROUPS):
            o_copy(o, n).wait_recv()
        lses.append(column(s_land[o - 1]))
        mixes.append(o_land[o - 1].astype(F32))
    top = lses[0]
    for one in lses[1:]:
        top = jnp.maximum(top, one)
    weights = [jnp.exp(one - top) for one in lses]
    total = weights[0]
    for one in weights[1:]:
        total = total + one
    mixed = mixes[0] * (weights[0] / total)
    for one, weight in zip(mixes[1:], weights[1:]):
        mixed += one * (weight / total)
    by_head = dot(rows_by_request(True), mixed.astype(BF16)).astype(BF16)
    uv_copy.wait()
    for n in range(NH):
        vals[:, n * 128 : (n + 1) * 128] = dot(
            by_head[n * 64 : (n + 1) * 64, :], uv_buf[n]
        ).astype(BF16)

    wo_copy.wait()
    width = out.shape[2]
    span = width * NB
    def pair_copy(ty):
        chips = pl.ds(ty * 4, 4)
        return remote(
            sbuf.at[other, chips], sib_land.at[chips], p_send.at[ty], p_recv.at[ty], {"head": sibling}
        )

    for n in (1, 2, 3, 0):
        ty = (y + n) % NY
        cols = pl.ds(pl.multiple_of(ty * span, 128), span)
        piece = dot(vals[...], wbuf[0 : w_o.shape[0], cols])
        for k in range(NB):
            sbuf[k % 2, ty * 4 + k // 2] = piece[:, k * width : (k + 1) * width].astype(BF16)
        pair_copy(ty).start()

    def out_copy(t):
        return remote(
            tbuf.at[t], rbuf.at[chip], d_send.at[t], d_recv.at[chip], {"head": t * 2 + c}
        )

    for n in (1, 2, 3, 0):
        ty = (y + n) % NY
        pair_copy(ty).wait_recv()
        for k in range(4):
            t = ty * 4 + k
            tbuf[t] = (sbuf[c, t].astype(F32) + sib_land[t].astype(F32)).astype(BF16)

            @pl.when(t != chip)
            def _():
                out_copy(t).start()

    def body(o, total):
        src = (chip + o) % 16
        remote(
            rbuf.at[src], rbuf.at[src], d_send.at[src], d_recv.at[src], {"head": src * 2 + c}
        ).wait_recv()
        return total + rbuf[src].astype(F32)

    result = lax.fori_loop(1, 16, body, tbuf[chip].astype(F32))
    out[...] = result.reshape(out.shape).astype(BF16)

    for o in (1, 2, 3):
        s_copy(o).wait_send()
        for n in range(GROUPS):
            o_copy(o, n).wait_send()
    for ty in range(NY):
        pair_copy(ty).wait_send()

    @pl.loop(1, 16)
    def _(o):
        out_copy((chip + o) % 16).wait_send()


def spec(space):
    return pl.BlockSpec(memory_space=space)


VM, SM, ANY = pltpu.VMEM, pltpu.SMEM, pl.ANY


def page_plan(block_table, ctx_pages, g, y, b, per_rank, pages_dev):
    flat = jnp.where(
        jnp.arange(MAXP, dtype=jnp.int32)[None, :] < ctx_pages[:, None], block_table, -1
    ).reshape(1, -1)
    at = jnp.arange(NG * NB * pages_dev, dtype=jnp.int32)
    per_plane = NB * pages_dev
    behind = at // per_plane
    plane = (g + NG - (behind ^ (behind >> 1))) % NG
    ids = plane * (N_HEAD * pages_dev) + y * per_plane + at % per_plane
    codes = jnp.arange(flat.shape[1], dtype=jnp.int32)[None, :]
    code = jnp.sum(jnp.where(flat == ids[:, None], codes, 0), axis=1)
    code = code.reshape(NG, NB, pages_dev)
    target = code // (per_rank * MAXP)
    within = jnp.arange(pages_dev, dtype=jnp.int32)
    alike = (target[..., :, None] == target[..., None, :]) & (within[None, :] < within[:, None])
    slot = jnp.sum(alike.astype(jnp.int32), axis=-1)
    places = jnp.arange(SLOT, dtype=jnp.int32)
    here = (target == g)[..., None, :] & (slot[..., None, :] == places[:, None])
    local = code % (per_rank * MAXP)
    held = jnp.sum(jnp.where(here, local[..., None, :] + 1, 0), axis=-1) - 1
    held = held.transpose(1, 0, 2).reshape(-1)
    owner = jnp.where(held >= 0, held // MAXP, per_rank)
    wanted = jnp.arange(per_rank * MAXP, dtype=jnp.int32)
    total = held.shape[0]
    spare = jnp.arange(total, dtype=jnp.int32) - total
    listed = total + jnp.sum(jnp.where(held[None, :] == wanted[:, None], spare[None, :], 0), axis=1)
    mine = lax.dynamic_slice(code, (0, b, 0), (1, 1, pages_dev)).reshape(-1)
    my_target = lax.dynamic_slice(target, (0, b, 0), (1, 1, pages_dev)).reshape(-1)
    my_slot = lax.dynamic_slice(slot, (0, b, 0), (1, 1, pages_dev)).reshape(-1)
    sends = (my_target[None, :] * SLOT + my_slot[None, :]) == jnp.arange(
        NG * SLOT, dtype=jnp.int32
    )[:, None]
    send_idx = jnp.sum(jnp.where(sends, within[None, :], 0), axis=1)
    spare = jnp.zeros(AT_OWNER - AT_DEPTH - pages_dev, jnp.int32)
    return jnp.concatenate([send_idx, mine % MAXP, spare, owner, listed])


def angle_tables():
    lane = np.arange(2 * ROPE)
    inverse_freq = 10000.0 ** (-2.0 * (lane % 32) / ROPE)
    steps = np.concatenate([np.arange(17) * PAGE, np.arange(2), np.zeros(5)])
    far = steps[:, None] * inverse_freq[None, :]
    near = (np.arange(32)[:, None] + 32 * (lane // ROPE)[None, :]) * inverse_freq[None, :]
    return [jnp.asarray(t, F32) for t in (np.cos(far), np.sin(far), np.cos(near), np.sin(near))]


def on_device(
    prompt, w_dkv, kv_gain, block_table, ctx_pages, dec_hidden, w_dq, q_gain, w_uq, w_uk, w_uv, w_o
):
    g = lax.axis_index("grp")
    h = lax.axis_index("head")
    y, b = h // NB, h % NB
    tokens, depth = prompt.shape
    pages_dev = tokens // PAGE
    per_rank = dec_hidden.shape[0]
    plan = page_plan(
        block_table, ctx_pages, g, y, b, per_rank, pages_dev
    )
    dma = pltpu.SemaphoreType.DMA
    width = depth // N_HEAD
    slots = NB * NG * SLOT
    out = pl.pallas_call(
        fused_kernel,
        out_shape=jax.ShapeDtypeStruct((per_rank, 2, width), BF16),
        in_specs=[spec(SM)] * 2 + [spec(VM)] * 6 + [spec(ANY)] * 8,
        out_specs=spec(VM),
        scratch_shapes=[
            pltpu.VMEM((tokens + 64, depth), BF16),
            pltpu.VMEM((per_rank, 2, depth), BF16),
            pltpu.VMEM((LAT + ROPE, depth), BF16),
            pltpu.VMEM((tokens + 64, LAT + ROPE), F32),
            pltpu.VMEM(w_uq.shape, BF16),
            pltpu.VMEM(w_uk.shape, BF16),
            pltpu.VMEM(w_uv.shape, BF16),
            pltpu.VMEM((pages_dev, PAGE, LAT), BF16),
            pltpu.VMEM((pages_dev, 32, 128), BF16),
            pltpu.VMEM((NG, ROWS, LAT), BF16),
            pltpu.VMEM((NG, RROWS, 128), BF16),
            pltpu.VMEM((384, QL), BF16),
            pltpu.VMEM((64, 128), F32),
            pltpu.VMEM((64, 128), F32),
            pltpu.VMEM((64, QL), F32),
            pltpu.VMEM((64, QL // 2), F32),
            pltpu.VMEM((64, QL // 2), F32),
            pltpu.VMEM((16, 8, 384), F32),
            pltpu.VMEM((8, 384), F32),
            pltpu.VMEM((64, QL), F32),
            pltpu.VMEM((256, LAT), BF16),
            pltpu.VMEM((256, 128), BF16),
            pltpu.VMEM((128, 128), BF16),
            pltpu.VMEM((64, LAT), BF16),
            pltpu.VMEM((64, 128), BF16),
            pltpu.VMEM((256, LAT), F32),
            pltpu.VMEM((256, 128), F32),
            pltpu.VMEM((NB, NG * ROWS, LAT), BF16),
            pltpu.VMEM((NB, NG * RROWS, 128), BF16),
            pltpu.VMEM((NY, 256, LAT), BF16),
            pltpu.VMEM((NY, 128, 128), BF16),
            pltpu.VMEM((32, 32, LAT + 128), F32),
            pltpu.VMEM((33, 32, LAT + 128), BF16),
            pltpu.VMEM((slots + 1, 32, LAT), BF16),
            pltpu.VMEM((slots + 1, 32, 128), F32),
            pltpu.VMEM((slots + 1, 32, 128), F32),
            pltpu.VMEM((NY, 256, LAT), BF16),
            pltpu.VMEM((NY, 256, 128), F32),
            pltpu.VMEM((NY, 8, 256), F32),
            pltpu.VMEM((3, 256, LAT), BF16),
            pltpu.VMEM((3, 8, 256), F32),
            pltpu.VMEM((128, 256), F32),
            pltpu.VMEM((64, LAT), BF16),
            pltpu.VMEM((2, 16, 64, width), BF16),
            pltpu.VMEM((16, 64, width), BF16),
            pltpu.VMEM((16, 64, width), BF16),
            pltpu.VMEM((16, 64, width), BF16),
            dma((depth // KCHUNK, 2)),
            dma((6,)),
            dma((2,)),
            dma((3, 2)),
            dma((3, 2)),
            dma((4, 2, 2)),
            dma((4, 2, 2)),
            dma((4, 2, 2)),
            dma((4, 2, 2)),
            dma((4, 4, 2)),
            dma((4, 4, 2)),
            dma((4,)),
            dma((16,)),
            dma((16,)),
            dma((16,)),
            dma((16,)),
            dma((3, 2)),
            dma((3, 2)),
            dma((3, GROUPS)),
            dma((3, GROUPS)),
            dma((3,)),
            dma((3,)),
            dma((4,)),
            dma((4,)),
            dma((16,)),
            dma((16,)),
        ],
        compiler_params=pltpu.CompilerParams(
            collective_id=0, has_side_effects=True, vmem_limit_bytes=58 * 1024 * 1024
        ),
    )(
        plan,
        ctx_pages,
        kv_gain,
        q_gain,
        *angle_tables(),
        prompt,
        dec_hidden,
        w_dq,
        w_dkv.T,
        w_uq,
        w_uk,
        w_uv,
        w_o,
    )
    return out


def solution(mesh):
    return jax.shard_map(
        on_device,
        mesh=mesh,
        in_specs=(
            P(("grp", "head"), None),
            P(),
            P(),
            P(),
            P(),
            P("grp", None, None),
            P("head", None),
            P(),
            P(None, "head"),
            P("head", None, None),
            P("head", None, None),
            P("head", None),
        ),
        out_specs=P("grp", None, "head"),
        check_vma=False,
    )
```
